512 devices in a mesh: grp: 128 (over z, x, core), tile: 4 (over y).
Axes of the slice: x: 4, y: 4, z: 16, core: 2. Of those that a mesh axis runs over, the one named last changes fastest.
Arguments:
- emb: bfloat16 [131072, 1024], P(('grp', 'tile')), as said below
- dest: int32 [131072], P(('grp', 'tile')), may hold values from 0 to 127, as said below
Outputs:
- similarity: float32 [131072], P(('grp', 'tile'))
The draws below stay inside these ranges and needn't reach their ends.
Inputs may be any that keep to these rules, and one draw needn't show every extreme that they name: `dest`: among the 256 clips of one device at most 3 name any one subgroup; in every draw one subgroup is named by exactly 3 clips of every device. `emb`: every row is nonzero.
All inputs are finite; a program needn't handle non-finite values.
Results may differ from the reference program's by a relative error of at most 0.00047.
Values may be sent and summed in bfloat16 or wider, within the bound.
A program may use at most 64 MiB of HBM per device.

```python
import jax
import jax.numpy as jnp
from jax import lax

D = 1024
CLIP_DEV = 256
FAM = 128
SLOT = 3
CLIPS = 131072
N_GRP = 128
N_TILE = 4


def layout(key):
    blocks = CLIPS // CLIP_DEV
    width = N_GRP * SLOT
    key_full, key_order, key_mix, key_family = jax.random.split(key, 4)
    full_group = jax.random.randint(key_full, (), 0, N_GRP)
    order = jax.vmap(lambda k: jax.random.permutation(k, width))(jax.random.split(key_order, blocks))
    grouping = jnp.arange(width, dtype=jnp.int32) // SLOT
    scores = order + jnp.where(grouping == full_group, width, 0)[None, :]
    picked = lax.top_k(scores, CLIP_DEV)[1]
    mixing = jax.vmap(lambda k: jax.random.permutation(k, CLIP_DEV))(jax.random.split(key_mix, blocks))
    picked = jnp.take_along_axis(picked, mixing, axis=1)
    dest = (picked // SLOT).reshape(CLIPS).astype(jnp.int32)
    family = jax.random.randint(key_family, (CLIPS,), 0, FAM).astype(jnp.int32)
    return (dest, family)


def draw_dest(key, part):
    return layout(key)[0]


def draw_emb(key, part):
    dest, family = layout(key)
    key = jax.random.fold_in(key, 7)
    key_vec, key_noise, key_weight = jax.random.split(key, 3)
    ident = dest * FAM + family
    shared = jax.vmap(lambda i: jax.random.normal(jax.random.fold_in(key_vec, i), (D,), jnp.float32))(ident)
    noise = jax.random.normal(key_noise, (CLIPS, D), jnp.float32)
    weight = jnp.exp(jax.random.uniform(key_weight, (CLIPS, 1), jnp.float32, -1.2, 1.1))
    return (weight * shared + noise).astype(jnp.bfloat16)


def setup_inputs(seed: int = 0) -> dict:
    key_of = jax.random.split(jax.random.key(seed), 3)
    return {
        "emb": draw_emb(jax.random.fold_in(key_of[2], 71), 0),
        "dest": draw_dest(jax.random.fold_in(key_of[2], 71), 0),
    }


def reference(emb, dest):
    wide = emb.astype(jnp.float32)
    unit = (wide / (jnp.sqrt(lax.optimization_barrier(jnp.sum(wide * wide, axis=1, keepdims=True))) + 1e-06)).astype(jnp.bfloat16)
    capacity = SLOT * N_GRP * N_TILE

    def one_group(group):
        picked = jnp.nonzero(dest == group, size=capacity, fill_value=CLIPS)[0].astype(jnp.int32)
        live = picked < CLIPS
        safe = jnp.minimum(picked, CLIPS - 1).astype(jnp.int32)
        rows = unit[safe].astype(jnp.float32)
        score = jnp.dot(rows, rows.T, precision=lax.Precision.HIGHEST, preferred_element_type=jnp.float32)
        counter = jnp.arange(capacity, dtype=jnp.int32)
        usable = live[:, None] & live[None, :] & (counter[:, None] != counter[None, :])
        best = lax.optimization_barrier(jnp.max(jnp.where(usable, score, jnp.float32(-1.0)), axis=1))
        return (picked, best)
    picked, best = lax.map(one_group, jnp.arange(N_GRP, dtype=jnp.int32))
    similarity = jnp.full((CLIPS,), -1.0, jnp.float32)
    return similarity.at[picked.reshape(-1)].set(best.reshape(-1), mode='drop')
```

```python
import functools

import jax
import jax.numpy as jnp
from jax import lax
from jax.experimental import pallas as pl
from jax.experimental.pallas import tpu as pltpu
from jax.sharding import PartitionSpec as P

MESH = pl.DeviceIdType.MESH
Z, X, C, Y = 16, 4, 2, 4
PLANE = X * C * Y
SLOT = 3
OWN = 256
D = 1024
SUB = D // 128
STEPS = Z // 2
CHUNK = 2 * PLANE * SLOT
ROWS = STEPS * CHUNK
GROUPS = Z * X * C
DEAD = 2.0
LOW = -8.0


def grp_of(z, x, c):
    return (z * X + x) * C + c


def holder_y(z, c):
    return (z + 2 * c) % Y


def body_kernel(
    emb_ref, dest_ref, out_ref,
    emb_v, unit, spread, outgoing, arrived, spread_in, rows, ra, ba, bs, bb,
    in_sem, met_sem, send_sem, recv_sem, a_send, a_recv, b_send, b_recv,
):
    g = lax.axis_index("grp")
    y = lax.axis_index("tile")
    z = g // (X * C)
    x = (g // C) % X
    c = g % C
    me = (x * C + c) * Y + y
    holder = y == holder_y(z, c)

    load = pltpu.make_async_copy(emb_ref, emb_v, in_sem)
    load.start()

    barrier = pltpu.get_barrier_semaphore()

    def greet_line(i, carry):
        to = (z * C + c + i) % (Z * C)
        pl.semaphore_signal(
            barrier, inc=1, device_id=(grp_of(to // C, x, to % C), y), device_id_type=MESH
        )
        return carry

    lax.fori_loop(1, Z * C, greet_line, 0)

    def greet_face(sem):
        def step(i, carry):
            to = (x * Y + y + i) % (X * Y)
            pl.semaphore_signal(
                sem, inc=1, device_id=(grp_of(z, to // Y, c), to % Y), device_id_type=MESH
            )
            return carry

        lax.fori_loop(1, X * Y, step, 0)

    greet_face(barrier)

    dest = dest_ref[...].reshape(1, OWN)
    sub = lax.broadcasted_iota(jnp.int32, (OWN, OWN), 0)
    lane = lax.broadcasted_iota(jnp.int32, (OWN, OWN), 1)
    dest_down = jnp.sum(jnp.where(sub == lane, dest, 0), axis=1, keepdims=True)
    rank = jnp.sum(jnp.where((dest_down == dest) & (sub < lane), 1, 0), axis=0, keepdims=True)
    position = dest * SLOT + rank

    load.wait()
    wide = emb_v[...].astype(jnp.float32)
    norm = jnp.sqrt(jnp.sum(wide * wide, axis=1, keepdims=True)) + 1e-6
    unit[...] = (wide / norm).astype(jnp.bfloat16)

    pl.semaphore_wait(barrier, Z * C - 1 + X * Y - 1)
    greet_face(met_sem)

    def plane_at(p, s):
        back = jnp.where(p == 0, 0, STEPS + p)
        return (z + jnp.where(s == 0, STEPS - p, back)) % Z

    def pack(p):
        first, second = plane_at(p, 0), plane_at(p, 1)
        span = X * C * SLOT
        r = lax.broadcasted_iota(jnp.int32, (2 * span, 1), 0)
        ids = r + jnp.where(r < span, first * span, second * span - span)
        pick = ids == position
        chosen = jnp.dot(
            jnp.where(pick, 1.0, 0.0).astype(jnp.bfloat16), unit[...],
            preferred_element_type=jnp.float32,
        )
        live = jnp.sum(jnp.where(pick, 1.0, 0.0), axis=1, keepdims=True)
        head = lax.broadcasted_iota(jnp.int32, (2 * span, 128), 1) == 0
        for k in range(SUB):
            part = chosen[:, 128 * k : 128 * (k + 1)]
            if k == 0:
                part = jnp.where(head & (live < 0.5), DEAD, part)
            spread[pl.ds(k, 2 * span, stride=SUB), :] = part
        outgoing[pl.ds(p * 2 * span, 2 * span)] = (
            spread[...].reshape(2 * span, SUB, 128).astype(jnp.bfloat16)
        )

    def send(p):
        def one(i, carry):
            s = i % 2
            to_z = plane_at(p, s)
            in_plane = (x * C + c + i // 2) % (X * C)
            to_y = holder_y(to_z, in_plane % C)
            to_g = to_z * (X * C) + in_plane
            src = outgoing.at[pl.ds((p * 2 + s) * (X * C * SLOT) + in_plane * SLOT, SLOT)]
            dst = arrived.at[pl.ds(((p * 2 + s) * PLANE + me) * SLOT, SLOT)]
            mine = (to_g == g) & (to_y == y)

            @pl.when(mine)
            def _():
                pltpu.make_async_copy(src, dst, recv_sem.at[0]).start()

            @pl.when(jnp.logical_not(mine))
            def _():
                pltpu.make_async_remote_copy(
                    src_ref=src, dst_ref=dst, send_sem=send_sem, recv_sem=recv_sem.at[p],
                    device_id=(to_g, to_y), device_id_type=MESH,
                ).start()

            return carry

        lax.fori_loop(0, 2 * X * C, one, 0)

    pack(0)
    pl.semaphore_wait(met_sem, X * Y - 1)

    def step_out(p, carry):
        send(p)

        @pl.when(p < STEPS - 1)
        def _():
            pack(p + 1)

        return carry

    lax.fori_loop(0, STEPS, step_out, 0)

    @pl.when(holder)
    def _():
        rows[...] = jnp.zeros((ROWS, D), jnp.bfloat16)
        sub = lax.broadcasted_iota(jnp.int32, (CHUNK, ROWS), 0)
        lane = lax.broadcasted_iota(jnp.int32, (CHUNK, ROWS), 1)
        shift = lane - sub
        lane1 = lax.broadcasted_iota(jnp.int32, (1, ROWS), 1)

        def take(p, carry):
            penalty, best = carry
            block = arrived.at[pl.ds(pl.multiple_of(p * CHUNK, CHUNK), CHUNK)]
            pltpu.make_async_copy(block, block, recv_sem.at[p]).wait()
            spread_in[...] = block[...].astype(jnp.float32).reshape(CHUNK * SUB, 128)
            here = pl.ds(pl.multiple_of(p * CHUNK, CHUNK), CHUNK)
            for k in range(SUB):
                rows[here, 128 * k : 128 * (k + 1)] = spread_in[
                    pl.ds(k, CHUNK, stride=SUB), :
                ].astype(jnp.bfloat16)
            new = rows[here, :]
            dead = spread_in[pl.ds(0, CHUNK, stride=SUB), :][:, 0:1] > 1.5
            down = jnp.where(dead, LOW, 0.0)
            same = shift == p * CHUNK
            across = jnp.sum(jnp.where(same, down, 0.0), axis=0, keepdims=True)
            inside = (lane1 >= p * CHUNK) & (lane1 < (p + 1) * CHUNK)
            penalty = jnp.where(inside, across, penalty)
            score = lax.dot_general(
                new, rows[...], (((1,), (1,)), ((), ())), preferred_element_type=jnp.float32
            )
            score = jnp.where(same, LOW, score + down + penalty)
            best = jnp.maximum(best, jnp.max(score, axis=0, keepdims=True))
            top = jnp.max(score, axis=1, keepdims=True)
            best = jnp.maximum(best, jnp.max(jnp.where(same, top, LOW), axis=0, keepdims=True))
            return penalty, best

        penalty = jnp.full((1, ROWS), LOW, jnp.float32)
        best = jnp.full((1, ROWS), -1.0, jnp.float32)
        penalty, best = lax.fori_loop(0, STEPS, take, (penalty, best))
        mine = z // Y
        width = PLANE * SLOT
        at = lax.broadcasted_iota(jnp.int32, (8, 128), 0) == mine
        for i in range(Z):
            line = jnp.concatenate(
                [best[:, i * width : (i + 1) * width], jnp.zeros((1, 128 - width), jnp.float32)], axis=1
            )
            ra[i] = jnp.where(at, line, 0.0)

        def answer(i, carry):
            p, s = i // 2, i % 2
            back = jnp.where(p == 0, 0, STEPS - p)
            to_z = (z + jnp.where(s == 0, STEPS + p, back)) % Z

            @pl.when(to_z == z)
            def _():
                pltpu.make_async_copy(ra.at[i], ba.at[mine], a_recv).start()

            @pl.when(to_z != z)
            def _():
                pltpu.make_async_remote_copy(
                    src_ref=ra.at[i], dst_ref=ba.at[mine], send_sem=a_send, recv_sem=a_recv,
                    device_id=(grp_of(to_z, x, c), y), device_id_type=MESH,
                ).start()

            return carry

        lax.fori_loop(0, Z, answer, 0)

    pltpu.make_async_copy(ba, ba, a_recv).wait()
    bs[...] = ba[0] + ba[1] + ba[2] + ba[3]
    bb[me] = bs[...]

    def pass_on(i, carry):
        to = (me + i) % PLANE
        pltpu.make_async_remote_copy(
            src_ref=bs, dst_ref=bb.at[me], send_sem=b_send, recv_sem=b_recv,
            device_id=(grp_of(z, to // (C * Y), (to // Y) % C), to % Y), device_id_type=MESH,
        ).start()
        return carry

    lax.fori_loop(1, PLANE, pass_on, 0)
    others = bb.at[pl.ds(0, PLANE - 1)]
    pltpu.make_async_copy(others, others, b_recv).wait()

    table = bb[...].reshape(PLANE * 8, 128)
    lane = lax.broadcasted_iota(jnp.int32, (PLANE * 8, 128), 1)
    down = [
        jnp.sum(jnp.where(lane == me * SLOT + j, table, 0.0), axis=1, keepdims=True)
        for j in range(SLOT)
    ]
    dz = dest // (X * C)
    dx = (dest // C) % X
    dc = dest % C
    line = ((dx * C + dc) * Y + holder_y(dz, dc)) * 8 + dz // Y
    sub = lax.broadcasted_iota(jnp.int32, (PLANE * 8, OWN), 0)
    value = jnp.where(rank == 0, down[0], jnp.where(rank == 1, down[1], down[2]))
    answer = jnp.sum(jnp.where(sub == line, value, 0.0), axis=0, keepdims=True)
    out_ref[...] = answer.reshape(OWN)

    pltpu.make_async_copy(others, others, b_send).wait()

    @pl.when(holder)
    def _():
        left = ra.at[pl.ds(0, Z - 1)]
        pltpu.make_async_copy(left, left, a_send).wait()
        sent = outgoing.at[pl.ds(0, (GROUPS - 1) * SLOT)]
        pltpu.make_async_copy(sent, sent, send_sem).wait()

    @pl.when(jnp.logical_not(holder))
    def _():
        pltpu.make_async_copy(outgoing, outgoing, send_sem).wait()


def shards(emb, dest):
    dma = pltpu.SemaphoreType.DMA
    return pl.pallas_call(
        body_kernel,
        out_shape=jax.ShapeDtypeStruct((OWN,), jnp.float32),
        in_specs=[
            pl.BlockSpec(memory_space=pl.ANY),
            pl.BlockSpec(memory_space=pltpu.VMEM),
        ],
        out_specs=pl.BlockSpec(memory_space=pltpu.VMEM),
        scratch_shapes=[
            pltpu.VMEM((OWN, D), jnp.bfloat16),
            pltpu.VMEM((OWN, D), jnp.bfloat16),
            pltpu.VMEM((2 * X * C * SLOT * SUB, 128), jnp.float32),
            pltpu.VMEM((GROUPS * SLOT, SUB, 128), jnp.bfloat16),
            pltpu.VMEM((ROWS, SUB, 128), jnp.bfloat16),
            pltpu.VMEM((CHUNK * SUB, 128), jnp.float32),
            pltpu.VMEM((ROWS, D), jnp.bfloat16),
            pltpu.VMEM((Z, 8, 128), jnp.float32),
            pltpu.VMEM((4, 8, 128), jnp.float32),
            pltpu.VMEM((8, 128), jnp.float32),
            pltpu.VMEM((PLANE, 8, 128), jnp.float32),
            dma,
            pltpu.SemaphoreType.REGULAR,
            dma,
            pltpu.SemaphoreType.DMA((STEPS,)),
            dma,
            dma,
            dma,
            dma,
        ],
        compiler_params=pltpu.CompilerParams(
            collective_id=0, has_side_effects=True, vmem_limit_bytes=40 << 20
        ),
        name="dedup",
    )(emb, dest)


def solution(mesh):
    in_specs = (P(("grp", "tile"), None), P(("grp", "tile")))
    out_specs = P(("grp", "tile"))
    return jax.shard_map(shards, mesh=mesh, in_specs=in_specs, out_specs=out_specs, check_vma=False)
```

```python
import jax
import jax.numpy as jnp
from jax import lax
from jax.experimental import pallas as pl
from jax.experimental.pallas import tpu as pltpu
from jax.sharding import PartitionSpec as P

MESH = pl.DeviceIdType.MESH
Z, X, C, Y = 16, 4, 2, 4
PLANE = X * C * Y
NEAR = Z // 4
SLOT = 3
OWN = 256
D = 1024
SUB = D // 128
STEPS = Z // 2
SPAN = X * C * SLOT
CHUNK = 2 * PLANE * SLOT
ROWS = STEPS * CHUNK
GROUPS = Z * X * C
LINES = Z // Y
DEAD = 2.0
LOW = -8.0


def grp_of(z, x, c):
    return (z * X + x) * C + c


def holder_y(z, c):
    return (z + 2 * c) % Y


def offset(e, s):
    d = jnp.where(e < 3, e + 1, 11 - e)
    return jnp.where(s == 0, d, jnp.where(e == 3, 0, Z - d))


def body_kernel(
    emb_ref, dest_ref, out_ref,
    emb_v, dest_v, unit, spread, outgoing, arrived, spread_in, rows, ra, ba, bs, bb,
    in_sem, near_sem, far_sem, send_sem, recv_sem, a_send, a_recv, b_send, b_recv,
):
    g = lax.axis_index("grp")
    y = lax.axis_index("tile")
    z = g // (X * C)
    x = (g // C) % X
    c = g % C
    me = (x * C + c) * Y + y
    holder = y == holder_y(z, c)

    load = pltpu.make_async_copy(emb_ref, emb_v, in_sem.at[0])
    load.start()
    load_dest = pltpu.make_async_copy(dest_ref, dest_v, in_sem.at[1])
    load_dest.start()

    barrier = pltpu.get_barrier_semaphore()

    def greet_line(sem_of):
        def step(d, carry):
            for to in ((z + d) % Z, (z + Z - d) % Z):
                pl.semaphore_signal(
                    sem_of(d), inc=1, device_id=(grp_of(to, x, c), y), device_id_type=MESH
                )
            return carry

        lax.fori_loop(1, NEAR + 1, step, 0)

    greet_line(lambda d: barrier)

    def greet_plane(i, carry):
        to = (me + i) % PLANE
        pl.semaphore_signal(
            barrier, inc=1, device_id=(grp_of(z, to // (C * Y), (to // Y) % C), to % Y),
            device_id_type=MESH,
        )
        return carry

    lax.fori_loop(1, PLANE, greet_plane, 0)

    load_dest.wait()
    dest = dest_v[...].reshape(1, OWN)
    sub = lax.broadcasted_iota(jnp.int32, (OWN, OWN), 0)
    lane = lax.broadcasted_iota(jnp.int32, (OWN, OWN), 1)
    dest_down = jnp.sum(jnp.where(sub == lane, dest, 0), axis=1, keepdims=True)
    rank = jnp.sum(jnp.where((dest_down == dest) & (sub < lane), 1, 0), axis=0, keepdims=True)
    position = dest * SLOT + rank

    load.wait()

    def normalise(i, carry):
        part = pl.ds(pl.multiple_of(i * 32, 32), 32)
        wide = emb_v[part, :].astype(jnp.float32)
        norm = jnp.sqrt(jnp.sum(wide * wide, axis=1, keepdims=True)) + 1e-6
        unit[part, :] = (wide / norm).astype(jnp.bfloat16)
        return carry

    lax.fori_loop(0, OWN // 32, normalise, 0)

    pl.semaphore_wait(barrier, 2 * NEAR + PLANE - 1)
    greet_line(lambda d: near_sem.at[d - 1])

    def pack(e):
        first, second = (z + offset(e, 0)) % Z, (z + offset(e, 1)) % Z
        r = lax.broadcasted_iota(jnp.int32, (2 * SPAN, 1), 0)
        ids = r + jnp.where(r < SPAN, first * SPAN, second * SPAN - SPAN)
        pick = ids == position
        chosen = jnp.dot(
            jnp.where(pick, 1.0, 0.0).astype(jnp.bfloat16), unit[...],
            preferred_element_type=jnp.float32,
        )
        live = jnp.sum(jnp.where(pick, 1.0, 0.0), axis=1, keepdims=True)
        head = lax.broadcasted_iota(jnp.int32, (2 * SPAN, 128), 1) == 0
        for k in range(SUB):
            part = chosen[:, 128 * k : 128 * (k + 1)]
            if k == 0:
                part = jnp.where(head & (live < 0.5), DEAD, part)
            spread[pl.ds(k, 2 * SPAN, stride=SUB), :] = part
        outgoing[pl.ds(e * 2 * SPAN, 2 * SPAN)] = (
            spread[...].reshape(2 * SPAN, SUB, 128).astype(jnp.bfloat16)
        )

    def send(e):
        def one(i, carry):
            s = i % 2
            to_z = (z + offset(e, s)) % Z
            in_plane = (x * C + c + i // 2) % (X * C)
            to_y = holder_y(to_z, in_plane % C)
            to_g = to_z * (X * C) + in_plane
            src = outgoing.at[pl.ds((e * 2 + s) * SPAN + in_plane * SLOT, SLOT)]
            dst = arrived.at[pl.ds(((e * 2 + s) * PLANE + me) * SLOT, SLOT)]
            mine = (to_g == g) & (to_y == y)

            @pl.when(mine)
            def _():
                pltpu.make_async_copy(src, dst, recv_sem.at[3]).start()

            @pl.when(jnp.logical_not(mine))
            def _():
                pltpu.make_async_remote_copy(
                    src_ref=src, dst_ref=dst, send_sem=send_sem, recv_sem=recv_sem.at[e],
                    device_id=(to_g, to_y), device_id_type=MESH,
                ).start()

            return carry

        lax.fori_loop(0, 2 * X * C, one, 0)

    def step_out(e, carry):
        pack(e)

        @pl.when(e < NEAR)
        def _():
            pl.semaphore_wait(near_sem.at[e], 2)

        @pl.when(e == NEAR - 1)
        def _():
            for to in ((z + NEAR) % Z, (z + Z - NEAR) % Z):
                pl.semaphore_signal(
                    far_sem, inc=1, device_id=(grp_of(to, x, c), y), device_id_type=MESH
                )
            pl.semaphore_wait(far_sem, 2)

        send(e)
        return carry

    lax.fori_loop(0, STEPS, step_out, 0)

    @pl.when(holder)
    def _():
        rows[...] = jnp.zeros((ROWS, D), jnp.bfloat16)
        sub = lax.broadcasted_iota(jnp.int32, (CHUNK, ROWS), 0)
        lane = lax.broadcasted_iota(jnp.int32, (CHUNK, ROWS), 1)
        shift = lane - sub
        lane1 = lax.broadcasted_iota(jnp.int32, (1, ROWS), 1)

        def take(e, carry):
            penalty, best = carry
            here = pl.ds(pl.multiple_of(e * CHUNK, CHUNK), CHUNK)
            block = arrived.at[here]
            pltpu.make_async_copy(block, block, recv_sem.at[e]).wait()
            spread_in[...] = block[...].astype(jnp.float32).reshape(CHUNK * SUB, 128)
            for k in range(SUB):
                rows[here, 128 * k : 128 * (k + 1)] = spread_in[
                    pl.ds(k, CHUNK, stride=SUB), :
                ].astype(jnp.bfloat16)
            new = rows[here, :]
            dead = spread_in[pl.ds(0, CHUNK, stride=SUB), :][:, 0:1] > 1.5
            down = jnp.where(dead, LOW, 0.0)
            same = shift == e * CHUNK
            across = jnp.sum(jnp.where(same, down, 0.0), axis=0, keepdims=True)
            inside = (lane1 >= e * CHUNK) & (lane1 < (e + 1) * CHUNK)
            penalty = jnp.where(inside, across, penalty)
            score = lax.dot_general(
                new, rows[...], (((1,), (1,)), ((), ())), preferred_element_type=jnp.float32
            )
            score = jnp.where(same, LOW, score + down + penalty)
            best = jnp.maximum(best, jnp.max(score, axis=0, keepdims=True))
            top = jnp.max(score, axis=1, keepdims=True)
            best = jnp.maximum(best, jnp.max(jnp.where(same, top, LOW), axis=0, keepdims=True))
            return penalty, best

        penalty = jnp.full((1, ROWS), LOW, jnp.float32)
        best = jnp.full((1, ROWS), -1.0, jnp.float32)
        penalty, best = lax.fori_loop(0, STEPS, take, (penalty, best))
        width = PLANE * SLOT
        fill = jnp.zeros((1, 128 - width), jnp.float32)
        for i in range(Z):
            ra[i] = jnp.concatenate([best[:, i * width : (i + 1) * width], fill], axis=1)

        def answer(i, carry):
            e, s = (i // 2 + 3) % STEPS, i % 2
            to_z = (z + Z - offset(e, s)) % Z
            src, dst = ra.at[e * 2 + s], ba.at[z // Y]

            @pl.when(to_z == z)
            def _():
                pltpu.make_async_copy(src, dst, a_recv).start()

            @pl.when(to_z != z)
            def _():
                pltpu.make_async_remote_copy(
                    src_ref=src, dst_ref=dst, send_sem=a_send, recv_sem=a_recv,
                    device_id=(grp_of(to_z, x, c), y), device_id_type=MESH,
                ).start()

            return carry

        lax.fori_loop(0, Z, answer, 0)

    pltpu.make_async_copy(ba, ba, a_recv).wait()
    sub = lax.broadcasted_iota(jnp.int32, (PLANE, 128), 0)
    lane = lax.broadcasted_iota(jnp.int32, (PLANE, 128), 1)
    turned = jnp.zeros((PLANE, 128), jnp.float32)
    for j in range(SLOT):
        its = lane == sub * SLOT + j
        for h in range(LINES):
            column = jnp.sum(jnp.where(its, ba[h], 0.0), axis=1, keepdims=True)
            turned = jnp.where(lane == h * SLOT + j, column, turned)
    bs[...] = turned.reshape(PLANE, 1, 128)

    def pass_on(i, carry):
        to_x, to_y, to_c = (x + 2 + i // (C * Y)) % X, (y + 2 + (i // C) % Y) % Y, (c + i) % C
        to = (to_x * C + to_c) * Y + to_y

        @pl.when(to == me)
        def _():
            pltpu.make_async_copy(bs.at[me], bb.at[me], b_recv).start()

        @pl.when(to != me)
        def _():
            pltpu.make_async_remote_copy(
                src_ref=bs.at[to], dst_ref=bb.at[me], send_sem=b_send, recv_sem=b_recv,
                device_id=(grp_of(z, to_x, to_c), to_y), device_id_type=MESH,
            ).start()

        return carry

    lax.fori_loop(0, PLANE, pass_on, 0)

    dz = dest // (X * C)
    dx = (dest // C) % X
    dc = dest % C
    line = (dx * C + dc) * Y + holder_y(dz, dc)
    spot = (dz // Y) * SLOT + rank
    sub = lax.broadcasted_iota(jnp.int32, (PLANE, OWN), 0)
    pltpu.make_async_copy(bb, bb, b_recv).wait()
    table = bb[...].reshape(PLANE, 128)
    value = jnp.zeros((PLANE, OWN), jnp.float32)
    for k in range(LINES * SLOT):
        value = jnp.where(spot == k, table[:, k : k + 1], value)
    answer = jnp.sum(jnp.where(sub == line, value, 0.0), axis=0, keepdims=True)
    out_ref[...] = answer.reshape(OWN)

    others = bs.at[pl.ds(0, PLANE - 1)]
    pltpu.make_async_copy(others, others, b_send).wait()

    @pl.when(holder)
    def _():
        left = ra.at[pl.ds(0, Z - 1)]
        pltpu.make_async_copy(left, left, a_send).wait()
        sent = outgoing.at[pl.ds(0, (GROUPS - 1) * SLOT)]
        pltpu.make_async_copy(sent, sent, send_sem).wait()

    @pl.when(jnp.logical_not(holder))
    def _():
        pltpu.make_async_copy(outgoing, outgoing, send_sem).wait()


def shards(emb, dest):
    dma = pltpu.SemaphoreType.DMA
    regular = pltpu.SemaphoreType.REGULAR
    return pl.pallas_call(
        body_kernel,
        out_shape=jax.ShapeDtypeStruct((OWN,), jnp.float32),
        in_specs=[pl.BlockSpec(memory_space=pl.ANY)] * 2,
        out_specs=pl.BlockSpec(memory_space=pltpu.VMEM),
        scratch_shapes=[
            pltpu.VMEM((OWN, D), jnp.bfloat16),
            pltpu.VMEM((OWN,), jnp.int32),
            pltpu.VMEM((OWN, D), jnp.bfloat16),
            pltpu.VMEM((2 * SPAN * SUB, 128), jnp.float32),
            pltpu.VMEM((GROUPS * SLOT, SUB, 128), jnp.bfloat16),
            pltpu.VMEM((ROWS, SUB, 128), jnp.bfloat16),
            pltpu.VMEM((CHUNK * SUB, 128), jnp.float32),
            pltpu.VMEM((ROWS, D), jnp.bfloat16),
            pltpu.VMEM((Z, 1, 128), jnp.float32),
            pltpu.VMEM((LINES, 1, 128), jnp.float32),
            pltpu.VMEM((PLANE, 1, 128), jnp.float32),
            pltpu.VMEM((PLANE, 1, 128), jnp.float32),
            pltpu.SemaphoreType.DMA((2,)),
            pltpu.SemaphoreType.REGULAR((NEAR,)),
            regular,
            dma,
            pltpu.SemaphoreType.DMA((STEPS,)),
            dma,
            dma,
            dma,
            dma,
        ],
        compiler_params=pltpu.CompilerParams(
            collective_id=0, has_side_effects=True, vmem_limit_bytes=60 << 20
        ),
        name="dedup",
    )(emb, dest)


def solution(mesh):
    in_specs = (P(("grp", "tile"), None), P(("grp", "tile")))
    out_specs = P(("grp", "tile"))
    return jax.shard_map(shards, mesh=mesh, in_specs=in_specs, out_specs=out_specs, check_vma=False)
```

```python
import jax
import jax.numpy as jnp
from jax import lax
from jax.experimental import pallas as pl
from jax.experimental.pallas import tpu as pltpu
from jax.sharding import PartitionSpec as P

MESH = pl.DeviceIdType.MESH
Z, X, C, Y = 16, 4, 2, 4
PLANE = X * C * Y
NEAR = Z // 4
SLOT = 3
OWN = 256
D = 1024
SUB = D // 128
STEPS = Z // 2
SPAN = X * C * SLOT
CHUNK = 2 * PLANE * SLOT
ROWS = STEPS * CHUNK
GROUPS = Z * X * C
LINES = Z // Y
DEAD = 2.0
LOW = -8.0


def grp_of(z, x, c):
    return (z * X + x) * C + c


def holder_y(z, c):
    return (z + 2 * c) % Y


def offset(e, s):
    d = jnp.where(e < 3, e + 2, jnp.where(e == STEPS - 1, 1, 11 - e))
    return jnp.where(s == 0, d, jnp.where(e == 3, 0, Z - d))


def body_kernel(
    emb_ref, dest_ref, out_ref,
    emb_v, dest_v, unit, spread, outgoing, arrived, spread_in, rows, ra, ba, bs, bb,
    in_sem, near_sem, far_sem, send_sem, recv_sem, a_send, a_recv, b_send, b_recv,
):
    g = lax.axis_index("grp")
    y = lax.axis_index("tile")
    z = g // (X * C)
    x = (g // C) % X
    c = g % C
    me = (x * C + c) * Y + y
    holder = y == holder_y(z, c)

    load = pltpu.make_async_copy(emb_ref, emb_v, in_sem.at[0])
    load.start()
    load_dest = pltpu.make_async_copy(dest_ref, dest_v, in_sem.at[1])
    load_dest.start()

    barrier = pltpu.get_barrier_semaphore()

    def greet_line(sem_of):
        def step(d, carry):
            for to in ((z + d) % Z, (z + Z - d) % Z):
                pl.semaphore_signal(
                    sem_of(d), inc=1, device_id=(grp_of(to, x, c), y), device_id_type=MESH
                )
            return carry

        lax.fori_loop(1, NEAR + 1, step, 0)

    greet_line(lambda d: barrier)

    def mate(i):
        return (x + 2 + i // (C * Y)) % X, (y + 2 + (i // C) % Y) % Y, (c + i) % C

    def greet_plane(i, carry):
        to_x, to_y, to_c = mate(i)

        @pl.when((to_x != x) | (to_y != y) | (to_c != c))
        def _():
            pl.semaphore_signal(
                barrier, inc=1, device_id=(grp_of(z, to_x, to_c), to_y), device_id_type=MESH
            )

        return carry

    lax.fori_loop(0, PLANE, greet_plane, 0)

    load_dest.wait()
    dest = dest_v[...].reshape(1, OWN)
    sub = lax.broadcasted_iota(jnp.int32, (OWN, OWN), 0)
    lane = lax.broadcasted_iota(jnp.int32, (OWN, OWN), 1)
    dest_down = jnp.sum(jnp.where(sub == lane, dest, 0), axis=1, keepdims=True)
    rank = jnp.sum(jnp.where((dest_down == dest) & (sub < lane), 1, 0), axis=0, keepdims=True)
    position = dest * SLOT + rank

    load.wait()

    def normalise(i, carry):
        part = pl.ds(pl.multiple_of(i * 32, 32), 32)
        wide = emb_v[part, :].astype(jnp.float32)
        norm = jnp.sqrt(jnp.sum(wide * wide, axis=1, keepdims=True)) + 1e-6
        unit[part, :] = (wide / norm).astype(jnp.bfloat16)
        return carry

    lax.fori_loop(0, OWN // 32, normalise, 0)

    pl.semaphore_wait(barrier, 2 * NEAR + PLANE - 1)
    greet_line(lambda d: near_sem.at[d - 1])

    def pack(e):
        first, second = (z + offset(e, 0)) % Z, (z + offset(e, 1)) % Z
        r = lax.broadcasted_iota(jnp.int32, (2 * SPAN, 1), 0)
        ids = r + jnp.where(r < SPAN, first * SPAN, second * SPAN - SPAN)
        pick = ids == position
        chosen = jnp.dot(
            jnp.where(pick, 1.0, 0.0).astype(jnp.bfloat16), unit[...],
            preferred_element_type=jnp.float32,
        )
        live = jnp.sum(jnp.where(pick, 1.0, 0.0), axis=1, keepdims=True)
        head = lax.broadcasted_iota(jnp.int32, (2 * SPAN, 128), 1) == 0
        for k in range(SUB):
            part = chosen[:, 128 * k : 128 * (k + 1)]
            if k == 0:
                part = jnp.where(head & (live < 0.5), DEAD, part)
            spread[pl.ds(k, 2 * SPAN, stride=SUB), :] = part
        outgoing[pl.ds(e * 2 * SPAN, 2 * SPAN)] = (
            spread[...].reshape(2 * SPAN, SUB, 128).astype(jnp.bfloat16)
        )

    def send(e):
        def one(i, carry):
            s = i % 2
            to_z = (z + offset(e, s)) % Z
            in_plane = (x * C + c + i // 2) % (X * C)
            to_y = holder_y(to_z, in_plane % C)
            to_g = to_z * (X * C) + in_plane
            src = outgoing.at[pl.ds((e * 2 + s) * SPAN + in_plane * SLOT, SLOT)]
            dst = arrived.at[pl.ds(((e * 2 + s) * PLANE + me) * SLOT, SLOT)]
            mine = (to_g == g) & (to_y == y)

            @pl.when(mine)
            def _():
                pltpu.make_async_copy(src, dst, recv_sem.at[3]).start()

            @pl.when(jnp.logical_not(mine))
            def _():
                pltpu.make_async_remote_copy(
                    src_ref=src, dst_ref=dst, send_sem=send_sem, recv_sem=recv_sem.at[e],
                    device_id=(to_g, to_y), device_id_type=MESH,
                ).start()

            return carry

        lax.fori_loop(0, 2 * X * C, one, 0)

    def step_out(e, carry):
        pack(e)

        @pl.when(e < NEAR - 1)
        def _():
            pl.semaphore_wait(near_sem.at[e + 1], 2)

        @pl.when(e == NEAR - 2)
        def _():
            pl.semaphore_wait(near_sem.at[0], 2)
            for to in ((z + NEAR) % Z, (z + Z - NEAR) % Z):
                pl.semaphore_signal(
                    far_sem, inc=1, device_id=(grp_of(to, x, c), y), device_id_type=MESH
                )

        @pl.when(e == NEAR - 1)
        def _():
            pl.semaphore_wait(far_sem, 2)

        send(e)
        return carry

    lax.fori_loop(0, STEPS, step_out, 0)

    @pl.when(holder)
    def _():
        rows[...] = jnp.zeros((ROWS, D), jnp.bfloat16)
        sub = lax.broadcasted_iota(jnp.int32, (CHUNK, ROWS), 0)
        lane = lax.broadcasted_iota(jnp.int32, (CHUNK, ROWS), 1)
        shift = lane - sub
        lane1 = lax.broadcasted_iota(jnp.int32, (1, ROWS), 1)

        def take(e, carry):
            penalty, best = carry
            here = pl.ds(pl.multiple_of(e * CHUNK, CHUNK), CHUNK)
            block = arrived.at[here]
            pltpu.make_async_copy(block, block, recv_sem.at[e]).wait()
            spread_in[...] = block[...].astype(jnp.float32).reshape(CHUNK * SUB, 128)
            for k in range(SUB):
                rows[here, 128 * k : 128 * (k + 1)] = spread_in[
                    pl.ds(k, CHUNK, stride=SUB), :
                ].astype(jnp.bfloat16)
            new = rows[here, :]
            dead = spread_in[pl.ds(0, CHUNK, stride=SUB), :][:, 0:1] > 1.5
            down = jnp.where(dead, LOW, 0.0)
            same = shift == e * CHUNK
            across = jnp.sum(jnp.where(same, down, 0.0), axis=0, keepdims=True)
            inside = (lane1 >= e * CHUNK) & (lane1 < (e + 1) * CHUNK)
            penalty = jnp.where(inside, across, penalty)
            score = lax.dot_general(
                new, rows[...], (((1,), (1,)), ((), ())), preferred_element_type=jnp.float32
            )
            score = jnp.where(same, LOW, score + down + penalty)
            best = jnp.maximum(best, jnp.max(score, axis=0, keepdims=True))
            top = jnp.max(score, axis=1, keepdims=True)
            best = jnp.maximum(best, jnp.max(jnp.where(same, top, LOW), axis=0, keepdims=True))
            return penalty, best

        penalty = jnp.full((1, ROWS), LOW, jnp.float32)
        best = jnp.full((1, ROWS), -1.0, jnp.float32)
        penalty, best = lax.fori_loop(0, STEPS, take, (penalty, best))
        width = PLANE * SLOT
        fill = jnp.zeros((1, 128 - width), jnp.float32)
        for i in range(Z):
            ra[i] = jnp.concatenate([best[:, i * width : (i + 1) * width], fill], axis=1)

        def answer(i, carry):
            e, s = (i // 2 + 3) % STEPS, i % 2
            to_z = (z + Z - offset(e, s)) % Z
            src, dst = ra.at[e * 2 + s], ba.at[z // Y]

            @pl.when(to_z == z)
            def _():
                pltpu.make_async_copy(src, dst, a_recv).start()

            @pl.when(to_z != z)
            def _():
                pltpu.make_async_remote_copy(
                    src_ref=src, dst_ref=dst, send_sem=a_send, recv_sem=a_recv,
                    device_id=(grp_of(to_z, x, c), y), device_id_type=MESH,
                ).start()

            return carry

        lax.fori_loop(0, Z, answer, 0)

    pltpu.make_async_copy(ba, ba, a_recv).wait()
    sub = lax.broadcasted_iota(jnp.int32, (PLANE, 128), 0)
    lane = lax.broadcasted_iota(jnp.int32, (PLANE, 128), 1)
    turned = jnp.zeros((PLANE, 128), jnp.float32)
    for j in range(SLOT):
        its = lane == sub * SLOT + j
        for h in range(LINES):
            column = jnp.sum(jnp.where(its, ba[h], 0.0), axis=1, keepdims=True)
            turned = jnp.where(lane == h * SLOT + j, column, turned)
    bs[...] = turned.reshape(PLANE, 1, 128)

    def pass_on(i, carry):
        to_x, to_y, to_c = mate(i)
        to = (to_x * C + to_c) * Y + to_y

        @pl.when(to == me)
        def _():
            pltpu.make_async_copy(bs.at[me], bb.at[me], b_recv).start()

        @pl.when(to != me)
        def _():
            pltpu.make_async_remote_copy(
                src_ref=bs.at[to], dst_ref=bb.at[me], send_sem=b_send, recv_sem=b_recv,
                device_id=(grp_of(z, to_x, to_c), to_y), device_id_type=MESH,
            ).start()

        return carry

    lax.fori_loop(0, PLANE, pass_on, 0)

    dz = dest // (X * C)
    dx = (dest // C) % X
    dc = dest % C
    line = (dx * C + dc) * Y + holder_y(dz, dc)
    spot = (dz // Y) * SLOT + rank
    sub = lax.broadcasted_iota(jnp.int32, (PLANE, OWN), 0)
    pltpu.make_async_copy(bb, bb, b_recv).wait()
    table = bb[...].reshape(PLANE, 128)
    value = jnp.zeros((PLANE, OWN), jnp.float32)
    for k in range(LINES * SLOT):
        value = jnp.where(spot == k, table[:, k : k + 1], value)
    answer = jnp.sum(jnp.where(sub == line, value, 0.0), axis=0, keepdims=True)
    out_ref[...] = answer.reshape(OWN)

    others = bs.at[pl.ds(0, PLANE - 1)]
    pltpu.make_async_copy(others, others, b_send).wait()

    @pl.when(holder)
    def _():
        left = ra.at[pl.ds(0, Z - 1)]
        pltpu.make_async_copy(left, left, a_send).wait()
        sent = outgoing.at[pl.ds(0, (GROUPS - 1) * SLOT)]
        pltpu.make_async_copy(sent, sent, send_sem).wait()

    @pl.when(jnp.logical_not(holder))
    def _():
        pltpu.make_async_copy(outgoing, outgoing, send_sem).wait()


def shards(emb, dest):
    dma = pltpu.SemaphoreType.DMA
    regular = pltpu.SemaphoreType.REGULAR
    return pl.pallas_call(
        body_kernel,
        out_shape=jax.ShapeDtypeStruct((OWN,), jnp.float32),
        in_specs=[pl.BlockSpec(memory_space=pltpu.HBM)] * 2,
        out_specs=pl.BlockSpec(memory_space=pltpu.VMEM),
        scratch_shapes=[
            pltpu.VMEM((OWN, D), jnp.bfloat16),
            pltpu.VMEM((OWN,), jnp.int32),
            pltpu.VMEM((OWN, D), jnp.bfloat16),
            pltpu.VMEM((2 * SPAN * SUB, 128), jnp.float32),
            pltpu.VMEM((GROUPS * SLOT, SUB, 128), jnp.bfloat16),
            pltpu.VMEM((ROWS, SUB, 128), jnp.bfloat16),
            pltpu.VMEM((CHUNK * SUB, 128), jnp.float32),
            pltpu.VMEM((ROWS, D), jnp.bfloat16),
            pltpu.VMEM((Z, 1, 128), jnp.float32),
            pltpu.VMEM((LINES, 1, 128), jnp.float32),
            pltpu.VMEM((PLANE, 1, 128), jnp.float32),
            pltpu.VMEM((PLANE, 1, 128), jnp.float32),
            pltpu.SemaphoreType.DMA((2,)),
            pltpu.SemaphoreType.REGULAR((NEAR,)),
            regular,
            dma,
            pltpu.SemaphoreType.DMA((STEPS,)),
            dma,
            dma,
            dma,
            dma,
        ],
        compiler_params=pltpu.CompilerParams(
            collective_id=0, has_side_effects=True, vmem_limit_bytes=40 << 20
        ),
        name="dedup",
    )(emb, dest)


def solution(mesh):
    in_specs = (P(("grp", "tile"), None), P(("grp", "tile")))
    out_specs = P(("grp", "tile"))
    return jax.shard_map(shards, mesh=mesh, in_specs=in_specs, out_specs=out_specs, check_vma=False)
```

```python
import jax
import jax.numpy as jnp
from jax import lax
from jax.experimental import pallas as pl
from jax.experimental.pallas import tpu as pltpu
from jax.sharding import PartitionSpec as P

MESH = pl.DeviceIdType.MESH
Z, X, C, Y = 16, 4, 2, 4
PLANE = X * C * Y
NEAR = Z // 4
FAR = Z // 4
SLOT = 3
OWN = 256
D = 1024
SUB = D // 128
STEPS = Z // 2
SPAN = X * C * SLOT
CHUNK = 2 * PLANE * SLOT
ROWS = STEPS * CHUNK
GROUPS = Z * X * C
LINES = Z // Y
DEAD = 2.0
LOW = -8.0


def grp_of(z, x, c):
    return (z * X + x) * C + c


def holder_y(z, c):
    return (z + 2 * c) % Y


def body_kernel(
    emb_ref, dest_ref, out_ref,
    emb_v, dest_v, unit, spread, outgoing, relay, arrived, spread_in, rows, ra, ba, bs, bb,
    in_sem, near_sem, far_sem, send_sem, recv_sem, relay_send, relay_recv, on_send, a_send, a_recv, b_send, b_recv,
):
    g = lax.axis_index("grp")
    y = lax.axis_index("tile")
    z = g // (X * C)
    x = (g // C) % X
    c = g % C
    me = (x * C + c) * Y + y
    holder = y == holder_y(z, c)

    load = pltpu.make_async_copy(emb_ref, emb_v, in_sem.at[0])
    load.start()
    load_dest = pltpu.make_async_copy(dest_ref, dest_v, in_sem.at[1])
    load_dest.start()

    barrier = pltpu.get_barrier_semaphore()

    def greet_line(sem_of):
        def step(d, carry):
            for to in ((z + d) % Z, (z + Z - d) % Z):
                pl.semaphore_signal(
                    sem_of(d), inc=1, device_id=(grp_of(to, x, c), y), device_id_type=MESH
                )
            return carry

        lax.fori_loop(1, NEAR + 1, step, 0)

    greet_line(lambda d: barrier)

    def mate(i):
        return (x + 2 + i // (C * Y)) % X, (y + 2 + (i // C) % Y) % Y, (c + i) % C

    def greet_plane(i, carry):
        to_x, to_y, to_c = mate(i)

        @pl.when((to_x != x) | (to_y != y) | (to_c != c))
        def _():
            pl.semaphore_signal(
                barrier, inc=1, device_id=(grp_of(z, to_x, to_c), to_y), device_id_type=MESH
            )

        return carry

    lax.fori_loop(0, PLANE, greet_plane, 0)

    load_dest.wait()
    dest = dest_v[...].reshape(1, OWN)
    sub = lax.broadcasted_iota(jnp.int32, (OWN, OWN), 0)
    lane = lax.broadcasted_iota(jnp.int32, (OWN, OWN), 1)
    dest_down = jnp.sum(jnp.where(sub == lane, dest, 0), axis=1, keepdims=True)
    rank = jnp.sum(jnp.where((dest_down == dest) & (sub < lane), 1, 0), axis=0, keepdims=True)
    position = dest * SLOT + rank

    load.wait()

    def normalise(i, carry):
        part = pl.ds(pl.multiple_of(i * 32, 32), 32)
        wide = emb_v[part, :].astype(jnp.float32)
        norm = jnp.sqrt(jnp.sum(wide * wide, axis=1, keepdims=True)) + 1e-6
        unit[part, :] = (wide / norm).astype(jnp.bfloat16)
        return carry

    lax.fori_loop(0, OWN // 32, normalise, 0)

    pl.semaphore_wait(barrier, 2 * NEAR + PLANE - 1)
    greet_line(lambda d: near_sem.at[d - 1])

    def up(d):
        return (z + d) % Z

    def down(d):
        return (z + Z - d) % Z

    def pack(e):
        first, second = up(e + 1), jnp.where(e == STEPS - 1, z, down(e + 1))
        r = lax.broadcasted_iota(jnp.int32, (2 * SPAN, 1), 0)
        ids = r + jnp.where(r < SPAN, first * SPAN, second * SPAN - SPAN)
        pick = ids == position
        chosen = jnp.dot(
            jnp.where(pick, 1.0, 0.0).astype(jnp.bfloat16), unit[...],
            preferred_element_type=jnp.float32,
        )
        live = jnp.sum(jnp.where(pick, 1.0, 0.0), axis=1, keepdims=True)
        head = lax.broadcasted_iota(jnp.int32, (2 * SPAN, 128), 1) == 0
        for k in range(SUB):
            part = chosen[:, 128 * k : 128 * (k + 1)]
            if k == 0:
                part = jnp.where(head & (live < 0.5), DEAD, part)
            spread[pl.ds(k, 2 * SPAN, stride=SUB), :] = part
        outgoing[pl.ds(e * 2 * SPAN, 2 * SPAN)] = (
            spread[...].reshape(2 * SPAN, SUB, 128).astype(jnp.bfloat16)
        )

    def post(src, to_z, in_plane, half, e, sem):
        dst = arrived.at[pl.ds((half * PLANE + me) * SLOT, SLOT)]
        to_y = holder_y(to_z, in_plane % C)
        pltpu.make_async_remote_copy(
            src_ref=src, dst_ref=dst, send_sem=sem, recv_sem=recv_sem.at[e],
            device_id=(to_z * (X * C) + in_plane, to_y), device_id_type=MESH,
        ).start()

    def from_outgoing(half, in_plane):
        return outgoing.at[pl.ds(half * SPAN + in_plane * SLOT, SLOT)]

    def send(e):
        def one(i, carry):
            s = i % 2
            in_plane = (x * C + c + i // 2) % (X * C)
            half = e * 2 + s
            post(
                from_outgoing(half, in_plane), jnp.where(s == 0, up(e + 1), down(e + 1)),
                in_plane, half, e, send_sem,
            )
            return carry

        lax.fori_loop(0, 2 * X * C, one, 0)

    def send_here():
        half, e = 2 * STEPS - 1, STEPS - 1

        def one(i, carry):
            in_plane = (x * C + c + i) % (X * C)
            mine = (in_plane == x * C + c) & holder
            src = from_outgoing(half, in_plane)

            @pl.when(mine)
            def _():
                dst = arrived.at[pl.ds((half * PLANE + me) * SLOT, SLOT)]
                pltpu.make_async_copy(src, dst, recv_sem.at[e]).start()

            @pl.when(jnp.logical_not(mine))
            def _():
                post(src, z, in_plane, half, e, send_sem)

            return carry

        lax.fori_loop(0, X * C, one, 0)

    def send_relay(k):
        e = STEPS - 1 - k

        def hop(to_z, src, dst):
            pltpu.make_async_remote_copy(
                src_ref=src, dst_ref=dst, send_sem=relay_send, recv_sem=relay_recv.at[k],
                device_id=(grp_of(to_z, x, c), y), device_id_type=MESH,
            ).start()

        @pl.when(k == 0)
        def _():
            lower = outgoing.at[pl.ds(2 * e * SPAN, SPAN // 2)]
            upper = outgoing.at[pl.ds(2 * e * SPAN + SPAN // 2, SPAN // 2)]
            hop(up(1), lower, relay.at[0, pl.ds(0, SPAN // 2)])
            hop(down(1), upper, relay.at[1, pl.ds(SPAN // 2, SPAN // 2)])

        @pl.when(k > 0)
        def _():
            hop(up(1), outgoing.at[pl.ds(2 * e * SPAN, SPAN)], relay.at[2 * k])
            hop(down(1), outgoing.at[pl.ds((2 * e + 1) * SPAN, SPAN)], relay.at[2 * k + 1])

    def pass_relay(k, carry):
        e = STEPS - 1 - k

        @pl.when(k == 0)
        def _():
            pltpu.make_async_copy(relay.at[0], relay.at[0], relay_recv.at[0]).wait()

        @pl.when(k > 0)
        def _():
            both = relay.at[pl.ds(2 * k, 2)]
            pltpu.make_async_copy(both, both, relay_recv.at[k]).wait()

        def one(i, carry):
            s = i % 2
            in_plane = (x * C + c + i // 2) % (X * C)
            half = 2 * e + jnp.where(k == 0, 0, s)

            @pl.when((k > 0) | (in_plane // (X * C // 2) == s))
            def _():
                post(
                    relay.at[2 * k + s, pl.ds(in_plane * SLOT, SLOT)],
                    jnp.where(s == 0, up(e), down(e)), in_plane, half, e, on_send,
                )

            return carry

        lax.fori_loop(0, 2 * X * C, one, 0)
        return carry

    def step_out(i, carry):
        e = jnp.where(i < FAR, STEPS - 1 - i, jnp.where(i == STEPS - 1, 0, i - FAR + 1))
        pack(e)

        @pl.when(i < FAR)
        def _():
            send_relay(i)

        @pl.when((i >= FAR) & (i < STEPS - 1))
        def _():
            pl.semaphore_wait(near_sem.at[e], 2)

        @pl.when(i == STEPS - 2)
        def _():
            pl.semaphore_wait(near_sem.at[0], 2)
            for to in (up(NEAR), down(NEAR)):
                pl.semaphore_signal(
                    far_sem, inc=1, device_id=(grp_of(to, x, c), y), device_id_type=MESH
                )

        @pl.when(i == STEPS - 1)
        def _():
            pl.semaphore_wait(far_sem, 2)
            lax.fori_loop(0, FAR, pass_relay, 0)

        @pl.when(i >= FAR)
        def _():
            send(e)

        @pl.when(i == FAR)
        def _():
            send_here()

        return carry

    lax.fori_loop(0, STEPS, step_out, 0)

    @pl.when(holder)
    def _():
        rows[...] = jnp.zeros((ROWS, D), jnp.bfloat16)
        sub = lax.broadcasted_iota(jnp.int32, (CHUNK, ROWS), 0)
        lane = lax.broadcasted_iota(jnp.int32, (CHUNK, ROWS), 1)
        shift = lane - sub
        lane1 = lax.broadcasted_iota(jnp.int32, (1, ROWS), 1)

        def take(i, carry):
            penalty, best = carry
            e = jnp.where(i < FAR - 1, i + 1, jnp.where(i == STEPS - 1, 0, STEPS + FAR - 2 - i))
            here = pl.ds(pl.multiple_of(e * CHUNK, CHUNK), CHUNK)
            block = arrived.at[here]
            pltpu.make_async_copy(block, block, recv_sem.at[e]).wait()
            spread_in[...] = block[...].astype(jnp.float32).reshape(CHUNK * SUB, 128)
            for k in range(SUB):
                rows[here, 128 * k : 128 * (k + 1)] = spread_in[
                    pl.ds(k, CHUNK, stride=SUB), :
                ].astype(jnp.bfloat16)
            new = rows[here, :]
            dead = spread_in[pl.ds(0, CHUNK, stride=SUB), :][:, 0:1] > 1.5
            minus = jnp.where(dead, LOW, 0.0)
            same = shift == e * CHUNK
            across = jnp.sum(jnp.where(same, minus, 0.0), axis=0, keepdims=True)
            inside = (lane1 >= e * CHUNK) & (lane1 < (e + 1) * CHUNK)
            penalty = jnp.where(inside, across, penalty)
            score = lax.dot_general(
                new, rows[...], (((1,), (1,)), ((), ())), preferred_element_type=jnp.float32
            )
            score = jnp.where(same, LOW, score + minus + penalty)
            best = jnp.maximum(best, jnp.max(score, axis=0, keepdims=True))
            top = jnp.max(score, axis=1, keepdims=True)
            best = jnp.maximum(best, jnp.max(jnp.where(same, top, LOW), axis=0, keepdims=True))
            return penalty, best

        penalty = jnp.full((1, ROWS), LOW, jnp.float32)
        best = jnp.full((1, ROWS), -1.0, jnp.float32)
        penalty, best = lax.fori_loop(0, STEPS, take, (penalty, best))
        width = PLANE * SLOT
        fill = jnp.zeros((1, 128 - width), jnp.float32)
        for i in range(Z):
            ra[i] = jnp.concatenate([best[:, i * width : (i + 1) * width], fill], axis=1)

        def answer(i, carry):
            e, s = STEPS - 1 - i // 2, i % 2
            to_z = jnp.where(s == 0, down(e + 1), jnp.where(e == STEPS - 1, z, up(e + 1)))
            src, dst = ra.at[e * 2 + s], ba.at[z // Y]

            @pl.when(to_z == z)
            def _():
                pltpu.make_async_copy(src, dst, a_recv).start()

            @pl.when(to_z != z)
            def _():
                pltpu.make_async_remote_copy(
                    src_ref=src, dst_ref=dst, send_sem=a_send, recv_sem=a_recv,
                    device_id=(grp_of(to_z, x, c), y), device_id_type=MESH,
                ).start()

            return carry

        lax.fori_loop(0, Z, answer, 0)

    pltpu.make_async_copy(ba, ba, a_recv).wait()
    sub = lax.broadcasted_iota(jnp.int32, (PLANE, 128), 0)
    lane = lax.broadcasted_iota(jnp.int32, (PLANE, 128), 1)
    turned = jnp.zeros((PLANE, 128), jnp.float32)
    for j in range(SLOT):
        its = lane == sub * SLOT + j
        for h in range(LINES):
            column = jnp.sum(jnp.where(its, ba[h], 0.0), axis=1, keepdims=True)
            turned = jnp.where(lane == h * SLOT + j, column, turned)
    bs[...] = turned.reshape(PLANE, 1, 128)

    def pass_on(i, carry):
        to_x, to_y, to_c = mate(i)
        to = (to_x * C + to_c) * Y + to_y

        @pl.when(to == me)
        def _():
            pltpu.make_async_copy(bs.at[me], bb.at[me], b_recv).start()

        @pl.when(to != me)
        def _():
            pltpu.make_async_remote_copy(
                src_ref=bs.at[to], dst_ref=bb.at[me], send_sem=b_send, recv_sem=b_recv,
                device_id=(grp_of(z, to_x, to_c), to_y), device_id_type=MESH,
            ).start()

        return carry

    lax.fori_loop(0, PLANE, pass_on, 0)

    dz = dest // (X * C)
    dx = (dest // C) % X
    dc = dest % C
    line = (dx * C + dc) * Y + holder_y(dz, dc)
    spot = (dz // Y) * SLOT + rank
    sub = lax.broadcasted_iota(jnp.int32, (PLANE, OWN), 0)
    pltpu.make_async_copy(bb, bb, b_recv).wait()
    table = bb[...].reshape(PLANE, 128)
    value = jnp.zeros((PLANE, OWN), jnp.float32)
    for k in range(LINES * SLOT):
        value = jnp.where(spot == k, table[:, k : k + 1], value)
    answer = jnp.sum(jnp.where(sub == line, value, 0.0), axis=0, keepdims=True)
    out_ref[...] = answer.reshape(OWN)

    others = bs.at[pl.ds(0, PLANE - 1)]
    pltpu.make_async_copy(others, others, b_send).wait()

    straight = 2 * FAR * SPAN + SPAN
    by_relay = 2 * FAR * SPAN - SPAN

    def all_left(count, sem):
        gone = outgoing.at[pl.ds(0, count)]
        pltpu.make_async_copy(gone, gone, sem).wait()

    all_left(by_relay, relay_send)
    all_left(by_relay, on_send)

    @pl.when(holder)
    def _():
        left = ra.at[pl.ds(0, Z - 1)]
        pltpu.make_async_copy(left, left, a_send).wait()
        all_left(straight - SLOT, send_sem)

    @pl.when(jnp.logical_not(holder))
    def _():
        all_left(straight, send_sem)


def shards(emb, dest):
    dma = pltpu.SemaphoreType.DMA
    regular = pltpu.SemaphoreType.REGULAR
    return pl.pallas_call(
        body_kernel,
        out_shape=jax.ShapeDtypeStruct((OWN,), jnp.float32),
        in_specs=[pl.BlockSpec(memory_space=pl.ANY)] * 2,
        out_specs=pl.BlockSpec(memory_space=pltpu.VMEM),
        scratch_shapes=[
            pltpu.VMEM((OWN, D), jnp.bfloat16),
            pltpu.VMEM((OWN,), jnp.int32),
            pltpu.VMEM((OWN, D), jnp.bfloat16),
            pltpu.VMEM((2 * SPAN * SUB, 128), jnp.float32),
            pltpu.VMEM((GROUPS * SLOT, SUB, 128), jnp.bfloat16),
            pltpu.VMEM((2 * FAR, SPAN, SUB, 128), jnp.bfloat16),
            pltpu.VMEM((ROWS, SUB, 128), jnp.bfloat16),
            pltpu.VMEM((CHUNK * SUB, 128), jnp.float32),
            pltpu.VMEM((ROWS, D), jnp.bfloat16),
            pltpu.VMEM((Z, 1, 128), jnp.float32),
            pltpu.VMEM((LINES, 1, 128), jnp.float32),
            pltpu.VMEM((PLANE, 1, 128), jnp.float32),
            pltpu.VMEM((PLANE, 1, 128), jnp.float32),
            pltpu.SemaphoreType.DMA((2,)),
            pltpu.SemaphoreType.REGULAR((NEAR,)),
            regular,
            dma,
            pltpu.SemaphoreType.DMA((STEPS,)),
            dma,
            pltpu.SemaphoreType.DMA((FAR,)),
            dma,
            dma,
            dma,
            dma,
            dma,
        ],
        compiler_params=pltpu.CompilerParams(
            collective_id=0, has_side_effects=True, vmem_limit_bytes=60 << 20
        ),
        name="dedup",
    )(emb, dest)


def solution(mesh):
    in_specs = (P(("grp", "tile"), None), P(("grp", "tile")))
    out_specs = P(("grp", "tile"))
    return jax.shard_map(shards, mesh=mesh, in_specs=in_specs, out_specs=out_specs, check_vma=False)
```

```python
import jax
import jax.numpy as jnp
from jax import lax
from jax.experimental import pallas as pl
from jax.experimental.pallas import tpu as pltpu
from jax.sharding import PartitionSpec as P

MESH = pl.DeviceIdType.MESH
Z, X, C, Y = 16, 4, 2, 4
PLANE = X * C * Y
HOPS = Z // 2
SLOT = 3
OWN = 256
D = 1024
SUB = D // 128
STEPS = Z // 2
SPAN = X * C * SLOT
CHUNK = 2 * PLANE * SLOT
ROWS = STEPS * CHUNK
GROUPS = Z * X * C
LINES = Z // Y
DEAD = 2.0
LOW = -8.0


def grp_of(z, x, c):
    return (z * X + x) * C + c


def holder_y(z, c):
    return (z + 2 * c) % Y


def body_kernel(
    emb_ref, dest_ref, out_ref,
    emb_v, dest_v, unit, spread, outgoing, moving, arrived, spread_in, new_v, rows, pen_v, best_v, ra, ba, bs, bb,
    in_sem, near_sem, send_sem, recv_sem, move_send, move_recv, a_send, a_recv, b_send, b_recv,
):
    g = lax.axis_index("grp")
    y = lax.axis_index("tile")
    z = g // (X * C)
    x = (g // C) % X
    c = g % C
    me = (x * C + c) * Y + y
    holder = y == holder_y(z, c)

    load = pltpu.make_async_copy(emb_ref, emb_v, in_sem.at[0])
    load.start()
    load_dest = pltpu.make_async_copy(dest_ref, dest_v, in_sem.at[1])
    load_dest.start()

    barrier = pltpu.get_barrier_semaphore()

    def up(d):
        return (z + d) % Z

    def down(d):
        return (z + Z - d) % Z

    def greet_neighbours(sem):
        for to in (up(1), down(1)):
            pl.semaphore_signal(
                sem, inc=1, device_id=(grp_of(to, x, c), y), device_id_type=MESH
            )

    greet_neighbours(barrier)

    def mate(i):
        return (x + 2 + i // (C * Y)) % X, (y + 2 + (i // C) % Y) % Y, (c + i) % C

    def greet_plane(i, carry):
        to_x, to_y, to_c = mate(i)

        @pl.when((to_x != x) | (to_y != y) | (to_c != c))
        def _():
            pl.semaphore_signal(
                barrier, inc=1, device_id=(grp_of(z, to_x, to_c), to_y), device_id_type=MESH
            )

        return carry

    lax.fori_loop(0, PLANE, greet_plane, 0)

    load_dest.wait()
    dest = dest_v[...].reshape(1, OWN)
    sub = lax.broadcasted_iota(jnp.int32, (OWN, OWN), 0)
    lane = lax.broadcasted_iota(jnp.int32, (OWN, OWN), 1)
    dest_down = jnp.sum(jnp.where(sub == lane, dest, 0), axis=1, keepdims=True)
    rank = jnp.sum(jnp.where((dest_down == dest) & (sub < lane), 1, 0), axis=0, keepdims=True)
    position = dest * SLOT + rank

    load.wait()

    def normalise(i, carry):
        part = pl.ds(pl.multiple_of(i * 32, 32), 32)
        wide = emb_v[part, :].astype(jnp.float32)
        norm = jnp.sqrt(jnp.sum(wide * wide, axis=1, keepdims=True)) + 1e-6
        unit[part, :] = (wide / norm).astype(jnp.bfloat16)
        return carry

    lax.fori_loop(0, OWN // 32, normalise, 0)

    pl.semaphore_wait(barrier, 2 + PLANE - 1)
    greet_neighbours(near_sem)

    def pack(e):
        first, second = up(e + 1), jnp.where(e == STEPS - 1, z, down(e + 1))
        r = lax.broadcasted_iota(jnp.int32, (2 * SPAN, 1), 0)
        ids = r + jnp.where(r < SPAN, first * SPAN, second * SPAN - SPAN)
        pick = ids == position
        chosen = jnp.dot(
            jnp.where(pick, 1.0, 0.0).astype(jnp.bfloat16), unit[...],
            preferred_element_type=jnp.float32,
        )
        live = jnp.sum(jnp.where(pick, 1.0, 0.0), axis=1, keepdims=True)
        head = lax.broadcasted_iota(jnp.int32, (2 * SPAN, 128), 1) == 0
        for k in range(SUB):
            part = chosen[:, 128 * k : 128 * (k + 1)]
            if k == 0:
                part = jnp.where(head & (live < 0.5), DEAD, part)
            spread[pl.ds(k, 2 * SPAN, stride=SUB), :] = part
        outgoing[pl.ds(e * 2 * SPAN, 2 * SPAN)] = (
            spread[...].reshape(2 * SPAN, SUB, 128).astype(jnp.bfloat16)
        )

    def post(src, to_z, in_plane, half, e, sem):
        dst = arrived.at[pl.ds((half * PLANE + me) * SLOT, SLOT)]
        to_y = holder_y(to_z, in_plane % C)
        pltpu.make_async_remote_copy(
            src_ref=src, dst_ref=dst, send_sem=sem, recv_sem=recv_sem.at[e],
            device_id=(to_z * (X * C) + in_plane, to_y), device_id_type=MESH,
        ).start()

    def from_outgoing(half, in_plane):
        return outgoing.at[pl.ds(half * SPAN + in_plane * SLOT, SLOT)]

    def send_here():
        half, e = 2 * STEPS - 1, STEPS - 1

        def one(i, carry):
            in_plane = (x * C + c + i) % (X * C)
            mine = (in_plane == x * C + c) & holder
            src = from_outgoing(half, in_plane)

            @pl.when(mine)
            def _():
                dst = arrived.at[pl.ds((half * PLANE + me) * SLOT, SLOT)]
                pltpu.make_async_copy(src, dst, recv_sem.at[e]).start()

            @pl.when(jnp.logical_not(mine))
            def _():
                post(src, z, in_plane, half, e, send_sem)

            return carry

        lax.fori_loop(0, X * C, one, 0)

    def go(a, r, s, block):
        far = a + r == HOPS
        mid = SPAN // 2
        spot = a * (HOPS - 1) + r - 2

        def hop(part):
            pltpu.make_async_remote_copy(
                src_ref=part(block), dst_ref=part(moving.at[s, spot]),
                send_sem=move_send, recv_sem=move_recv.at[s, spot],
                device_id=(grp_of(up(1) if s == 0 else down(1), x, c), y), device_id_type=MESH,
            ).start()

        @pl.when((r >= 2) & jnp.logical_not(far))
        def _():
            hop(lambda ref: ref)

        @pl.when((r >= 2) & far)
        def _():
            hop(lambda ref: ref.at[pl.ds(s * mid, mid)])

        @pl.when(r == 1)
        def _():
            def one(i, carry):
                in_plane = (x * C + c + i) % (X * C)

                @pl.when(jnp.logical_not(far) | (in_plane // (X * C // 2) == s))
                def _():
                    post(
                        block.at[pl.ds(in_plane * SLOT, SLOT)], up(1) if s == 0 else down(1),
                        in_plane, 2 * a + jnp.where(far, 0, s), a, send_sem,
                    )

                return carry

            lax.fori_loop(0, X * C, one, 0)

    def first(k, carry):
        e = STEPS - 1 - k
        pack(e)

        @pl.when(e == 0)
        def _():
            pl.semaphore_wait(near_sem, 2)

        for s in range(2):
            half = 2 * e + jnp.where(e == STEPS - 1, 0, s)
            go(0, e + 1, s, outgoing.at[pl.ds(half * SPAN, SPAN)])
        return carry

    lax.fori_loop(0, STEPS, first, 0)
    send_here()

    def forward(a):
        def one(j, carry):
            r = HOPS - a - j
            far = j == 0
            mid = SPAN // 2
            for s in range(2):
                spot = (a - 1) * (HOPS - 1) + r - 1
                block = moving.at[s, spot]

                @pl.when(far)
                def _():
                    part = block.at[pl.ds(s * mid, mid)]
                    pltpu.make_async_copy(part, part, move_recv.at[s, spot]).wait()

                @pl.when(jnp.logical_not(far))
                def _():
                    pltpu.make_async_copy(block, block, move_recv.at[s, spot]).wait()

                go(a, r, s, block)
            return carry

        lax.fori_loop(0, HOPS - a, one, 0)

    @pl.when(holder)
    def _():
        rows[...] = jnp.zeros((ROWS, D), jnp.bfloat16)
        pen_v[...] = jnp.full((1, ROWS), LOW, jnp.float32)
        best_v[...] = jnp.full((1, ROWS), -1.0, jnp.float32)

    def take(e):
        here = pl.ds(pl.multiple_of(e * CHUNK, CHUNK), CHUNK)
        block = arrived.at[here]
        pltpu.make_async_copy(block, block, recv_sem.at[e]).wait()
        spread_in[...] = block[...].astype(jnp.float32).reshape(CHUNK * SUB, 128)
        for k in range(SUB):
            new_v[:, 128 * k : 128 * (k + 1)] = spread_in[
                pl.ds(k, CHUNK, stride=SUB), :
            ].astype(jnp.bfloat16)
        new = new_v[...]
        dead = spread_in[pl.ds(0, CHUNK, stride=SUB), :][:, 0:1] > 1.5
        minus = jnp.where(dead, LOW, 0.0)
        sub = lax.broadcasted_iota(jnp.int32, (CHUNK, CHUNK), 0)
        lane = lax.broadcasted_iota(jnp.int32, (CHUNK, CHUNK), 1)
        same = sub == lane

        def scores(others):
            return lax.dot_general(
                new, others, (((1,), (1,)), ((), ())), preferred_element_type=jnp.float32
            )

        old = scores(rows[...])
        own = jnp.where(same, LOW, scores(new) + minus)
        best = jnp.maximum(best_v[...], jnp.max(old + minus, axis=0, keepdims=True))
        top = jnp.max(old + pen_v[...], axis=1, keepdims=True)
        mine = jnp.maximum(
            jnp.max(own, axis=0, keepdims=True),
            jnp.max(jnp.where(same, top, LOW), axis=0, keepdims=True),
        )
        across = jnp.sum(jnp.where(same, minus, 0.0), axis=0, keepdims=True)
        at = lax.broadcasted_iota(jnp.int32, (1, ROWS), 1)
        inside = (at >= e * CHUNK) & (at < (e + 1) * CHUNK)
        best_v[...] = jnp.where(inside, jnp.concatenate([mine] * STEPS, axis=1), best)
        pen_v[...] = jnp.where(inside, jnp.concatenate([across] * STEPS, axis=1), pen_v[...])
        rows[here, :] = new

    def step_on(a, carry):
        @pl.when(a < HOPS)
        def _():
            forward(a)

        @pl.when(holder & (a >= 2))
        def _():
            take(a - 2)

        return carry

    lax.fori_loop(1, HOPS + 2, step_on, 0)

    @pl.when(holder)
    def _():
        best = jnp.maximum(best_v[...], -1.0)
        width = PLANE * SLOT
        fill = jnp.zeros((1, 128 - width), jnp.float32)
        for i in range(Z):
            ra[i] = jnp.concatenate([best[:, i * width : (i + 1) * width], fill], axis=1)

        def answer(i, carry):
            e, s = STEPS - 1 - i // 2, i % 2
            to_z = jnp.where(s == 0, down(e + 1), jnp.where(e == STEPS - 1, z, up(e + 1)))
            src, dst = ra.at[e * 2 + s], ba.at[z // Y]

            @pl.when(to_z == z)
            def _():
                pltpu.make_async_copy(src, dst, a_recv).start()

            @pl.when(to_z != z)
            def _():
                pltpu.make_async_remote_copy(
                    src_ref=src, dst_ref=dst, send_sem=a_send, recv_sem=a_recv,
                    device_id=(grp_of(to_z, x, c), y), device_id_type=MESH,
                ).start()

            return carry

        lax.fori_loop(0, Z, answer, 0)

    pltpu.make_async_copy(ba, ba, a_recv).wait()
    sub = lax.broadcasted_iota(jnp.int32, (PLANE, 128), 0)
    lane = lax.broadcasted_iota(jnp.int32, (PLANE, 128), 1)
    turned = jnp.zeros((PLANE, 128), jnp.float32)
    for j in range(SLOT):
        its = lane == sub * SLOT + j
        for h in range(LINES):
            column = jnp.sum(jnp.where(its, ba[h], 0.0), axis=1, keepdims=True)
            turned = jnp.where(lane == h * SLOT + j, column, turned)
    bs[...] = turned.reshape(PLANE, 1, 128)

    def pass_on(i, carry):
        to_x, to_y, to_c = mate(i)
        to = (to_x * C + to_c) * Y + to_y

        @pl.when(to == me)
        def _():
            pltpu.make_async_copy(bs.at[me], bb.at[me], b_recv).start()

        @pl.when(to != me)
        def _():
            pltpu.make_async_remote_copy(
                src_ref=bs.at[to], dst_ref=bb.at[me], send_sem=b_send, recv_sem=b_recv,
                device_id=(grp_of(z, to_x, to_c), to_y), device_id_type=MESH,
            ).start()

        return carry

    lax.fori_loop(0, PLANE, pass_on, 0)

    dz = dest // (X * C)
    dx = (dest // C) % X
    dc = dest % C
    line = (dx * C + dc) * Y + holder_y(dz, dc)
    spot = (dz // Y) * SLOT + rank
    sub = lax.broadcasted_iota(jnp.int32, (PLANE, OWN), 0)
    pltpu.make_async_copy(bb, bb, b_recv).wait()
    table = bb[...].reshape(PLANE, 128)
    value = jnp.zeros((PLANE, OWN), jnp.float32)
    for k in range(LINES * SLOT):
        value = jnp.where(spot == k, table[:, k : k + 1], value)
    answer = jnp.sum(jnp.where(sub == line, value, 0.0), axis=0, keepdims=True)
    out_ref[...] = answer.reshape(OWN)

    others = bs.at[pl.ds(0, PLANE - 1)]
    pltpu.make_async_copy(others, others, b_send).wait()

    pltpu.make_async_copy(moving.at[0], moving.at[0], move_send).wait()

    def all_left(count, sem):
        gone = outgoing.at[pl.ds(0, count)]
        pltpu.make_async_copy(gone, gone, sem).wait()

    @pl.when(holder)
    def _():
        left = ra.at[pl.ds(0, Z - 1)]
        pltpu.make_async_copy(left, left, a_send).wait()
        all_left((GROUPS - 1) * SLOT, send_sem)

    @pl.when(jnp.logical_not(holder))
    def _():
        all_left(GROUPS * SLOT, send_sem)


def shards(emb, dest):
    dma = pltpu.SemaphoreType.DMA
    regular = pltpu.SemaphoreType.REGULAR
    return pl.pallas_call(
        body_kernel,
        out_shape=jax.ShapeDtypeStruct((OWN,), jnp.float32),
        in_specs=[pl.BlockSpec(memory_space=pl.ANY)] * 2,
        out_specs=pl.BlockSpec(memory_space=pltpu.VMEM),
        scratch_shapes=[
            pltpu.VMEM((OWN, D), jnp.bfloat16),
            pltpu.VMEM((OWN,), jnp.int32),
            pltpu.VMEM((OWN, D), jnp.bfloat16),
            pltpu.VMEM((2 * SPAN * SUB, 128), jnp.float32),
            pltpu.VMEM((GROUPS * SLOT, SUB, 128), jnp.bfloat16),
            pltpu.VMEM((2, (HOPS - 1) ** 2, SPAN, SUB, 128), jnp.bfloat16),
            pltpu.VMEM((ROWS, SUB, 128), jnp.bfloat16),
            pltpu.VMEM((CHUNK * SUB, 128), jnp.float32),
            pltpu.VMEM((CHUNK, D), jnp.bfloat16),
            pltpu.VMEM((ROWS, D), jnp.bfloat16),
            pltpu.VMEM((1, ROWS), jnp.float32),
            pltpu.VMEM((1, ROWS), jnp.float32),
            pltpu.VMEM((Z, 1, 128), jnp.float32),
            pltpu.VMEM((LINES, 1, 128), jnp.float32),
            pltpu.VMEM((PLANE, 1, 128), jnp.float32),
            pltpu.VMEM((PLANE, 1, 128), jnp.float32),
            pltpu.SemaphoreType.DMA((2,)),
            regular,
            dma,
            pltpu.SemaphoreType.DMA((STEPS,)),
            dma,
            pltpu.SemaphoreType.DMA((2, (HOPS - 1) ** 2)),
            dma,
            dma,
            dma,
            dma,
        ],
        compiler_params=pltpu.CompilerParams(
            collective_id=0, has_side_effects=True, vmem_limit_bytes=60 << 20
        ),
        name="dedup",
    )(emb, dest)


def solution(mesh):
    in_specs = (P(("grp", "tile"), None), P(("grp", "tile")))
    out_specs = P(("grp", "tile"))
    return jax.shard_map(shards, mesh=mesh, in_specs=in_specs, out_specs=out_specs, check_vma=False)
```

```python
import jax
import jax.numpy as jnp
from jax import lax
from jax.experimental import pallas as pl
from jax.experimental.pallas import tpu as pltpu
from jax.sharding import PartitionSpec as P

MESH = pl.DeviceIdType.MESH
Z, X, C, Y = 16, 4, 2, 4
PLANE = X * C * Y
HOPS = Z // 2
SLOT = 3
OWN = 256
D = 1024
SUB = D // 128
STEPS = Z // 2
SPAN = X * C * SLOT
CHUNK = 2 * PLANE * SLOT
ROWS = STEPS * CHUNK
GROUPS = Z * X * C
LINES = Z // Y
FIRST = ((0, 5), (0, 8), (0, 7), (0, 6))
JOBS = (
    ((0, 2), (1, 4), (1, 7), (1, 6), (1, 5), (1, 1), (2, 3), (2, 6), (2, 5), (0, 1)),
    ((2, 4), (3, 5), (3, 2), (0, 3)),
    ((3, 4), (4, 4), (0, 4), (4, 1), (3, 3), (5, 3), (1, 2)),
    ((4, 3), (1, 3), (6, 2), (4, 2), (2, 1), (5, 2), (7, 1), (2, 2), (5, 1), (6, 1), (3, 1)),
)
ORDER = (2, 1, 5, 3, 8, 6, 7, 4)
PACKS = (5, 8, 7, 6, 2, 1, 3, 4)
ROUNDS = 5
DEAD = 2.0
LOW = -8.0


def grp_of(z, x, c):
    return (z * X + x) * C + c


def holder_y(z, c):
    return (z + 2 * c) % Y


def body_kernel(
    emb_ref, dest_ref, out_ref,
    emb_v, dest_v, unit, spread, outgoing, moving, arrived, spread_in, new_v, rows, pen_v, best_v, ra, ba, bs, bb,
    in_sem, met_sem, send_sem, recv_sem, move_send, move_recv, a_send, a_recv, b_send, b_recv,
):
    g = lax.axis_index("grp")
    y = lax.axis_index("tile")
    z = g // (X * C)
    x = (g // C) % X
    c = g % C
    me = (x * C + c) * Y + y
    holder = y == holder_y(z, c)

    load = pltpu.make_async_copy(emb_ref, emb_v, in_sem.at[0])
    load.start()
    load_dest = pltpu.make_async_copy(dest_ref, dest_v, in_sem.at[1])
    load_dest.start()

    def up(d):
        return (z + d) % Z

    def down(d):
        return (z + Z - d) % Z

    def mate(i):
        return (x + 2 + i // (C * Y)) % X, (y + 2 + (i // C) % Y) % Y, (c + i) % C

    barrier = pltpu.get_barrier_semaphore()
    neighbours = (
        (grp_of(up(1), x, c), y), (grp_of(down(1), x, c), y),
        (grp_of(z, (x + 1) % X, c), y), (grp_of(z, (x + X - 1) % X, c), y),
        (g, (y + 1) % Y), (g, (y + Y - 1) % Y),
        (grp_of(z, x, 1 - c), y),
    )

    def greet(sem):
        for to in neighbours:
            pl.semaphore_signal(sem, inc=1, device_id=to, device_id_type=MESH)

    def meet(k):
        pl.semaphore_wait(met_sem.at[k], len(neighbours))
        if k + 1 < ROUNDS:
            greet(met_sem.at[k + 1])

    greet(barrier)

    load_dest.wait()
    dest = dest_v[...].reshape(1, OWN)
    sub = lax.broadcasted_iota(jnp.int32, (OWN, OWN), 0)
    lane = lax.broadcasted_iota(jnp.int32, (OWN, OWN), 1)
    dest_down = jnp.sum(jnp.where(sub == lane, dest, 0), axis=1, keepdims=True)
    rank = jnp.sum(jnp.where((dest_down == dest) & (sub < lane), 1, 0), axis=0, keepdims=True)
    position = dest * SLOT + rank

    load.wait()

    def normalise(i, carry):
        part = pl.ds(pl.multiple_of(i * 32, 32), 32)
        wide = emb_v[part, :].astype(jnp.float32)
        norm = jnp.sqrt(jnp.sum(wide * wide, axis=1, keepdims=True)) + 1e-6
        unit[part, :] = (wide / norm).astype(jnp.bfloat16)
        return carry

    lax.fori_loop(0, OWN // 32, normalise, 0)

    def pack(e):
        first, second = up(e + 1), jnp.where(e == STEPS - 1, z, down(e + 1))
        r = lax.broadcasted_iota(jnp.int32, (2 * SPAN, 1), 0)
        ids = r + jnp.where(r < SPAN, first * SPAN, second * SPAN - SPAN)
        pick = ids == position
        chosen = jnp.dot(
            jnp.where(pick, 1.0, 0.0).astype(jnp.bfloat16), unit[...],
            preferred_element_type=jnp.float32,
        )
        live = jnp.sum(jnp.where(pick, 1.0, 0.0), axis=1, keepdims=True)
        head = lax.broadcasted_iota(jnp.int32, (2 * SPAN, 128), 1) == 0
        for k in range(SUB):
            part = chosen[:, 128 * k : 128 * (k + 1)]
            if k == 0:
                part = jnp.where(head & (live < 0.5), DEAD, part)
            spread[pl.ds(k, 2 * SPAN, stride=SUB), :] = part
        outgoing[pl.ds(e * 2 * SPAN, 2 * SPAN)] = (
            spread[...].reshape(2 * SPAN, SUB, 128).astype(jnp.bfloat16)
        )

    def post(src, to_z, in_plane, half, e, sem):
        dst = arrived.at[pl.ds((half * PLANE + me) * SLOT, SLOT)]
        to_y = holder_y(to_z, in_plane % C)
        pltpu.make_async_remote_copy(
            src_ref=src, dst_ref=dst, send_sem=sem, recv_sem=recv_sem.at[e],
            device_id=(to_z * (X * C) + in_plane, to_y), device_id_type=MESH,
        ).start()

    def from_outgoing(half, in_plane):
        return outgoing.at[pl.ds(half * SPAN + in_plane * SLOT, SLOT)]

    def send_here():
        half, e = 2 * STEPS - 1, STEPS - 1

        def one(i, carry):
            in_plane = (x * C + c + i) % (X * C)
            mine = (in_plane == x * C + c) & holder
            src = from_outgoing(half, in_plane)

            @pl.when(mine)
            def _():
                dst = arrived.at[pl.ds((half * PLANE + me) * SLOT, SLOT)]
                pltpu.make_async_copy(src, dst, recv_sem.at[e]).start()

            @pl.when(jnp.logical_not(mine))
            def _():
                post(src, z, in_plane, half, e, send_sem)

            return carry

        lax.fori_loop(0, X * C, one, 0)

    mid = SPAN // 2

    def spot(a, r):
        return a * (HOPS - 1) + r - 2

    def go(a, r):
        d = a + r
        blocks = []
        for s in range(2):
            part = (lambda ref: ref.at[pl.ds(s * mid, mid)]) if d == HOPS else (lambda ref: ref)
            if a == 0:
                half = 2 * (d - 1) + (0 if d == HOPS else s)
                block = outgoing.at[pl.ds(half * SPAN, SPAN)]
            else:
                block = moving.at[s, spot(a - 1, r + 1)]
                pltpu.make_async_copy(
                    part(block), part(block), move_recv.at[s, spot(a - 1, r + 1)]
                ).wait()
            blocks.append(block)
            if r >= 2:
                pltpu.make_async_remote_copy(
                    src_ref=part(block), dst_ref=part(moving.at[s, spot(a, r)]),
                    send_sem=move_send, recv_sem=move_recv.at[s, spot(a, r)],
                    device_id=neighbours[s], device_id_type=MESH,
                ).start()
        if r > 1:
            return

        def one(i, carry):
            for s in range(2):
                if d == HOPS:
                    in_plane = s * (X * C // 2) + (x * C + c + i) % (X * C // 2)
                    half = 2 * (d - 1)
                else:
                    in_plane = (x * C + c + i) % (X * C)
                    half = 2 * (d - 1) + s
                post(
                    blocks[s].at[pl.ds(in_plane * SLOT, SLOT)], up(1) if s == 0 else down(1),
                    in_plane, half, d - 1, send_sem,
                )
            return carry

        lax.fori_loop(0, X * C // (2 if d == HOPS else 1), one, 0)

    def chosen_of(table, i):
        value = table[0]
        for k in range(1, len(table)):
            value = jnp.where(i == k, table[k], value)
        return value

    def lay_out(i, carry):
        pack(chosen_of(PACKS, i) - 1)

        @pl.when(i == 0)
        def _():
            pl.semaphore_wait(barrier, len(neighbours))
            greet(met_sem.at[0])

        for k, job in enumerate(FIRST):

            @pl.when(i == k)
            def _():
                go(*job)

        return carry

    lax.fori_loop(0, STEPS, lay_out, 0)

    @pl.when(holder)
    def _():
        rows[...] = jnp.zeros((ROWS, D), jnp.bfloat16)
        pen_v[...] = jnp.full((1, ROWS), LOW, jnp.float32)
        best_v[...] = jnp.full((1, ROWS), -1.0, jnp.float32)

    def take(e):
        here = pl.ds(pl.multiple_of(e * CHUNK, CHUNK), CHUNK)
        block = arrived.at[here]
        pltpu.make_async_copy(block, block, recv_sem.at[e]).wait()
        spread_in[...] = block[...].astype(jnp.float32).reshape(CHUNK * SUB, 128)
        for k in range(SUB):
            new_v[:, 128 * k : 128 * (k + 1)] = spread_in[
                pl.ds(k, CHUNK, stride=SUB), :
            ].astype(jnp.bfloat16)
        new = new_v[...]
        dead = spread_in[pl.ds(0, CHUNK, stride=SUB), :][:, 0:1] > 1.5
        minus = jnp.where(dead, LOW, 0.0)
        sub = lax.broadcasted_iota(jnp.int32, (CHUNK, CHUNK), 0)
        lane = lax.broadcasted_iota(jnp.int32, (CHUNK, CHUNK), 1)
        same = sub == lane

        def scores(others):
            return lax.dot_general(
                new, others, (((1,), (1,)), ((), ())), preferred_element_type=jnp.float32
            )

        old = scores(rows[...])
        own = jnp.where(same, LOW, scores(new) + minus)
        best = jnp.maximum(best_v[...], jnp.max(old + minus, axis=0, keepdims=True))
        top = jnp.max(old + pen_v[...], axis=1, keepdims=True)
        mine = jnp.maximum(
            jnp.max(own, axis=0, keepdims=True),
            jnp.max(jnp.where(same, top, LOW), axis=0, keepdims=True),
        )
        across = jnp.sum(jnp.where(same, minus, 0.0), axis=0, keepdims=True)
        at = lax.broadcasted_iota(jnp.int32, (1, ROWS), 1)
        inside = (at >= e * CHUNK) & (at < (e + 1) * CHUNK)
        best_v[...] = jnp.where(inside, jnp.concatenate([mine] * STEPS, axis=1), best)
        pen_v[...] = jnp.where(inside, jnp.concatenate([across] * STEPS, axis=1), pen_v[...])
        rows[here, :] = new

    def phase(i, carry):
        for k, jobs in enumerate(JOBS):

            @pl.when(i == k)
            def _():
                for n, job in enumerate(jobs):
                    if k == 0 and n < ROUNDS:
                        meet(n)
                    if k == 0 and n == ROUNDS:
                        send_here()
                    go(*job)

        @pl.when(holder)
        def _():
            take(chosen_of(ORDER, i) - 1)

        return carry

    lax.fori_loop(0, STEPS, phase, 0)

    @pl.when(holder)
    def _():
        best = jnp.maximum(best_v[...], -1.0)
        width = PLANE * SLOT
        fill = jnp.zeros((1, 128 - width), jnp.float32)
        for i in range(Z):
            ra[i] = jnp.concatenate([best[:, i * width : (i + 1) * width], fill], axis=1)

        def answer(i, carry):
            e, s = STEPS - 1 - i // 2, i % 2
            to_z = jnp.where(s == 0, down(e + 1), jnp.where(e == STEPS - 1, z, up(e + 1)))
            src, dst = ra.at[e * 2 + s], ba.at[z // Y]

            @pl.when(to_z == z)
            def _():
                pltpu.make_async_copy(src, dst, a_recv).start()

            @pl.when(to_z != z)
            def _():
                pltpu.make_async_remote_copy(
                    src_ref=src, dst_ref=dst, send_sem=a_send, recv_sem=a_recv,
                    device_id=(grp_of(to_z, x, c), y), device_id_type=MESH,
                ).start()

            return carry

        lax.fori_loop(0, Z, answer, 0)

    pltpu.make_async_copy(ba, ba, a_recv).wait()
    sub = lax.broadcasted_iota(jnp.int32, (PLANE, 128), 0)
    lane = lax.broadcasted_iota(jnp.int32, (PLANE, 128), 1)
    turned = jnp.zeros((PLANE, 128), jnp.float32)
    for j in range(SLOT):
        its = lane == sub * SLOT + j
        for h in range(LINES):
            column = jnp.sum(jnp.where(its, ba[h], 0.0), axis=1, keepdims=True)
            turned = jnp.where(lane == h * SLOT + j, column, turned)
    bs[...] = turned.reshape(PLANE, 1, 128)

    def pass_on(i, carry):
        to_x, to_y, to_c = mate(i)
        to = (to_x * C + to_c) * Y + to_y

        @pl.when(to == me)
        def _():
            pltpu.make_async_copy(bs.at[me], bb.at[me], b_recv).start()

        @pl.when(to != me)
        def _():
            pltpu.make_async_remote_copy(
                src_ref=bs.at[to], dst_ref=bb.at[me], send_sem=b_send, recv_sem=b_recv,
                device_id=(grp_of(z, to_x, to_c), to_y), device_id_type=MESH,
            ).start()

        return carry

    lax.fori_loop(0, PLANE, pass_on, 0)

    dz = dest // (X * C)
    dx = (dest // C) % X
    dc = dest % C
    line = (dx * C + dc) * Y + holder_y(dz, dc)
    spot = (dz // Y) * SLOT + rank
    sub = lax.broadcasted_iota(jnp.int32, (PLANE, OWN), 0)
    pltpu.make_async_copy(bb, bb, b_recv).wait()
    table = bb[...].reshape(PLANE, 128)
    value = jnp.zeros((PLANE, OWN), jnp.float32)
    for k in range(LINES * SLOT):
        value = jnp.where(spot == k, table[:, k : k + 1], value)
    answer = jnp.sum(jnp.where(sub == line, value, 0.0), axis=0, keepdims=True)
    out_ref[...] = answer.reshape(OWN)

    others = bs.at[pl.ds(0, PLANE - 1)]
    pltpu.make_async_copy(others, others, b_send).wait()

    pltpu.make_async_copy(moving.at[0], moving.at[0], move_send).wait()

    def all_left(count, sem):
        gone = outgoing.at[pl.ds(0, count)]
        pltpu.make_async_copy(gone, gone, sem).wait()

    @pl.when(holder)
    def _():
        left = ra.at[pl.ds(0, Z - 1)]
        pltpu.make_async_copy(left, left, a_send).wait()
        all_left((GROUPS - 1) * SLOT, send_sem)

    @pl.when(jnp.logical_not(holder))
    def _():
        all_left(GROUPS * SLOT, send_sem)


def shards(emb, dest):
    dma = pltpu.SemaphoreType.DMA
    return pl.pallas_call(
        body_kernel,
        out_shape=jax.ShapeDtypeStruct((OWN,), jnp.float32),
        in_specs=[pl.BlockSpec(memory_space=pl.ANY)] * 2,
        out_specs=pl.BlockSpec(memory_space=pltpu.VMEM),
        scratch_shapes=[
            pltpu.VMEM((OWN, D), jnp.bfloat16),
            pltpu.VMEM((OWN,), jnp.int32),
            pltpu.VMEM((OWN, D), jnp.bfloat16),
            pltpu.VMEM((2 * SPAN * SUB, 128), jnp.float32),
            pltpu.VMEM((GROUPS * SLOT, SUB, 128), jnp.bfloat16),
            pltpu.VMEM((2, (HOPS - 1) ** 2, SPAN, SUB, 128), jnp.bfloat16),
            pltpu.VMEM((ROWS, SUB, 128), jnp.bfloat16),
            pltpu.VMEM((CHUNK * SUB, 128), jnp.float32),
            pltpu.VMEM((CHUNK, D), jnp.bfloat16),
            pltpu.VMEM((ROWS, D), jnp.bfloat16),
            pltpu.VMEM((1, ROWS), jnp.float32),
            pltpu.VMEM((1, ROWS), jnp.float32),
            pltpu.VMEM((Z, 1, 128), jnp.float32),
            pltpu.VMEM((LINES, 1, 128), jnp.float32),
            pltpu.VMEM((PLANE, 1, 128), jnp.float32),
            pltpu.VMEM((PLANE, 1, 128), jnp.float32),
            pltpu.SemaphoreType.DMA((2,)),
            pltpu.SemaphoreType.REGULAR((ROUNDS,)),
            dma,
            pltpu.SemaphoreType.DMA((STEPS,)),
            dma,
            pltpu.SemaphoreType.DMA((2, (HOPS - 1) ** 2)),
            dma,
            dma,
            dma,
            dma,
        ],
        compiler_params=pltpu.CompilerParams(
            collective_id=0, has_side_effects=True, vmem_limit_bytes=60 << 20
        ),
        name="dedup",
    )(emb, dest)


def solution(mesh):
    in_specs = (P(("grp", "tile"), None), P(("grp", "tile")))
    out_specs = P(("grp", "tile"))
    return jax.shard_map(shards, mesh=mesh, in_specs=in_specs, out_specs=out_specs, check_vma=False)
```

```python
import jax
import jax.numpy as jnp
from jax import lax
from jax.experimental import pallas as pl
from jax.experimental.pallas import tpu as pltpu
from jax.sharding import PartitionSpec as P

MESH = pl.DeviceIdType.MESH
Z, X, C, Y = 16, 4, 2, 4
CHIPS = X * Y
PLANE = CHIPS * C
SLOT = 3
OWN = 256
D = 1024
SUB = D // 128
STEPS = Z // 2
HOPS = Z // 2
HERE = X * C
SPAN = HERE * SLOT
HALF = PLANE * SLOT
CHUNK = 2 * HALF
ROWS = STEPS * CHUNK
LINES = Z // 2
JOBS = (
    (0, 3), (0, 8), (0, 4), (0, 7), (0, 6), (1, 2), (1, 7), (1, 3), (1, 6), (1, 5), (2, 1), (2, 6),
    (2, 2), (2, 5), (0, 5), (2, 4), (3, 5), (3, 1), (3, 4), (1, 4), (3, 3), (4, 4), (0, 2), (4, 3),
    (2, 3), (4, 2), (5, 3), (1, 1), (5, 2), (3, 2), (5, 1), (6, 2), (0, 1), (6, 1), (4, 1), (7, 1),
)
ORDER = (3, 4, 2, 6, 1, 7, 5, 8)
PACKS = (3, 8, 4, 7, 6, 5, 2, 1)
ROUNDS = 5
DEAD = 2.0
LOW = -8.0


def grp_of(z, x, c):
    return (z * X + x) * C + c


def holder_y(z, k):
    return (z + 2 * k) % Y


def chosen_of(table, i):
    value = table[0]
    for k in range(1, len(table)):
        value = jnp.where(i == k, table[k], value)
    return value


def body_kernel(
    emb_ref, dest_ref, out_ref,
    emb_v, dest_v, unit, spread, own, outgoing, moving, arrived, spread_in, new_v, rows, pen_v, best_v,
    ra, ba, bs, bb,
    in_sem, met_sem, hand_send, hand_recv, send_sem, recv_sem, move_send, move_recv,
    a_send, a_recv, b_send, b_recv,
):
    g = lax.axis_index("grp")
    y = lax.axis_index("tile")
    z = g // (X * C)
    x = (g // C) % X
    c = g % C
    chip = x * Y + y
    me = chip * C + c
    carrier = c == 1
    keeper = c == 0
    holder = keeper & ((y == holder_y(z, 0)) | (y == holder_y(z, 1)))

    load = pltpu.make_async_copy(emb_ref, emb_v, in_sem.at[0])
    load.start()
    load_dest = pltpu.make_async_copy(dest_ref, dest_v, in_sem.at[1])
    load_dest.start()

    def up(d):
        return (z + d) % Z

    def down(d):
        return (z + Z - d) % Z

    barrier = pltpu.get_barrier_semaphore()
    mate = (grp_of(z, x, 1 - c), y)
    neighbours = (
        (grp_of(up(1), x, c), y), (grp_of(down(1), x, c), y),
        (grp_of(z, (x + 1) % X, c), y), (grp_of(z, (x + X - 1) % X, c), y),
        (g, (y + 1) % Y), (g, (y + Y - 1) % Y),
        mate,
    )

    def greet(sem):
        for to in neighbours:
            pl.semaphore_signal(sem, inc=1, device_id=to, device_id_type=MESH)

    def meet(k):
        pl.semaphore_wait(met_sem.at[k], len(neighbours))
        if k + 1 < ROUNDS:
            greet(met_sem.at[k + 1])

    greet(barrier)

    load_dest.wait()
    dest = dest_v[...].reshape(1, OWN)
    sub = lax.broadcasted_iota(jnp.int32, (OWN, OWN), 0)
    lane = lax.broadcasted_iota(jnp.int32, (OWN, OWN), 1)
    dest_down = jnp.sum(jnp.where(sub == lane, dest, 0), axis=1, keepdims=True)
    rank = jnp.sum(jnp.where((dest_down == dest) & (sub < lane), 1, 0), axis=0, keepdims=True)
    position = dest * SLOT + rank

    load.wait()

    def normalise(i, carry):
        part = pl.ds(pl.multiple_of(i * 32, 32), 32)
        wide = emb_v[part, :].astype(jnp.float32)
        norm = jnp.sqrt(jnp.sum(wide * wide, axis=1, keepdims=True)) + 1e-6
        unit[part, :] = (wide / norm).astype(jnp.bfloat16)
        return carry

    lax.fori_loop(0, OWN // 32, normalise, 0)

    def pack(e):
        first, second = up(e + 1), jnp.where(e == STEPS - 1, z, down(e + 1))
        r = lax.broadcasted_iota(jnp.int32, (2 * SPAN, 1), 0)
        ids = r + jnp.where(r < SPAN, first * SPAN, second * SPAN - SPAN)
        pick = ids == position
        chosen = jnp.dot(
            jnp.where(pick, 1.0, 0.0).astype(jnp.bfloat16), unit[...],
            preferred_element_type=jnp.float32,
        )
        live = jnp.sum(jnp.where(pick, 1.0, 0.0), axis=1, keepdims=True)
        head = lax.broadcasted_iota(jnp.int32, (2 * SPAN, 128), 1) == 0
        for k in range(SUB):
            part = chosen[:, 128 * k : 128 * (k + 1)]
            if k == 0:
                part = jnp.where(head & (live < 0.5), DEAD, part)
            spread[pl.ds(k, 2 * SPAN, stride=SUB), :] = part
        own[pl.ds(2 * e, 2)] = (
            spread[...].reshape(2, HERE, SLOT, SUB, 128).astype(jnp.bfloat16)
        )

    def lay_out(i, carry):
        e = chosen_of(PACKS, i) - 1
        pack(e)
        both = pl.ds(2 * e, 2)

        @pl.when(i == 0)
        def _():
            pl.semaphore_wait(barrier, len(neighbours))
            greet(met_sem.at[0])

        @pl.when(carrier)
        def _():
            pltpu.make_async_copy(
                own.at[both], outgoing.at[both, :, 1], hand_recv.at[e]
            ).start()

        @pl.when(keeper)
        def _():
            pltpu.make_async_remote_copy(
                src_ref=own.at[both], dst_ref=outgoing.at[both, :, 0],
                send_sem=hand_send, recv_sem=hand_recv.at[e],
                device_id=mate, device_id_type=MESH,
            ).start()

        return carry

    lax.fori_loop(0, STEPS, lay_out, 0)

    def post(src, to_z, in_plane, half, e):
        pltpu.make_async_remote_copy(
            src_ref=src, dst_ref=arrived.at[half, chip], send_sem=send_sem, recv_sem=recv_sem.at[e],
            device_id=(grp_of(to_z, in_plane // C, 0), holder_y(to_z, in_plane % C)),
            device_id_type=MESH,
        ).start()

    def send_here():
        def one(i, carry):
            in_plane = (x * C + c + i) % HERE
            post(outgoing.at[2 * STEPS - 1, in_plane], z, in_plane, 2 * STEPS - 1, STEPS - 1)
            return carry

        lax.fori_loop(0, HERE, one, 0)

    mid = HERE // 2

    def spot(a, r):
        return a * (HOPS - 1) + r - 2

    def go(a, r):
        d = a + r
        blocks = []
        for s in range(2):
            part = (lambda ref: ref.at[pl.ds(s * mid, mid)]) if d == HOPS else (lambda ref: ref)
            if a == 0:
                block = outgoing.at[2 * (d - 1) + (0 if d == HOPS else s)]
            else:
                block = moving.at[s, spot(a - 1, r + 1)]
                pltpu.make_async_copy(
                    part(block), part(block), move_recv.at[s, spot(a - 1, r + 1)]
                ).wait()
            blocks.append(block)
            if r >= 2:
                pltpu.make_async_remote_copy(
                    src_ref=part(block), dst_ref=part(moving.at[s, spot(a, r)]),
                    send_sem=move_send, recv_sem=move_recv.at[s, spot(a, r)],
                    device_id=neighbours[s], device_id_type=MESH,
                ).start()
        if r > 1:
            return

        def one(i, carry):
            for s in range(2):
                if d == HOPS:
                    in_plane = s * mid + (x + y + i) % mid
                    half = 2 * (d - 1)
                else:
                    in_plane = (2 * x + y + i) % HERE
                    half = 2 * (d - 1) + s
                post(
                    blocks[s].at[in_plane], up(1) if s == 0 else down(1), in_plane, half, d - 1
                )
            return carry

        lax.fori_loop(0, mid if d == HOPS else HERE, one, 0)

    @pl.when(carrier)
    def _():
        for n, job in enumerate(JOBS):
            if 5 <= n < 5 + ROUNDS:
                meet(n - 5)
            if n == 5 + ROUNDS:
                send_here()
            if job[0] == 0:
                e = job[1] - 1
                both = outgoing.at[pl.ds(2 * e, 2)]
                pltpu.make_async_copy(both, both, hand_recv.at[e]).wait()
            go(*job)

    @pl.when(keeper)
    def _():
        for k in range(ROUNDS):
            meet(k)

    def take(e):
        block = arrived.at[pl.ds(2 * e, 2)]
        pltpu.make_async_copy(block, block, recv_sem.at[e]).wait()
        spread_in[...] = block[...].astype(jnp.float32).reshape(CHUNK * SUB, 128)
        for k in range(SUB):
            new_v[:, 128 * k : 128 * (k + 1)] = spread_in[
                pl.ds(k, CHUNK, stride=SUB), :
            ].astype(jnp.bfloat16)
        new = new_v[...]
        dead = spread_in[pl.ds(0, CHUNK, stride=SUB), :][:, 0:1] > 1.5
        minus = jnp.where(dead, LOW, 0.0)
        sub = lax.broadcasted_iota(jnp.int32, (CHUNK, CHUNK), 0)
        lane = lax.broadcasted_iota(jnp.int32, (CHUNK, CHUNK), 1)
        same = sub == lane

        def scores(others):
            return lax.dot_general(
                new, others, (((1,), (1,)), ((), ())), preferred_element_type=jnp.float32
            )

        old = scores(rows[...])
        within = jnp.where(same, LOW, scores(new) + minus)
        best = jnp.maximum(best_v[...], jnp.max(old + minus, axis=0, keepdims=True))
        top = jnp.max(old + pen_v[...], axis=1, keepdims=True)
        mine = jnp.maximum(
            jnp.max(within, axis=0, keepdims=True),
            jnp.max(jnp.where(same, top, LOW), axis=0, keepdims=True),
        )
        across = jnp.sum(jnp.where(same, minus, 0.0), axis=0, keepdims=True)
        at = lax.broadcasted_iota(jnp.int32, (1, ROWS), 1)
        inside = (at >= e * CHUNK) & (at < (e + 1) * CHUNK)
        best_v[...] = jnp.where(inside, jnp.concatenate([mine] * STEPS, axis=1), best)
        pen_v[...] = jnp.where(inside, jnp.concatenate([across] * STEPS, axis=1), pen_v[...])
        rows[pl.ds(pl.multiple_of(e * CHUNK, CHUNK), CHUNK), :] = new

    @pl.when(holder)
    def _():
        rows[...] = jnp.zeros((ROWS, D), jnp.bfloat16)
        pen_v[...] = jnp.full((1, ROWS), LOW, jnp.float32)
        best_v[...] = jnp.full((1, ROWS), -1.0, jnp.float32)

        def compare(i, carry):
            take(chosen_of(ORDER, i) - 1)
            return carry

        lax.fori_loop(0, STEPS, compare, 0)
        best = jnp.maximum(best_v[...], -1.0)
        fill = jnp.zeros((1, 128 - HALF), jnp.float32)
        for i in range(Z):
            ra[i] = jnp.concatenate([best[:, i * HALF : (i + 1) * HALF], fill], axis=1)

        def answer(i, carry):
            e, s = STEPS - 1 - i // 2, i % 2
            to_z = jnp.where(s == 0, down(e + 1), jnp.where(e == STEPS - 1, z, up(e + 1)))
            src, dst = ra.at[e * 2 + s], ba.at[z // 2]

            @pl.when(to_z == z)
            def _():
                pltpu.make_async_copy(src, dst, a_recv).start()

            @pl.when(to_z != z)
            def _():
                pltpu.make_async_remote_copy(
                    src_ref=src, dst_ref=dst, send_sem=a_send, recv_sem=a_recv,
                    device_id=(grp_of(to_z, x, 0), y), device_id_type=MESH,
                ).start()

            return carry

        lax.fori_loop(0, Z, answer, 0)

    @pl.when(keeper)
    def _():
        pltpu.make_async_copy(ba, ba, a_recv).wait()
        sub = lax.broadcasted_iota(jnp.int32, (PLANE, 128), 0)
        lane = lax.broadcasted_iota(jnp.int32, (PLANE, 128), 1)
        turned = jnp.zeros((PLANE, 128), jnp.float32)
        for j in range(SLOT):
            its = lane == sub * SLOT + j
            for h in range(LINES):
                column = jnp.sum(jnp.where(its, ba[h], 0.0), axis=1, keepdims=True)
                turned = jnp.where(lane == h * SLOT + j, column, turned)
        bs[...] = turned.reshape(PLANE, 1, 128)

        def pass_on(i, carry):
            to_x, to_y, to_c = (x + 2 + i // (C * Y)) % X, (y + 2 + (i // C) % Y) % Y, (c + i) % C
            to = (to_x * Y + to_y) * C + to_c

            @pl.when(to == me)
            def _():
                pltpu.make_async_copy(bs.at[me], bb.at[chip], b_recv).start()

            @pl.when(to != me)
            def _():
                pltpu.make_async_remote_copy(
                    src_ref=bs.at[to], dst_ref=bb.at[chip], send_sem=b_send, recv_sem=b_recv,
                    device_id=(grp_of(z, to_x, to_c), to_y), device_id_type=MESH,
                ).start()

            return carry

        lax.fori_loop(0, PLANE, pass_on, 0)

    dz = dest // (X * C)
    line = ((dest // C) % X) * Y + holder_y(dz, dest % C)
    place = (dz // 2) * SLOT + rank
    sub = lax.broadcasted_iota(jnp.int32, (CHIPS, OWN), 0)
    pltpu.make_async_copy(bb, bb, b_recv).wait()
    table = bb[...].reshape(CHIPS, 128)
    value = jnp.zeros((CHIPS, OWN), jnp.float32)
    for k in range(LINES * SLOT):
        value = jnp.where(place == k, table[:, k : k + 1], value)
    answer = jnp.sum(jnp.where(sub == line, value, 0.0), axis=0, keepdims=True)
    out_ref[...] = answer.reshape(OWN)

    @pl.when(carrier)
    def _():
        pltpu.make_async_copy(moving.at[0], moving.at[0], move_send).wait()
        pltpu.make_async_copy(outgoing, outgoing, send_sem).wait()

    @pl.when(keeper)
    def _():
        pltpu.make_async_copy(own, own, hand_send).wait()
        others = bs.at[pl.ds(0, PLANE - 1)]
        pltpu.make_async_copy(others, others, b_send).wait()

    @pl.when(holder)
    def _():
        left = ra.at[pl.ds(0, Z - 1)]
        pltpu.make_async_copy(left, left, a_send).wait()


def shards(emb, dest):
    dma = pltpu.SemaphoreType.DMA
    return pl.pallas_call(
        body_kernel,
        out_shape=jax.ShapeDtypeStruct((OWN,), jnp.float32),
        in_specs=[pl.BlockSpec(memory_space=pl.ANY)] * 2,
        out_specs=pl.BlockSpec(memory_space=pltpu.VMEM),
        scratch_shapes=[
            pltpu.VMEM((OWN, D), jnp.bfloat16),
            pltpu.VMEM((OWN,), jnp.int32),
            pltpu.VMEM((OWN, D), jnp.bfloat16),
            pltpu.VMEM((2 * SPAN * SUB, 128), jnp.float32),
            pltpu.VMEM((Z, HERE, SLOT, SUB, 128), jnp.bfloat16),
            pltpu.VMEM((Z, HERE, C, SLOT, SUB, 128), jnp.bfloat16),
            pltpu.VMEM((2, (HOPS - 1) ** 2, HERE, C, SLOT, SUB, 128), jnp.bfloat16),
            pltpu.VMEM((Z, CHIPS, C, SLOT, SUB, 128), jnp.bfloat16),
            pltpu.VMEM((CHUNK * SUB, 128), jnp.float32),
            pltpu.VMEM((CHUNK, D), jnp.bfloat16),
            pltpu.VMEM((ROWS, D), jnp.bfloat16),
            pltpu.VMEM((1, ROWS), jnp.float32),
            pltpu.VMEM((1, ROWS), jnp.float32),
            pltpu.VMEM((Z, 1, 128), jnp.float32),
            pltpu.VMEM((LINES, 1, 128), jnp.float32),
            pltpu.VMEM((PLANE, 1, 128), jnp.float32),
            pltpu.VMEM((CHIPS, 1, 128), jnp.float32),
            pltpu.SemaphoreType.DMA((2,)),
            pltpu.SemaphoreType.REGULAR((ROUNDS,)),
            dma,
            pltpu.SemaphoreType.DMA((STEPS,)),
            dma,
            pltpu.SemaphoreType.DMA((STEPS,)),
            dma,
            pltpu.SemaphoreType.DMA((2, (HOPS - 1) ** 2)),
            dma,
            dma,
            dma,
            dma,
        ],
        compiler_params=pltpu.CompilerParams(
            collective_id=0, has_side_effects=True, vmem_limit_bytes=60 << 20
        ),
        name="dedup",
    )(emb, dest)


def solution(mesh):
    in_specs = (P(("grp", "tile"), None), P(("grp", "tile")))
    out_specs = P(("grp", "tile"))
    return jax.shard_map(shards, mesh=mesh, in_specs=in_specs, out_specs=out_specs, check_vma=False)
```

```python
import jax
import jax.numpy as jnp
from jax import lax
from jax.experimental import pallas as pl
from jax.experimental.pallas import tpu as pltpu
from jax.sharding import PartitionSpec as P

MESH = pl.DeviceIdType.MESH
Z, X, C, Y = 16, 4, 2, 4
CHIPS = X * Y
PLANE = CHIPS * C
SLOT = 3
OWN = 256
D = 1024
SUB = D // 128
STEPS = Z // 2
HERE = X * C
SPAN = HERE * SLOT
HALF = PLANE * SLOT
CHUNK = 2 * HALF
ROWS = STEPS * CHUNK
LINES = Z // Y
NEAR = Z // 4
ORDER = (2, 3, 4, 8, 7, 6, 5, 1)
DEAD = 2.0
LOW = -8.0


def grp_of(z, x, c):
    return (z * X + x) * C + c


def holder_y(z, c):
    return (z + 2 * c) % Y


def chosen_of(table, i):
    value = table[0]
    for k in range(1, len(table)):
        value = jnp.where(i == k, table[k], value)
    return value


def body_kernel(
    emb_ref, dest_ref, out_ref,
    emb_v, dest_v, unit, spread, own, outgoing, arrived, spread_in, new_v, rows, pen_v, best_v,
    ra, ba, bs, bb,
    in_sem, near_sem, far_sem, hand_send, hand_recv, send_sem, recv_sem,
    a_send, a_recv, b_send, b_recv,
):
    g = lax.axis_index("grp")
    y = lax.axis_index("tile")
    z = g // (X * C)
    x = (g // C) % X
    c = g % C
    chip = x * Y + y
    me = chip * C + c
    holder = y == holder_y(z, c)

    load = pltpu.make_async_copy(emb_ref, emb_v, in_sem.at[0])
    load.start()
    load_dest = pltpu.make_async_copy(dest_ref, dest_v, in_sem.at[1])
    load_dest.start()

    def up(d):
        return (z + d) % Z

    def down(d):
        return (z + Z - d) % Z

    barrier = pltpu.get_barrier_semaphore()
    mate = (grp_of(z, x, 1 - c), y)

    def fellow(i):
        return (x + 2 + i // (C * Y)) % X, (y + 2 + (i // C) % Y) % Y, (c + i) % C

    def greet_line(sem_of):
        def step(d, carry):
            for to in (up(d), down(d)):
                pl.semaphore_signal(
                    sem_of(d), inc=1, device_id=(grp_of(to, x, c), y), device_id_type=MESH
                )
            return carry

        lax.fori_loop(1, NEAR + 1, step, 0)

    def greet_plane(i, carry):
        to_x, to_y, to_c = fellow(i)

        @pl.when((to_x != x) | (to_y != y) | (to_c != c))
        def _():
            pl.semaphore_signal(
                barrier, inc=1, device_id=(grp_of(z, to_x, to_c), to_y), device_id_type=MESH
            )

        return carry

    greet_line(lambda d: barrier)
    lax.fori_loop(0, PLANE, greet_plane, 0)

    load_dest.wait()
    dest = dest_v[...].reshape(1, OWN)
    sub = lax.broadcasted_iota(jnp.int32, (OWN, OWN), 0)
    lane = lax.broadcasted_iota(jnp.int32, (OWN, OWN), 1)
    dest_down = jnp.sum(jnp.where(sub == lane, dest, 0), axis=1, keepdims=True)
    rank = jnp.sum(jnp.where((dest_down == dest) & (sub < lane), 1, 0), axis=0, keepdims=True)
    position = dest * SLOT + rank

    load.wait()

    def normalise(i, carry):
        part = pl.ds(pl.multiple_of(i * 32, 32), 32)
        wide = emb_v[part, :].astype(jnp.float32)
        norm = jnp.sqrt(jnp.sum(wide * wide, axis=1, keepdims=True)) + 1e-6
        unit[part, :] = (wide / norm).astype(jnp.bfloat16)
        return carry

    lax.fori_loop(0, OWN // 32, normalise, 0)

    def pack(e):
        first, second = up(e + 1), jnp.where(e == STEPS - 1, z, down(e + 1))
        r = lax.broadcasted_iota(jnp.int32, (2 * SPAN, 1), 0)
        ids = r + jnp.where(r < SPAN, first * SPAN, second * SPAN - SPAN)
        pick = ids == position
        chosen = jnp.dot(
            jnp.where(pick, 1.0, 0.0).astype(jnp.bfloat16), unit[...],
            preferred_element_type=jnp.float32,
        )
        live = jnp.sum(jnp.where(pick, 1.0, 0.0), axis=1, keepdims=True)
        head = lax.broadcasted_iota(jnp.int32, (2 * SPAN, 128), 1) == 0
        for k in range(SUB):
            part = chosen[:, 128 * k : 128 * (k + 1)]
            if k == 0:
                part = jnp.where(head & (live < 0.5), DEAD, part)
            spread[pl.ds(k, 2 * SPAN, stride=SUB), :] = part
        own[pl.ds(2 * e, 2)] = (
            spread[...].reshape(2, HERE, SLOT, SUB, 128).astype(jnp.bfloat16)
        )

    mid = HERE // 2

    def lay_out(i, carry):
        e = chosen_of(ORDER, i) - 1
        pack(e)

        @pl.when(i == 0)
        def _():
            pl.semaphore_wait(barrier, 2 * NEAR + PLANE - 1)
            greet_line(lambda d: near_sem.at[d - 1])

        def keep(src, dst):
            pltpu.make_async_copy(src, dst, hand_recv.at[e]).start()

        def give(src, dst):
            pltpu.make_async_remote_copy(
                src_ref=src, dst_ref=dst, send_sem=hand_send, recv_sem=hand_recv.at[e],
                device_id=mate, device_id_type=MESH,
            ).start()

        @pl.when(e < STEPS - 1)
        def _():
            keep(own.at[2 * e + c], outgoing.at[e, :, c])
            give(own.at[2 * e + 1 - c], outgoing.at[e, :, c])

        @pl.when(e == STEPS - 1)
        def _():
            for s in range(2):
                spot = outgoing.at[e, pl.ds(s * mid, mid), c]
                keep(own.at[2 * e + s, pl.ds(c * mid, mid)], spot)
                give(own.at[2 * e + s, pl.ds((1 - c) * mid, mid)], spot)

        return carry

    lax.fori_loop(0, STEPS, lay_out, 0)

    def post(src, to_z, in_plane, half, e):
        pltpu.make_async_remote_copy(
            src_ref=src, dst_ref=arrived.at[half, chip], send_sem=send_sem, recv_sem=recv_sem.at[e],
            device_id=(to_z * (X * C) + in_plane, holder_y(to_z, in_plane % C)),
            device_id_type=MESH,
        ).start()

    itself = holder & ((x * C + c) // mid == c)

    def send(i, carry):
        e = chosen_of(ORDER, i) - 1
        pltpu.make_async_copy(outgoing.at[e], outgoing.at[e], hand_recv.at[e]).wait()

        @pl.when(i < NEAR - 1)
        def _():
            pl.semaphore_wait(near_sem.at[e], 2)

        @pl.when(i == NEAR - 2)
        def _():
            pl.semaphore_wait(near_sem.at[0], 2)
            for to in (up(NEAR), down(NEAR)):
                pl.semaphore_signal(
                    far_sem, inc=1, device_id=(grp_of(to, x, c), y), device_id_type=MESH
                )

        @pl.when(i == NEAR - 1)
        def _():
            pl.semaphore_wait(far_sem, 2)

        @pl.when(e < STEPS - 1)
        def _():
            def one(j, carry):
                in_plane = (x * C + y + j) % HERE
                post(
                    outgoing.at[e, in_plane], jnp.where(c == 0, up(e + 1), down(e + 1)),
                    in_plane, 2 * e + c, e,
                )
                return carry

            lax.fori_loop(0, HERE, one, 0)

        @pl.when(e == STEPS - 1)
        def _():
            def one(j, carry):
                q = (x + y + j) % mid
                in_plane = c * mid + q
                post(outgoing.at[e, q], up(e + 1), in_plane, 2 * e, e)
                mine = holder & (in_plane == x * C + c)
                src = outgoing.at[e, mid + q]

                @pl.when(mine)
                def _():
                    pltpu.make_async_copy(src, arrived.at[2 * e + 1, chip], recv_sem.at[e]).start()

                @pl.when(jnp.logical_not(mine))
                def _():
                    post(src, z, in_plane, 2 * e + 1, e)

                return carry

            lax.fori_loop(0, mid, one, 0)

        return carry

    lax.fori_loop(0, STEPS, send, 0)

    def take(e):
        block = arrived.at[pl.ds(2 * e, 2)]
        pltpu.make_async_copy(block, block, recv_sem.at[e]).wait()
        spread_in[...] = block[...].astype(jnp.float32).reshape(CHUNK * SUB, 128)
        for k in range(SUB):
            new_v[:, 128 * k : 128 * (k + 1)] = spread_in[
                pl.ds(k, CHUNK, stride=SUB), :
            ].astype(jnp.bfloat16)
        new = new_v[...]
        dead = spread_in[pl.ds(0, CHUNK, stride=SUB), :][:, 0:1] > 1.5
        minus = jnp.where(dead, LOW, 0.0)
        sub = lax.broadcasted_iota(jnp.int32, (CHUNK, CHUNK), 0)
        lane = lax.broadcasted_iota(jnp.int32, (CHUNK, CHUNK), 1)
        same = sub == lane

        def scores(others):
            return lax.dot_general(
                new, others, (((1,), (1,)), ((), ())), preferred_element_type=jnp.float32
            )

        old = scores(rows[...])
        within = jnp.where(same, LOW, scores(new) + minus)
        best = jnp.maximum(best_v[...], jnp.max(old + minus, axis=0, keepdims=True))
        top = jnp.max(old + pen_v[...], axis=1, keepdims=True)
        mine = jnp.maximum(
            jnp.max(within, axis=0, keepdims=True),
            jnp.max(jnp.where(same, top, LOW), axis=0, keepdims=True),
        )
        across = jnp.sum(jnp.where(same, minus, 0.0), axis=0, keepdims=True)
        at = lax.broadcasted_iota(jnp.int32, (1, ROWS), 1)
        inside = (at >= e * CHUNK) & (at < (e + 1) * CHUNK)
        best_v[...] = jnp.where(inside, jnp.concatenate([mine] * STEPS, axis=1), best)
        pen_v[...] = jnp.where(inside, jnp.concatenate([across] * STEPS, axis=1), pen_v[...])
        rows[pl.ds(pl.multiple_of(e * CHUNK, CHUNK), CHUNK), :] = new

    @pl.when(holder)
    def _():
        rows[...] = jnp.zeros((ROWS, D), jnp.bfloat16)
        pen_v[...] = jnp.full((1, ROWS), LOW, jnp.float32)
        best_v[...] = jnp.full((1, ROWS), -1.0, jnp.float32)

        def compare(i, carry):
            take(chosen_of(ORDER, i) - 1)
            return carry

        lax.fori_loop(0, STEPS, compare, 0)
        best = jnp.maximum(best_v[...], -1.0)
        fill = jnp.zeros((1, 128 - HALF), jnp.float32)
        for i in range(Z):
            ra[i] = jnp.concatenate([best[:, i * HALF : (i + 1) * HALF], fill], axis=1)

        def answer(i, carry):
            e, s = STEPS - 1 - i // 2, i % 2
            to_z = jnp.where(s == 0, down(e + 1), jnp.where(e == STEPS - 1, z, up(e + 1)))
            src, dst = ra.at[e * 2 + s], ba.at[z // Y]

            @pl.when(to_z == z)
            def _():
                pltpu.make_async_copy(src, dst, a_recv).start()

            @pl.when(to_z != z)
            def _():
                pltpu.make_async_remote_copy(
                    src_ref=src, dst_ref=dst, send_sem=a_send, recv_sem=a_recv,
                    device_id=(grp_of(to_z, x, c), y), device_id_type=MESH,
                ).start()

            return carry

        lax.fori_loop(0, Z, answer, 0)

    pltpu.make_async_copy(ba, ba, a_recv).wait()
    sub = lax.broadcasted_iota(jnp.int32, (PLANE, 128), 0)
    lane = lax.broadcasted_iota(jnp.int32, (PLANE, 128), 1)
    turned = jnp.zeros((PLANE, 128), jnp.float32)
    for j in range(SLOT):
        its = lane == sub * SLOT + j
        for h in range(LINES):
            column = jnp.sum(jnp.where(its, ba[h], 0.0), axis=1, keepdims=True)
            turned = jnp.where(lane == h * SLOT + j, column, turned)
    bs[...] = turned.reshape(PLANE, 1, 128)

    def pass_on(i, carry):
        to_x, to_y, to_c = fellow(i)
        to = (to_x * Y + to_y) * C + to_c

        @pl.when(to == me)
        def _():
            pltpu.make_async_copy(bs.at[me], bb.at[me], b_recv).start()

        @pl.when(to != me)
        def _():
            pltpu.make_async_remote_copy(
                src_ref=bs.at[to], dst_ref=bb.at[me], send_sem=b_send, recv_sem=b_recv,
                device_id=(grp_of(z, to_x, to_c), to_y), device_id_type=MESH,
            ).start()

        return carry

    lax.fori_loop(0, PLANE, pass_on, 0)

    dz = dest // (X * C)
    line = (((dest // C) % X) * Y + holder_y(dz, dest % C)) * C + dest % C
    place = (dz // Y) * SLOT + rank
    sub = lax.broadcasted_iota(jnp.int32, (PLANE, OWN), 0)
    pltpu.make_async_copy(bb, bb, b_recv).wait()
    table = bb[...].reshape(PLANE, 128)
    value = jnp.zeros((PLANE, OWN), jnp.float32)
    for k in range(LINES * SLOT):
        value = jnp.where(place == k, table[:, k : k + 1], value)
    answer = jnp.sum(jnp.where(sub == line, value, 0.0), axis=0, keepdims=True)
    out_ref[...] = answer.reshape(OWN)

    given = own.at[pl.ds(0, STEPS)]
    pltpu.make_async_copy(given, given, hand_send).wait()
    others = bs.at[pl.ds(0, PLANE - 1)]
    pltpu.make_async_copy(others, others, b_send).wait()
    sent = outgoing.at[pl.ds(0, STEPS - 1)]
    pltpu.make_async_copy(sent, sent, send_sem).wait()
    sent = outgoing.at[STEPS - 1, pl.ds(0, HERE - 1)]
    pltpu.make_async_copy(sent, sent, send_sem).wait()

    @pl.when(jnp.logical_not(itself))
    def _():
        last = outgoing.at[STEPS - 1, HERE - 1]
        pltpu.make_async_copy(last, last, send_sem).wait()

    @pl.when(holder)
    def _():
        left = ra.at[pl.ds(0, Z - 1)]
        pltpu.make_async_copy(left, left, a_send).wait()


def shards(emb, dest):
    dma = pltpu.SemaphoreType.DMA
    return pl.pallas_call(
        body_kernel,
        out_shape=jax.ShapeDtypeStruct((OWN,), jnp.float32),
        in_specs=[pl.BlockSpec(memory_space=pl.ANY)] * 2,
        out_specs=pl.BlockSpec(memory_space=pltpu.VMEM),
        scratch_shapes=[
            pltpu.VMEM((OWN, D), jnp.bfloat16),
            pltpu.VMEM((OWN,), jnp.int32),
            pltpu.VMEM((OWN, D), jnp.bfloat16),
            pltpu.VMEM((2 * SPAN * SUB, 128), jnp.float32),
            pltpu.VMEM((Z, HERE, SLOT, SUB, 128), jnp.bfloat16),
            pltpu.VMEM((STEPS, HERE, C, SLOT, SUB, 128), jnp.bfloat16),
            pltpu.VMEM((Z, CHIPS, C, SLOT, SUB, 128), jnp.bfloat16),
            pltpu.VMEM((CHUNK * SUB, 128), jnp.float32),
            pltpu.VMEM((CHUNK, D), jnp.bfloat16),
            pltpu.VMEM((ROWS, D), jnp.bfloat16),
            pltpu.VMEM((1, ROWS), jnp.float32),
            pltpu.VMEM((1, ROWS), jnp.float32),
            pltpu.VMEM((Z, 1, 128), jnp.float32),
            pltpu.VMEM((LINES, 1, 128), jnp.float32),
            pltpu.VMEM((PLANE, 1, 128), jnp.float32),
            pltpu.VMEM((PLANE, 1, 128), jnp.float32),
            pltpu.SemaphoreType.DMA((2,)),
            pltpu.SemaphoreType.REGULAR((NEAR,)),
            pltpu.SemaphoreType.REGULAR,
            dma,
            pltpu.SemaphoreType.DMA((STEPS,)),
            dma,
            pltpu.SemaphoreType.DMA((STEPS,)),
            dma,
            dma,
            dma,
            dma,
        ],
        compiler_params=pltpu.CompilerParams(
            collective_id=0, has_side_effects=True, vmem_limit_bytes=60 << 20
        ),
        name="dedup",
    )(emb, dest)


def solution(mesh):
    in_specs = (P(("grp", "tile"), None), P(("grp", "tile")))
    out_specs = P(("grp", "tile"))
    return jax.shard_map(shards, mesh=mesh, in_specs=in_specs, out_specs=out_specs, check_vma=False)
```

```python
import jax
import jax.numpy as jnp
from jax import lax
from jax.experimental import pallas as pl
from jax.experimental.pallas import tpu as pltpu
from jax.sharding import PartitionSpec as P

MESH = pl.DeviceIdType.MESH
Z, X, C, Y = 16, 4, 2, 4
PLANE = X * C * Y
NEAR = Z // 4
FAR = Z // 4
SLOT = 3
OWN = 256
D = 1024
SUB = D // 128
STEPS = Z // 2
SPAN = X * C * SLOT
CHUNK = 2 * PLANE * SLOT
ROWS = STEPS * CHUNK
GROUPS = Z * X * C
LINES = Z // Y
DEAD = 2.0
LOW = -8.0


def grp_of(z, x, c):
    return (z * X + x) * C + c


def holder_y(z, c):
    return (z + 2 * c) % Y


def body_kernel(
    emb_ref, dest_ref, out_ref,
    emb_v, dest_v, unit, spread, outgoing, relay, arrived, spread_in, new_v, rows, pen_v, best_v, ra, ba, bs, bb,
    in_sem, near_sem, far_sem, send_sem, recv_sem, relay_send, relay_recv, on_send, a_send, a_recv, b_send, b_recv,
):
    g = lax.axis_index("grp")
    y = lax.axis_index("tile")
    z = g // (X * C)
    x = (g // C) % X
    c = g % C
    me = (x * C + c) * Y + y
    holder = y == holder_y(z, c)

    load = pltpu.make_async_copy(emb_ref, emb_v, in_sem.at[0])
    load.start()
    load_dest = pltpu.make_async_copy(dest_ref, dest_v, in_sem.at[1])
    load_dest.start()

    barrier = pltpu.get_barrier_semaphore()

    def greet_line(sem_of):
        def step(d, carry):
            for to in ((z + d) % Z, (z + Z - d) % Z):
                pl.semaphore_signal(
                    sem_of(d), inc=1, device_id=(grp_of(to, x, c), y), device_id_type=MESH
                )
            return carry

        lax.fori_loop(1, NEAR + 1, step, 0)

    greet_line(lambda d: barrier)

    def mate(i):
        return (x + 2 + i // (C * Y)) % X, (y + 2 + (i // C) % Y) % Y, (c + i) % C

    def greet_plane(i, carry):
        to_x, to_y, to_c = mate(i)

        @pl.when((to_x != x) | (to_y != y) | (to_c != c))
        def _():
            pl.semaphore_signal(
                barrier, inc=1, device_id=(grp_of(z, to_x, to_c), to_y), device_id_type=MESH
            )

        return carry

    lax.fori_loop(0, PLANE, greet_plane, 0)

    load_dest.wait()
    dest = dest_v[...].reshape(1, OWN)
    sub = lax.broadcasted_iota(jnp.int32, (OWN, OWN), 0)
    lane = lax.broadcasted_iota(jnp.int32, (OWN, OWN), 1)
    dest_down = jnp.sum(jnp.where(sub == lane, dest, 0), axis=1, keepdims=True)
    rank = jnp.sum(jnp.where((dest_down == dest) & (sub < lane), 1, 0), axis=0, keepdims=True)
    position = dest * SLOT + rank

    load.wait()

    def normalise(i, carry):
        part = pl.ds(pl.multiple_of(i * 32, 32), 32)
        wide = emb_v[part, :].astype(jnp.float32)
        norm = jnp.sqrt(jnp.sum(wide * wide, axis=1, keepdims=True)) + 1e-6
        unit[part, :] = (wide / norm).astype(jnp.bfloat16)
        return carry

    lax.fori_loop(0, OWN // 32, normalise, 0)

    pl.semaphore_wait(barrier, 2 * NEAR + PLANE - 1)
    greet_line(lambda d: near_sem.at[d - 1])

    def up(d):
        return (z + d) % Z

    def down(d):
        return (z + Z - d) % Z

    def pack(e):
        first, second = up(e + 1), jnp.where(e == STEPS - 1, z, down(e + 1))
        r = lax.broadcasted_iota(jnp.int32, (2 * SPAN, 1), 0)
        ids = r + jnp.where(r < SPAN, first * SPAN, second * SPAN - SPAN)
        pick = ids == position
        chosen = jnp.dot(
            jnp.where(pick, 1.0, 0.0).astype(jnp.bfloat16), unit[...],
            preferred_element_type=jnp.float32,
        )
        live = jnp.sum(jnp.where(pick, 1.0, 0.0), axis=1, keepdims=True)
        head = lax.broadcasted_iota(jnp.int32, (2 * SPAN, 128), 1) == 0
        for k in range(SUB):
            part = chosen[:, 128 * k : 128 * (k + 1)]
            if k == 0:
                part = jnp.where(head & (live < 0.5), DEAD, part)
            spread[pl.ds(k, 2 * SPAN, stride=SUB), :] = part
        outgoing[pl.ds(e * 2 * SPAN, 2 * SPAN)] = (
            spread[...].reshape(2 * SPAN, SUB, 128).astype(jnp.bfloat16)
        )

    def post(src, to_z, in_plane, half, e, sem):
        dst = arrived.at[pl.ds((half * PLANE + me) * SLOT, SLOT)]
        to_y = holder_y(to_z, in_plane % C)
        pltpu.make_async_remote_copy(
            src_ref=src, dst_ref=dst, send_sem=sem, recv_sem=recv_sem.at[e],
            device_id=(to_z * (X * C) + in_plane, to_y), device_id_type=MESH,
        ).start()

    def from_outgoing(half, in_plane):
        return outgoing.at[pl.ds(half * SPAN + in_plane * SLOT, SLOT)]

    def send(e):
        def one(i, carry):
            s = i % 2
            in_plane = (x * C + c + i // 2) % (X * C)
            half = e * 2 + s
            post(
                from_outgoing(half, in_plane), jnp.where(s == 0, up(e + 1), down(e + 1)),
                in_plane, half, e, send_sem,
            )
            return carry

        lax.fori_loop(0, 2 * X * C, one, 0)

    def send_here():
        half, e = 2 * STEPS - 1, STEPS - 1

        def one(i, carry):
            in_plane = (x * C + c + i) % (X * C)
            mine = (in_plane == x * C + c) & holder
            src = from_outgoing(half, in_plane)

            @pl.when(mine)
            def _():
                dst = arrived.at[pl.ds((half * PLANE + me) * SLOT, SLOT)]
                pltpu.make_async_copy(src, dst, recv_sem.at[e]).start()

            @pl.when(jnp.logical_not(mine))
            def _():
                post(src, z, in_plane, half, e, send_sem)

            return carry

        lax.fori_loop(0, X * C, one, 0)

    def send_relay(k):
        e = STEPS - 1 - k

        def hop(to_z, src, dst):
            pltpu.make_async_remote_copy(
                src_ref=src, dst_ref=dst, send_sem=relay_send, recv_sem=relay_recv.at[k],
                device_id=(grp_of(to_z, x, c), y), device_id_type=MESH,
            ).start()

        @pl.when(k == 0)
        def _():
            lower = outgoing.at[pl.ds(2 * e * SPAN, SPAN // 2)]
            upper = outgoing.at[pl.ds(2 * e * SPAN + SPAN // 2, SPAN // 2)]
            hop(up(1), lower, relay.at[0, pl.ds(0, SPAN // 2)])
            hop(down(1), upper, relay.at[1, pl.ds(SPAN // 2, SPAN // 2)])

        @pl.when(k > 0)
        def _():
            hop(up(1), outgoing.at[pl.ds(2 * e * SPAN, SPAN)], relay.at[2 * k])
            hop(down(1), outgoing.at[pl.ds((2 * e + 1) * SPAN, SPAN)], relay.at[2 * k + 1])

    def pass_relay(k, carry):
        e = STEPS - 1 - k

        @pl.when(k == 0)
        def _():
            pltpu.make_async_copy(relay.at[0], relay.at[0], relay_recv.at[0]).wait()

        @pl.when(k > 0)
        def _():
            both = relay.at[pl.ds(2 * k, 2)]
            pltpu.make_async_copy(both, both, relay_recv.at[k]).wait()

        def one(i, carry):
            s = i % 2
            in_plane = (x * C + c + i // 2) % (X * C)
            half = 2 * e + jnp.where(k == 0, 0, s)

            @pl.when((k > 0) | (in_plane // (X * C // 2) == s))
            def _():
                post(
                    relay.at[2 * k + s, pl.ds(in_plane * SLOT, SLOT)],
                    jnp.where(s == 0, up(e), down(e)), in_plane, half, e, on_send,
                )

            return carry

        lax.fori_loop(0, 2 * X * C, one, 0)
        return carry

    def step_out(i, carry):
        e = jnp.where(i < FAR, STEPS - 1 - i, jnp.where(i == STEPS - 1, 0, i - FAR + 1))
        pack(e)

        @pl.when(i < FAR)
        def _():
            send_relay(i)

        @pl.when((i >= FAR) & (i < STEPS - 1))
        def _():
            pl.semaphore_wait(near_sem.at[e], 2)

        @pl.when(i == STEPS - 2)
        def _():
            pl.semaphore_wait(near_sem.at[0], 2)
            for to in (up(NEAR), down(NEAR)):
                pl.semaphore_signal(
                    far_sem, inc=1, device_id=(grp_of(to, x, c), y), device_id_type=MESH
                )

        @pl.when(i == STEPS - 1)
        def _():
            pl.semaphore_wait(far_sem, 2)
            lax.fori_loop(0, FAR, pass_relay, 0)

        @pl.when(i >= FAR)
        def _():
            send(e)

        @pl.when(i == FAR)
        def _():
            send_here()

        return carry

    lax.fori_loop(0, STEPS, step_out, 0)

    def take(e):
        here = pl.ds(pl.multiple_of(e * CHUNK, CHUNK), CHUNK)
        block = arrived.at[here]
        pltpu.make_async_copy(block, block, recv_sem.at[e]).wait()
        spread_in[...] = block[...].astype(jnp.float32).reshape(CHUNK * SUB, 128)
        for k in range(SUB):
            new_v[:, 128 * k : 128 * (k + 1)] = spread_in[
                pl.ds(k, CHUNK, stride=SUB), :
            ].astype(jnp.bfloat16)
        new = new_v[...]
        dead = spread_in[pl.ds(0, CHUNK, stride=SUB), :][:, 0:1] > 1.5
        minus = jnp.where(dead, LOW, 0.0)
        sub = lax.broadcasted_iota(jnp.int32, (CHUNK, CHUNK), 0)
        lane = lax.broadcasted_iota(jnp.int32, (CHUNK, CHUNK), 1)
        same = sub == lane

        def scores(others):
            return lax.dot_general(
                new, others, (((1,), (1,)), ((), ())), preferred_element_type=jnp.float32
            )

        old = scores(rows[...])
        own = jnp.where(same, LOW, scores(new) + minus)
        best = jnp.maximum(best_v[...], jnp.max(old + minus, axis=0, keepdims=True))
        top = jnp.max(old + pen_v[...], axis=1, keepdims=True)
        mine = jnp.maximum(
            jnp.max(own, axis=0, keepdims=True),
            jnp.max(jnp.where(same, top, LOW), axis=0, keepdims=True),
        )
        across = jnp.sum(jnp.where(same, minus, 0.0), axis=0, keepdims=True)
        at = lax.broadcasted_iota(jnp.int32, (1, ROWS), 1)
        inside = (at >= e * CHUNK) & (at < (e + 1) * CHUNK)
        best_v[...] = jnp.where(inside, jnp.concatenate([mine] * STEPS, axis=1), best)
        pen_v[...] = jnp.where(inside, jnp.concatenate([across] * STEPS, axis=1), pen_v[...])
        rows[here, :] = new

    @pl.when(holder)
    def _():
        rows[...] = jnp.zeros((ROWS, D), jnp.bfloat16)
        pen_v[...] = jnp.full((1, ROWS), LOW, jnp.float32)
        best_v[...] = jnp.full((1, ROWS), -1.0, jnp.float32)

        def compare(i, carry):
            take(jnp.where(i < FAR - 1, i + 1, jnp.where(i == STEPS - 1, 0, STEPS + FAR - 2 - i)))
            return carry

        lax.fori_loop(0, STEPS, compare, 0)
        best = jnp.maximum(best_v[...], -1.0)
        width = PLANE * SLOT
        fill = jnp.zeros((1, 128 - width), jnp.float32)
        for i in range(Z):
            ra[i] = jnp.concatenate([best[:, i * width : (i + 1) * width], fill], axis=1)

        def answer(i, carry):
            e, s = STEPS - 1 - i // 2, i % 2
            to_z = jnp.where(s == 0, down(e + 1), jnp.where(e == STEPS - 1, z, up(e + 1)))
            src, dst = ra.at[e * 2 + s], ba.at[z // Y]

            @pl.when(to_z == z)
            def _():
                pltpu.make_async_copy(src, dst, a_recv).start()

            @pl.when(to_z != z)
            def _():
                pltpu.make_async_remote_copy(
                    src_ref=src, dst_ref=dst, send_sem=a_send, recv_sem=a_recv,
                    device_id=(grp_of(to_z, x, c), y), device_id_type=MESH,
                ).start()

            return carry

        lax.fori_loop(0, Z, answer, 0)

    pltpu.make_async_copy(ba, ba, a_recv).wait()
    sub = lax.broadcasted_iota(jnp.int32, (PLANE, 128), 0)
    lane = lax.broadcasted_iota(jnp.int32, (PLANE, 128), 1)
    turned = jnp.zeros((PLANE, 128), jnp.float32)
    for j in range(SLOT):
        its = lane == sub * SLOT + j
        for h in range(LINES):
            column = jnp.sum(jnp.where(its, ba[h], 0.0), axis=1, keepdims=True)
            turned = jnp.where(lane == h * SLOT + j, column, turned)
    bs[...] = turned.reshape(PLANE, 1, 128)

    def pass_on(i, carry):
        to_x, to_y, to_c = mate(i)
        to = (to_x * C + to_c) * Y + to_y

        @pl.when(to == me)
        def _():
            pltpu.make_async_copy(bs.at[me], bb.at[me], b_recv).start()

        @pl.when(to != me)
        def _():
            pltpu.make_async_remote_copy(
                src_ref=bs.at[to], dst_ref=bb.at[me], send_sem=b_send, recv_sem=b_recv,
                device_id=(grp_of(z, to_x, to_c), to_y), device_id_type=MESH,
            ).start()

        return carry

    lax.fori_loop(0, PLANE, pass_on, 0)

    dz = dest // (X * C)
    dx = (dest // C) % X
    dc = dest % C
    line = (dx * C + dc) * Y + holder_y(dz, dc)
    spot = (dz // Y) * SLOT + rank
    sub = lax.broadcasted_iota(jnp.int32, (PLANE, OWN), 0)
    pltpu.make_async_copy(bb, bb, b_recv).wait()
    table = bb[...].reshape(PLANE, 128)
    value = jnp.zeros((PLANE, OWN), jnp.float32)
    for k in range(LINES * SLOT):
        value = jnp.where(spot == k, table[:, k : k + 1], value)
    answer = jnp.sum(jnp.where(sub == line, value, 0.0), axis=0, keepdims=True)
    out_ref[...] = answer.reshape(OWN)

    others = bs.at[pl.ds(0, PLANE - 1)]
    pltpu.make_async_copy(others, others, b_send).wait()

    straight = 2 * FAR * SPAN + SPAN
    by_relay = 2 * FAR * SPAN - SPAN

    def all_left(count, sem):
        gone = outgoing.at[pl.ds(0, count)]
        pltpu.make_async_copy(gone, gone, sem).wait()

    all_left(by_relay, relay_send)
    all_left(by_relay, on_send)

    @pl.when(holder)
    def _():
        left = ra.at[pl.ds(0, Z - 1)]
        pltpu.make_async_copy(left, left, a_send).wait()
        all_left(straight - SLOT, send_sem)

    @pl.when(jnp.logical_not(holder))
    def _():
        all_left(straight, send_sem)


def shards(emb, dest):
    dma = pltpu.SemaphoreType.DMA
    regular = pltpu.SemaphoreType.REGULAR
    return pl.pallas_call(
        body_kernel,
        out_shape=jax.ShapeDtypeStruct((OWN,), jnp.float32),
        in_specs=[pl.BlockSpec(memory_space=pl.ANY)] * 2,
        out_specs=pl.BlockSpec(memory_space=pltpu.VMEM),
        scratch_shapes=[
            pltpu.VMEM((OWN, D), jnp.bfloat16),
            pltpu.VMEM((OWN,), jnp.int32),
            pltpu.VMEM((OWN, D), jnp.bfloat16),
            pltpu.VMEM((2 * SPAN * SUB, 128), jnp.float32),
            pltpu.VMEM((GROUPS * SLOT, SUB, 128), jnp.bfloat16),
            pltpu.VMEM((2 * FAR, SPAN, SUB, 128), jnp.bfloat16),
            pltpu.VMEM((ROWS, SUB, 128), jnp.bfloat16),
            pltpu.VMEM((CHUNK * SUB, 128), jnp.float32),
            pltpu.VMEM((CHUNK, D), jnp.bfloat16),
            pltpu.VMEM((ROWS, D), jnp.bfloat16),
            pltpu.VMEM((1, ROWS), jnp.float32),
            pltpu.VMEM((1, ROWS), jnp.float32),
            pltpu.VMEM((Z, 1, 128), jnp.float32),
            pltpu.VMEM((LINES, 1, 128), jnp.float32),
            pltpu.VMEM((PLANE, 1, 128), jnp.float32),
            pltpu.VMEM((PLANE, 1, 128), jnp.float32),
            pltpu.SemaphoreType.DMA((2,)),
            pltpu.SemaphoreType.REGULAR((NEAR,)),
            regular,
            dma,
            pltpu.SemaphoreType.DMA((STEPS,)),
            dma,
            pltpu.SemaphoreType.DMA((FAR,)),
            dma,
            dma,
            dma,
            dma,
            dma,
        ],
        compiler_params=pltpu.CompilerParams(
            collective_id=0, has_side_effects=True, vmem_limit_bytes=60 << 20
        ),
        name="dedup",
    )(emb, dest)


def solution(mesh):
    in_specs = (P(("grp", "tile"), None), P(("grp", "tile")))
    out_specs = P(("grp", "tile"))
    return jax.shard_map(shards, mesh=mesh, in_specs=in_specs, out_specs=out_specs, check_vma=False)
```

```python
import jax
import jax.numpy as jnp
from jax import lax
from jax.experimental import pallas as pl
from jax.experimental.pallas import tpu as pltpu
from jax.sharding import PartitionSpec as P

MESH = pl.DeviceIdType.MESH
Z, X, C, Y = 16, 4, 2, 4
PLANE = X * C * Y
NEAR = Z // 4
FAR = Z // 4
SLOT = 3
OWN = 256
D = 1024
SUB = D // 128
STEPS = Z // 2
SPAN = X * C * SLOT
CHUNK = 2 * PLANE * SLOT
ROWS = STEPS * CHUNK
GROUPS = Z * X * C
LINES = Z // Y
DEAD = 2.0
LOW = -8.0


def grp_of(z, x, c):
    return (z * X + x) * C + c


def holder_y(z, c):
    return (z + 2 * c) % Y


def body_kernel(
    emb_ref, dest_ref, out_ref,
    emb_v, dest_v, unit, spread, outgoing, relay, arrived, spread_in, new_v, rows, pen_v, best_v, ra, ba, bs, bb,
    in_sem, near_sem, far_sem, send_sem, recv_sem, relay_send, relay_recv, on_send, a_send, a_recv, b_send, b_recv,
):
    g = lax.axis_index("grp")
    y = lax.axis_index("tile")
    z = g // (X * C)
    x = (g // C) % X
    c = g % C
    me = (x * C + c) * Y + y
    holder = y == holder_y(z, c)

    load = pltpu.make_async_copy(emb_ref, emb_v, in_sem.at[0])
    load.start()
    load_dest = pltpu.make_async_copy(dest_ref, dest_v, in_sem.at[1])
    load_dest.start()

    barrier = pltpu.get_barrier_semaphore()

    def greet_line(sem_of):
        def step(d, carry):
            for to in ((z + d) % Z, (z + Z - d) % Z):
                pl.semaphore_signal(
                    sem_of(d), inc=1, device_id=(grp_of(to, x, c), y), device_id_type=MESH
                )
            return carry

        lax.fori_loop(1, NEAR + 1, step, 0)

    greet_line(lambda d: barrier)

    def mate(i):
        return (x + 2 + i // (C * Y)) % X, (y + 2 + (i // C) % Y) % Y, (c + i) % C

    def greet_plane(i, carry):
        to_x, to_y, to_c = mate(i)

        @pl.when((to_x != x) | (to_y != y) | (to_c != c))
        def _():
            pl.semaphore_signal(
                barrier, inc=1, device_id=(grp_of(z, to_x, to_c), to_y), device_id_type=MESH
            )

        return carry

    lax.fori_loop(0, PLANE, greet_plane, 0)

    load_dest.wait()
    dest = dest_v[...].reshape(1, OWN)
    sub = lax.broadcasted_iota(jnp.int32, (OWN, OWN), 0)
    lane = lax.broadcasted_iota(jnp.int32, (OWN, OWN), 1)
    dest_down = jnp.sum(jnp.where(sub == lane, dest, 0), axis=1, keepdims=True)
    rank = jnp.sum(jnp.where((dest_down == dest) & (sub < lane), 1, 0), axis=0, keepdims=True)
    position = dest * SLOT + rank

    load.wait()

    def normalise(i, carry):
        part = pl.ds(pl.multiple_of(i * 32, 32), 32)
        wide = emb_v[part, :].astype(jnp.float32)
        norm = jnp.sqrt(jnp.sum(wide * wide, axis=1, keepdims=True)) + 1e-6
        unit[part, :] = (wide / norm).astype(jnp.bfloat16)
        return carry

    lax.fori_loop(0, OWN // 32, normalise, 0)

    pl.semaphore_wait(barrier, 2 * NEAR + PLANE - 1)
    greet_line(lambda d: near_sem.at[d - 1])

    def up(d):
        return (z + d) % Z

    def down(d):
        return (z + Z - d) % Z

    def pack(e):
        first, second = up(e + 1), jnp.where(e == STEPS - 1, z, down(e + 1))
        r = lax.broadcasted_iota(jnp.int32, (2 * SPAN, 1), 0)
        ids = r + jnp.where(r < SPAN, first * SPAN, second * SPAN - SPAN)
        pick = ids == position
        chosen = jnp.dot(
            jnp.where(pick, 1.0, 0.0).astype(jnp.bfloat16), unit[...],
            preferred_element_type=jnp.float32,
        )
        live = jnp.sum(jnp.where(pick, 1.0, 0.0), axis=1, keepdims=True)
        head = lax.broadcasted_iota(jnp.int32, (2 * SPAN, 128), 1) == 0
        for k in range(SUB):
            part = chosen[:, 128 * k : 128 * (k + 1)]
            if k == 0:
                part = jnp.where(head & (live < 0.5), DEAD, part)
            spread[pl.ds(k, 2 * SPAN, stride=SUB), :] = part
        outgoing[pl.ds(e * 2 * SPAN, 2 * SPAN)] = (
            spread[...].reshape(2 * SPAN, SUB, 128).astype(jnp.bfloat16)
        )

    def post(src, to_z, in_plane, half, e, sem):
        dst = arrived.at[pl.ds((half * PLANE + me) * SLOT, SLOT)]
        to_y = holder_y(to_z, in_plane % C)
        pltpu.make_async_remote_copy(
            src_ref=src, dst_ref=dst, send_sem=sem, recv_sem=recv_sem.at[e],
            device_id=(to_z * (X * C) + in_plane, to_y), device_id_type=MESH,
        ).start()

    def from_outgoing(half, in_plane):
        return outgoing.at[pl.ds(half * SPAN + in_plane * SLOT, SLOT)]

    def send(e):
        def one(i, carry):
            s = i % 2
            in_plane = (x * C + c + i // 2) % (X * C)
            half = e * 2 + s
            post(
                from_outgoing(half, in_plane), jnp.where(s == 0, up(e + 1), down(e + 1)),
                in_plane, half, e, send_sem,
            )
            return carry

        lax.fori_loop(0, 2 * X * C, one, 0)

    def send_here():
        half, e = 2 * STEPS - 1, STEPS - 1

        def one(i, carry):
            in_plane = (x * C + c + i) % (X * C)
            mine = (in_plane == x * C + c) & holder
            src = from_outgoing(half, in_plane)

            @pl.when(mine)
            def _():
                dst = arrived.at[pl.ds((half * PLANE + me) * SLOT, SLOT)]
                pltpu.make_async_copy(src, dst, recv_sem.at[e]).start()

            @pl.when(jnp.logical_not(mine))
            def _():
                post(src, z, in_plane, half, e, send_sem)

            return carry

        lax.fori_loop(0, X * C, one, 0)

    def send_relay(k):
        e = STEPS - 1 - k

        def hop(to_z, src, dst):
            pltpu.make_async_remote_copy(
                src_ref=src, dst_ref=dst, send_sem=relay_send, recv_sem=relay_recv.at[k],
                device_id=(grp_of(to_z, x, c), y), device_id_type=MESH,
            ).start()

        @pl.when(k == 0)
        def _():
            lower = outgoing.at[pl.ds(2 * e * SPAN, SPAN // 2)]
            upper = outgoing.at[pl.ds(2 * e * SPAN + SPAN // 2, SPAN // 2)]
            hop(up(1), lower, relay.at[0, pl.ds(0, SPAN // 2)])
            hop(down(1), upper, relay.at[1, pl.ds(SPAN // 2, SPAN // 2)])

        @pl.when(k > 0)
        def _():
            hop(up(1), outgoing.at[pl.ds(2 * e * SPAN, SPAN)], relay.at[2 * k])
            hop(down(1), outgoing.at[pl.ds((2 * e + 1) * SPAN, SPAN)], relay.at[2 * k + 1])

    def pass_relay(k, carry):
        e = STEPS - 1 - k

        @pl.when(k == 0)
        def _():
            pltpu.make_async_copy(relay.at[0], relay.at[0], relay_recv.at[0]).wait()

        @pl.when(k > 0)
        def _():
            both = relay.at[pl.ds(2 * k, 2)]
            pltpu.make_async_copy(both, both, relay_recv.at[k]).wait()

        def one(i, carry):
            s = i % 2
            in_plane = (x * C + c + i // 2) % (X * C)
            half = 2 * e + jnp.where(k == 0, 0, s)

            @pl.when((k > 0) | (in_plane // (X * C // 2) == s))
            def _():
                post(
                    relay.at[2 * k + s, pl.ds(in_plane * SLOT, SLOT)],
                    jnp.where(s == 0, up(e), down(e)), in_plane, half, e, on_send,
                )

            return carry

        lax.fori_loop(0, 2 * X * C, one, 0)
        return carry

    def step_out(i, carry):
        e = jnp.where(i < FAR, STEPS - 1 - i, jnp.where(i == STEPS - 1, 0, i - FAR + 1))
        pack(e)

        @pl.when(i < FAR)
        def _():
            send_relay(i)

        @pl.when((i >= FAR) & (i < STEPS - 1))
        def _():
            pl.semaphore_wait(near_sem.at[e], 2)

        @pl.when(i == STEPS - 2)
        def _():
            pl.semaphore_wait(near_sem.at[0], 2)
            for to in (up(NEAR), down(NEAR)):
                pl.semaphore_signal(
                    far_sem, inc=1, device_id=(grp_of(to, x, c), y), device_id_type=MESH
                )

        @pl.when(i == STEPS - 1)
        def _():
            pl.semaphore_wait(far_sem, 2)
            lax.fori_loop(0, FAR, pass_relay, 0)

        @pl.when(i >= FAR)
        def _():
            send(e)

        @pl.when(i == FAR)
        def _():
            send_here()

        return carry

    lax.fori_loop(0, STEPS, step_out, 0)

    def take(e, n):
        count = n * CHUNK
        here = pl.ds(pl.multiple_of(e * CHUNK, CHUNK), count)
        for k in reversed(range(n)):
            block = arrived.at[pl.ds(pl.multiple_of((e + k) * CHUNK, CHUNK), CHUNK)]
            pltpu.make_async_copy(block, block, recv_sem.at[e + k]).wait()
        spread_in[0 : count * SUB, :] = (
            arrived[here].astype(jnp.float32).reshape(count * SUB, 128)
        )
        for k in range(SUB):
            new_v[0:count, 128 * k : 128 * (k + 1)] = spread_in[
                pl.ds(k, count, stride=SUB), :
            ].astype(jnp.bfloat16)
        new = new_v[0:count, :]
        dead = spread_in[pl.ds(0, count, stride=SUB), :][:, 0:1] > 1.5
        minus = jnp.where(dead, LOW, 0.0)
        sub = lax.broadcasted_iota(jnp.int32, (count, count), 0)
        lane = lax.broadcasted_iota(jnp.int32, (count, count), 1)
        same = sub == lane

        def scores(others):
            return lax.dot_general(
                new, others, (((1,), (1,)), ((), ())), preferred_element_type=jnp.float32
            )

        old = scores(rows[...])
        own = jnp.where(same, LOW, scores(new) + minus)
        best = jnp.maximum(best_v[...], jnp.max(old + minus, axis=0, keepdims=True))
        top = jnp.max(old + pen_v[...], axis=1, keepdims=True)
        mine = jnp.maximum(
            jnp.max(own, axis=0, keepdims=True),
            jnp.max(jnp.where(same, top, LOW), axis=0, keepdims=True),
        )
        across = jnp.sum(jnp.where(same, minus, 0.0), axis=0, keepdims=True)
        at = lax.broadcasted_iota(jnp.int32, (1, ROWS), 1)
        inside = (at >= e * CHUNK) & (at < e * CHUNK + count)
        best_v[...] = jnp.where(inside, jnp.concatenate([mine] * (STEPS // n), axis=1), best)
        pen_v[...] = jnp.where(
            inside, jnp.concatenate([across] * (STEPS // n), axis=1), pen_v[...]
        )
        rows[here, :] = new

    @pl.when(holder)
    def _():
        rows[...] = jnp.zeros((ROWS, D), jnp.bfloat16)
        pen_v[...] = jnp.full((1, ROWS), LOW, jnp.float32)
        best_v[...] = jnp.full((1, ROWS), -1.0, jnp.float32)

        def compare(i, carry):
            single = (i < FAR - 1) | (i == FAR + 1)

            @pl.when(single)
            def _():
                take(jnp.where(i < FAR - 1, i + 1, 0), 1)

            @pl.when(jnp.logical_not(single))
            def _():
                take(jnp.where(i == FAR - 1, STEPS - 2, STEPS - 4), 2)

            return carry

        lax.fori_loop(0, FAR + 2, compare, 0)
        best = jnp.maximum(best_v[...], -1.0)
        width = PLANE * SLOT
        fill = jnp.zeros((1, 128 - width), jnp.float32)
        for i in range(Z):
            ra[i] = jnp.concatenate([best[:, i * width : (i + 1) * width], fill], axis=1)

        def answer(i, carry):
            e, s = STEPS - 1 - i // 2, i % 2
            to_z = jnp.where(s == 0, down(e + 1), jnp.where(e == STEPS - 1, z, up(e + 1)))
            src, dst = ra.at[e * 2 + s], ba.at[z // Y]

            @pl.when(to_z == z)
            def _():
                pltpu.make_async_copy(src, dst, a_recv).start()

            @pl.when(to_z != z)
            def _():
                pltpu.make_async_remote_copy(
                    src_ref=src, dst_ref=dst, send_sem=a_send, recv_sem=a_recv,
                    device_id=(grp_of(to_z, x, c), y), device_id_type=MESH,
                ).start()

            return carry

        lax.fori_loop(0, Z, answer, 0)

    pltpu.make_async_copy(ba, ba, a_recv).wait()
    sub = lax.broadcasted_iota(jnp.int32, (PLANE, 128), 0)
    lane = lax.broadcasted_iota(jnp.int32, (PLANE, 128), 1)
    turned = jnp.zeros((PLANE, 128), jnp.float32)
    for j in range(SLOT):
        its = lane == sub * SLOT + j
        for h in range(LINES):
            column = jnp.sum(jnp.where(its, ba[h], 0.0), axis=1, keepdims=True)
            turned = jnp.where(lane == h * SLOT + j, column, turned)
    bs[...] = turned.reshape(PLANE, 1, 128)

    def pass_on(i, carry):
        to_x, to_y, to_c = mate(i)
        to = (to_x * C + to_c) * Y + to_y

        @pl.when(to == me)
        def _():
            pltpu.make_async_copy(bs.at[me], bb.at[me], b_recv).start()

        @pl.when(to != me)
        def _():
            pltpu.make_async_remote_copy(
                src_ref=bs.at[to], dst_ref=bb.at[me], send_sem=b_send, recv_sem=b_recv,
                device_id=(grp_of(z, to_x, to_c), to_y), device_id_type=MESH,
            ).start()

        return carry

    lax.fori_loop(0, PLANE, pass_on, 0)

    dz = dest // (X * C)
    dx = (dest // C) % X
    dc = dest % C
    line = (dx * C + dc) * Y + holder_y(dz, dc)
    spot = (dz // Y) * SLOT + rank
    sub = lax.broadcasted_iota(jnp.int32, (PLANE, OWN), 0)
    pltpu.make_async_copy(bb, bb, b_recv).wait()
    table = bb[...].reshape(PLANE, 128)
    value = jnp.zeros((PLANE, OWN), jnp.float32)
    for k in range(LINES * SLOT):
        value = jnp.where(spot == k, table[:, k : k + 1], value)
    answer = jnp.sum(jnp.where(sub == line, value, 0.0), axis=0, keepdims=True)
    out_ref[...] = answer.reshape(OWN)

    others = bs.at[pl.ds(0, PLANE - 1)]
    pltpu.make_async_copy(others, others, b_send).wait()

    straight = 2 * FAR * SPAN + SPAN
    by_relay = 2 * FAR * SPAN - SPAN

    def all_left(count, sem):
        gone = outgoing.at[pl.ds(0, count)]
        pltpu.make_async_copy(gone, gone, sem).wait()

    all_left(by_relay, relay_send)
    all_left(by_relay, on_send)

    @pl.when(holder)
    def _():
        left = ra.at[pl.ds(0, Z - 1)]
        pltpu.make_async_copy(left, left, a_send).wait()
        all_left(straight - SLOT, send_sem)

    @pl.when(jnp.logical_not(holder))
    def _():
        all_left(straight, send_sem)


def shards(emb, dest):
    dma = pltpu.SemaphoreType.DMA
    regular = pltpu.SemaphoreType.REGULAR
    return pl.pallas_call(
        body_kernel,
        out_shape=jax.ShapeDtypeStruct((OWN,), jnp.float32),
        in_specs=[pl.BlockSpec(memory_space=pl.ANY)] * 2,
        out_specs=pl.BlockSpec(memory_space=pltpu.VMEM),
        scratch_shapes=[
            pltpu.VMEM((OWN, D), jnp.bfloat16),
            pltpu.VMEM((OWN,), jnp.int32),
            pltpu.VMEM((OWN, D), jnp.bfloat16),
            pltpu.VMEM((2 * SPAN * SUB, 128), jnp.float32),
            pltpu.VMEM((GROUPS * SLOT, SUB, 128), jnp.bfloat16),
            pltpu.VMEM((2 * FAR, SPAN, SUB, 128), jnp.bfloat16),
            pltpu.VMEM((ROWS, SUB, 128), jnp.bfloat16),
            pltpu.VMEM((2 * CHUNK * SUB, 128), jnp.float32),
            pltpu.VMEM((2 * CHUNK, D), jnp.bfloat16),
            pltpu.VMEM((ROWS, D), jnp.bfloat16),
            pltpu.VMEM((1, ROWS), jnp.float32),
            pltpu.VMEM((1, ROWS), jnp.float32),
            pltpu.VMEM((Z, 1, 128), jnp.float32),
            pltpu.VMEM((LINES, 1, 128), jnp.float32),
            pltpu.VMEM((PLANE, 1, 128), jnp.float32),
            pltpu.VMEM((PLANE, 1, 128), jnp.float32),
            pltpu.SemaphoreType.DMA((2,)),
            pltpu.SemaphoreType.REGULAR((NEAR,)),
            regular,
            dma,
            pltpu.SemaphoreType.DMA((STEPS,)),
            dma,
            pltpu.SemaphoreType.DMA((FAR,)),
            dma,
            dma,
            dma,
            dma,
            dma,
        ],
        compiler_params=pltpu.CompilerParams(
            collective_id=0, has_side_effects=True, vmem_limit_bytes=60 << 20
        ),
        name="dedup",
    )(emb, dest)


def solution(mesh):
    in_specs = (P(("grp", "tile"), None), P(("grp", "tile")))
    out_specs = P(("grp", "tile"))
    return jax.shard_map(shards, mesh=mesh, in_specs=in_specs, out_specs=out_specs, check_vma=False)
```

```python
import jax
import jax.numpy as jnp
from jax import lax
from jax.experimental import pallas as pl
from jax.experimental.pallas import tpu as pltpu
from jax.sharding import PartitionSpec as P

MESH = pl.DeviceIdType.MESH
Z, X, C, Y = 16, 4, 2, 4
PLANE = X * C * Y
NEAR = Z // 4
FAR = Z // 4
SLOT = 3
OWN = 256
D = 1024
SUB = D // 128
STEPS = Z // 2
SPAN = X * C * SLOT
CHUNK = 2 * PLANE * SLOT
ROWS = STEPS * CHUNK
GROUPS = Z * X * C
LINES = Z // Y
DEAD = 2.0
LOW = -8.0


def grp_of(z, x, c):
    return (z * X + x) * C + c


def holder_y(z, c):
    return (z + 2 * c) % Y


def body_kernel(
    emb_ref, dest_ref, out_ref,
    emb_v, dest_v, unit, spread, outgoing, relay, arrived, spread_in, new_v, rows, pen_v, best_v, ra, ba, bs, bb,
    in_sem, near_sem, far_sem, send_sem, recv_sem, relay_send, relay_recv, on_send, a_send, a_recv, b_send, b_recv,
):
    g = lax.axis_index("grp")
    y = lax.axis_index("tile")
    z = g // (X * C)
    x = (g // C) % X
    c = g % C
    me = (x * C + c) * Y + y
    holder = y == holder_y(z, c)

    load = pltpu.make_async_copy(emb_ref, emb_v, in_sem.at[0])
    load.start()
    load_dest = pltpu.make_async_copy(dest_ref, dest_v, in_sem.at[1])
    load_dest.start()

    barrier = pltpu.get_barrier_semaphore()

    def greet_line(sem_of):
        def step(d, carry):
            for to in ((z + d) % Z, (z + Z - d) % Z):
                pl.semaphore_signal(
                    sem_of(d), inc=1, device_id=(grp_of(to, x, c), y), device_id_type=MESH
                )
            return carry

        lax.fori_loop(1, NEAR + 1, step, 0)

    greet_line(lambda d: barrier)

    def mate(i):
        return (x + 2 + i // (C * Y)) % X, (y + 2 + (i // C) % Y) % Y, (c + i) % C

    itself = X // 2 * C * Y + Y // 2 * C

    for i in range(PLANE):
        if i != itself:
            to_x, to_y, to_c = mate(i)
            pl.semaphore_signal(
                barrier, inc=1, device_id=(grp_of(z, to_x, to_c), to_y), device_id_type=MESH
            )

    load_dest.wait()
    dest = dest_v[...].reshape(1, OWN)
    sub = lax.broadcasted_iota(jnp.int32, (OWN, OWN), 0)
    lane = lax.broadcasted_iota(jnp.int32, (OWN, OWN), 1)
    dest_down = jnp.sum(jnp.where(sub == lane, dest, 0), axis=1, keepdims=True)
    rank = jnp.sum(jnp.where((dest_down == dest) & (sub < lane), 1, 0), axis=0, keepdims=True)
    position = dest * SLOT + rank

    load.wait()

    def normalise(i, carry):
        part = pl.ds(pl.multiple_of(i * 32, 32), 32)
        wide = emb_v[part, :].astype(jnp.float32)
        norm = jnp.sqrt(jnp.sum(wide * wide, axis=1, keepdims=True)) + 1e-6
        unit[part, :] = (wide / norm).astype(jnp.bfloat16)
        return carry

    lax.fori_loop(0, OWN // 32, normalise, 0)

    pl.semaphore_wait(barrier, 2 * NEAR + PLANE - 1)
    greet_line(lambda d: near_sem.at[d - 1])

    def up(d):
        return (z + d) % Z

    def down(d):
        return (z + Z - d) % Z

    def pack(e):
        first, second = up(e + 1), jnp.where(e == STEPS - 1, z, down(e + 1))
        r = lax.broadcasted_iota(jnp.int32, (2 * SPAN, 1), 0)
        ids = r + jnp.where(r < SPAN, first * SPAN, second * SPAN - SPAN)
        pick = ids == position
        chosen = jnp.dot(
            jnp.where(pick, 1.0, 0.0).astype(jnp.bfloat16), unit[...],
            preferred_element_type=jnp.float32,
        )
        live = jnp.sum(jnp.where(pick, 1.0, 0.0), axis=1, keepdims=True)
        head = lax.broadcasted_iota(jnp.int32, (2 * SPAN, 128), 1) == 0
        for k in range(SUB):
            part = chosen[:, 128 * k : 128 * (k + 1)]
            if k == 0:
                part = jnp.where(head & (live < 0.5), DEAD, part)
            spread[pl.ds(k, 2 * SPAN, stride=SUB), :] = part
        outgoing[pl.ds(e * 2 * SPAN, 2 * SPAN)] = (
            spread[...].reshape(2 * SPAN, SUB, 128).astype(jnp.bfloat16)
        )

    def post(src, to_z, in_plane, half, e, sem):
        dst = arrived.at[pl.ds((half * PLANE + me) * SLOT, SLOT)]
        to_y = holder_y(to_z, in_plane % C)
        pltpu.make_async_remote_copy(
            src_ref=src, dst_ref=dst, send_sem=sem, recv_sem=recv_sem.at[e],
            device_id=(to_z * (X * C) + in_plane, to_y), device_id_type=MESH,
        ).start()

    def from_outgoing(half, in_plane):
        return outgoing.at[pl.ds(half * SPAN + in_plane * SLOT, SLOT)]

    def send(e):
        def one(i, carry):
            s = i % 2
            in_plane = (x * C + c + i // 2) % (X * C)
            half = e * 2 + s
            post(
                from_outgoing(half, in_plane), jnp.where(s == 0, up(e + 1), down(e + 1)),
                in_plane, half, e, send_sem,
            )
            return carry

        lax.fori_loop(0, 2 * X * C, one, 0)

    def send_here():
        half, e = 2 * STEPS - 1, STEPS - 1

        def one(i, carry):
            in_plane = (x * C + c + i) % (X * C)
            mine = (in_plane == x * C + c) & holder
            src = from_outgoing(half, in_plane)

            @pl.when(mine)
            def _():
                dst = arrived.at[pl.ds((half * PLANE + me) * SLOT, SLOT)]
                pltpu.make_async_copy(src, dst, recv_sem.at[e]).start()

            @pl.when(jnp.logical_not(mine))
            def _():
                post(src, z, in_plane, half, e, send_sem)

            return carry

        lax.fori_loop(0, X * C, one, 0)

    def send_relay(k):
        e = STEPS - 1 - k

        def hop(to_z, src, dst):
            pltpu.make_async_remote_copy(
                src_ref=src, dst_ref=dst, send_sem=relay_send, recv_sem=relay_recv.at[k],
                device_id=(grp_of(to_z, x, c), y), device_id_type=MESH,
            ).start()

        @pl.when(k == 0)
        def _():
            lower = outgoing.at[pl.ds(2 * e * SPAN, SPAN // 2)]
            upper = outgoing.at[pl.ds(2 * e * SPAN + SPAN // 2, SPAN // 2)]
            hop(up(1), lower, relay.at[0, pl.ds(0, SPAN // 2)])
            hop(down(1), upper, relay.at[1, pl.ds(SPAN // 2, SPAN // 2)])

        @pl.when(k > 0)
        def _():
            hop(up(1), outgoing.at[pl.ds(2 * e * SPAN, SPAN)], relay.at[2 * k])
            hop(down(1), outgoing.at[pl.ds((2 * e + 1) * SPAN, SPAN)], relay.at[2 * k + 1])

    def pass_relay(k, carry):
        e = STEPS - 1 - k

        @pl.when(k == 0)
        def _():
            pltpu.make_async_copy(relay.at[0], relay.at[0], relay_recv.at[0]).wait()

        @pl.when(k > 0)
        def _():
            both = relay.at[pl.ds(2 * k, 2)]
            pltpu.make_async_copy(both, both, relay_recv.at[k]).wait()

        def one(i, carry):
            s = i % 2
            in_plane = (x * C + c + i // 2) % (X * C)
            half = 2 * e + jnp.where(k == 0, 0, s)

            @pl.when((k > 0) | (in_plane // (X * C // 2) == s))
            def _():
                post(
                    relay.at[2 * k + s, pl.ds(in_plane * SLOT, SLOT)],
                    jnp.where(s == 0, up(e), down(e)), in_plane, half, e, on_send,
                )

            return carry

        lax.fori_loop(0, 2 * X * C, one, 0)
        return carry

    def step_out(i, carry):
        e = jnp.where(i < FAR, STEPS - 1 - i, jnp.where(i == STEPS - 1, 0, i - FAR + 1))
        pack(e)

        @pl.when(i < FAR)
        def _():
            send_relay(i)

        @pl.when((i >= FAR) & (i < STEPS - 1))
        def _():
            pl.semaphore_wait(near_sem.at[e], 2)

        @pl.when(i == STEPS - 2)
        def _():
            pl.semaphore_wait(near_sem.at[0], 2)
            for to in (up(NEAR), down(NEAR)):
                pl.semaphore_signal(
                    far_sem, inc=1, device_id=(grp_of(to, x, c), y), device_id_type=MESH
                )

        @pl.when(i == STEPS - 1)
        def _():
            pl.semaphore_wait(far_sem, 2)
            lax.fori_loop(0, FAR, pass_relay, 0)

        @pl.when(i >= FAR)
        def _():
            send(e)

        @pl.when(i == FAR)
        def _():
            send_here()

        return carry

    lax.fori_loop(0, STEPS, step_out, 0)

    def take(e):
        here = pl.ds(pl.multiple_of(e * CHUNK, CHUNK), CHUNK)
        block = arrived.at[here]
        pltpu.make_async_copy(block, block, recv_sem.at[e]).wait()
        spread_in[...] = block[...].astype(jnp.float32).reshape(CHUNK * SUB, 128)
        for k in range(SUB):
            new_v[:, 128 * k : 128 * (k + 1)] = spread_in[
                pl.ds(k, CHUNK, stride=SUB), :
            ].astype(jnp.bfloat16)
        new = new_v[...]
        dead = spread_in[pl.ds(0, CHUNK, stride=SUB), :][:, 0:1] > 1.5
        minus = jnp.where(dead, LOW, 0.0)
        sub = lax.broadcasted_iota(jnp.int32, (CHUNK, CHUNK), 0)
        lane = lax.broadcasted_iota(jnp.int32, (CHUNK, CHUNK), 1)
        same = sub == lane

        def scores(others):
            return lax.dot_general(
                new, others, (((1,), (1,)), ((), ())), preferred_element_type=jnp.float32
            )

        old = scores(rows[...])
        own = jnp.where(same, LOW, scores(new) + minus)
        best = jnp.maximum(best_v[...], jnp.max(old + minus, axis=0, keepdims=True))
        top = jnp.max(old + pen_v[...], axis=1, keepdims=True)
        mine = jnp.maximum(
            jnp.max(own, axis=0, keepdims=True),
            jnp.max(jnp.where(same, top, LOW), axis=0, keepdims=True),
        )
        across = jnp.sum(jnp.where(same, minus, 0.0), axis=0, keepdims=True)
        at = lax.broadcasted_iota(jnp.int32, (1, ROWS), 1)
        inside = (at >= e * CHUNK) & (at < (e + 1) * CHUNK)
        best_v[...] = jnp.where(inside, jnp.concatenate([mine] * STEPS, axis=1), best)
        pen_v[...] = jnp.where(inside, jnp.concatenate([across] * STEPS, axis=1), pen_v[...])
        rows[here, :] = new

    @pl.when(holder)
    def _():
        rows[...] = jnp.zeros((ROWS, D), jnp.bfloat16)
        pen_v[...] = jnp.full((1, ROWS), LOW, jnp.float32)
        best_v[...] = jnp.full((1, ROWS), -1.0, jnp.float32)

        def compare(i, carry):
            take(jnp.where(i < FAR - 1, i + 1, jnp.where(i == STEPS - 1, 0, STEPS + FAR - 2 - i)))
            return carry

        lax.fori_loop(0, STEPS, compare, 0)
        best = jnp.maximum(best_v[...], -1.0)
        width = PLANE * SLOT
        fill = jnp.zeros((1, 128 - width), jnp.float32)
        for e in reversed(range(STEPS)):
            for s in range(2):
                i = e * 2 + s
                ra[i] = jnp.concatenate([best[:, i * width : (i + 1) * width], fill], axis=1)
                src, dst = ra.at[i], ba.at[z // Y]
                if i == Z - 1:
                    pltpu.make_async_copy(src, dst, a_recv).start()
                else:
                    to_z = down(e + 1) if s == 0 else up(e + 1)
                    pltpu.make_async_remote_copy(
                        src_ref=src, dst_ref=dst, send_sem=a_send, recv_sem=a_recv,
                        device_id=(grp_of(to_z, x, c), y), device_id_type=MESH,
                    ).start()

    pltpu.make_async_copy(ba, ba, a_recv).wait()
    sub = lax.broadcasted_iota(jnp.int32, (PLANE, 128), 0)
    lane = lax.broadcasted_iota(jnp.int32, (PLANE, 128), 1)
    turned = jnp.zeros((PLANE, 128), jnp.float32)
    for j in range(SLOT):
        its = lane == sub * SLOT + j
        for h in range(LINES):
            column = jnp.sum(jnp.where(its, ba[h], 0.0), axis=1, keepdims=True)
            turned = jnp.where(lane == h * SLOT + j, column, turned)
    bs[...] = turned.reshape(PLANE, 1, 128)

    for i in range(PLANE):
        to_x, to_y, to_c = mate(i)
        to = (to_x * C + to_c) * Y + to_y
        if i == itself:
            pltpu.make_async_copy(bs.at[me], bb.at[me], b_recv).start()
        else:
            pltpu.make_async_remote_copy(
                src_ref=bs.at[to], dst_ref=bb.at[me], send_sem=b_send, recv_sem=b_recv,
                device_id=(grp_of(z, to_x, to_c), to_y), device_id_type=MESH,
            ).start()

    dz = dest // (X * C)
    dx = (dest // C) % X
    dc = dest % C
    line = (dx * C + dc) * Y + holder_y(dz, dc)
    spot = (dz // Y) * SLOT + rank
    sub = lax.broadcasted_iota(jnp.int32, (PLANE, OWN), 0)
    pltpu.make_async_copy(bb, bb, b_recv).wait()
    table = bb[...].reshape(PLANE, 128)
    value = jnp.zeros((PLANE, OWN), jnp.float32)
    for k in range(LINES * SLOT):
        value = jnp.where(spot == k, table[:, k : k + 1], value)
    answer = jnp.sum(jnp.where(sub == line, value, 0.0), axis=0, keepdims=True)
    out_ref[...] = answer.reshape(OWN)

    others = bs.at[pl.ds(0, PLANE - 1)]
    pltpu.make_async_copy(others, others, b_send).wait()

    straight = 2 * FAR * SPAN + SPAN
    by_relay = 2 * FAR * SPAN - SPAN

    def all_left(count, sem):
        gone = outgoing.at[pl.ds(0, count)]
        pltpu.make_async_copy(gone, gone, sem).wait()

    all_left(by_relay, relay_send)
    all_left(by_relay, on_send)

    @pl.when(holder)
    def _():
        left = ra.at[pl.ds(0, Z - 1)]
        pltpu.make_async_copy(left, left, a_send).wait()
        all_left(straight - SLOT, send_sem)

    @pl.when(jnp.logical_not(holder))
    def _():
        all_left(straight, send_sem)


def shards(emb, dest):
    dma = pltpu.SemaphoreType.DMA
    regular = pltpu.SemaphoreType.REGULAR
    return pl.pallas_call(
        body_kernel,
        out_shape=jax.ShapeDtypeStruct((OWN,), jnp.float32),
        in_specs=[pl.BlockSpec(memory_space=pl.ANY)] * 2,
        out_specs=pl.BlockSpec(memory_space=pltpu.VMEM),
        scratch_shapes=[
            pltpu.VMEM((OWN, D), jnp.bfloat16),
            pltpu.VMEM((OWN,), jnp.int32),
            pltpu.VMEM((OWN, D), jnp.bfloat16),
            pltpu.VMEM((2 * SPAN * SUB, 128), jnp.float32),
            pltpu.VMEM((GROUPS * SLOT, SUB, 128), jnp.bfloat16),
            pltpu.VMEM((2 * FAR, SPAN, SUB, 128), jnp.bfloat16),
            pltpu.VMEM((ROWS, SUB, 128), jnp.bfloat16),
            pltpu.VMEM((CHUNK * SUB, 128), jnp.float32),
            pltpu.VMEM((CHUNK, D), jnp.bfloat16),
            pltpu.VMEM((ROWS, D), jnp.bfloat16),
            pltpu.VMEM((1, ROWS), jnp.float32),
            pltpu.VMEM((1, ROWS), jnp.float32),
            pltpu.VMEM((Z, 1, 128), jnp.float32),
            pltpu.VMEM((LINES, 1, 128), jnp.float32),
            pltpu.VMEM((PLANE, 1, 128), jnp.float32),
            pltpu.VMEM((PLANE, 1, 128), jnp.float32),
            pltpu.SemaphoreType.DMA((2,)),
            pltpu.SemaphoreType.REGULAR((NEAR,)),
            regular,
            dma,
            pltpu.SemaphoreType.DMA((STEPS,)),
            dma,
            pltpu.SemaphoreType.DMA((FAR,)),
            dma,
            dma,
            dma,
            dma,
            dma,
        ],
        compiler_params=pltpu.CompilerParams(
            collective_id=0, has_side_effects=True, vmem_limit_bytes=60 << 20
        ),
        name="dedup",
    )(emb, dest)


def solution(mesh):
    in_specs = (P(("grp", "tile"), None), P(("grp", "tile")))
    out_specs = P(("grp", "tile"))
    return jax.shard_map(shards, mesh=mesh, in_specs=in_specs, out_specs=out_specs, check_vma=False)
```

```python
import jax
import jax.numpy as jnp
from jax import lax
from jax.experimental import pallas as pl
from jax.experimental.pallas import tpu as pltpu
from jax.sharding import PartitionSpec as P

MESH = pl.DeviceIdType.MESH
Z, X, C, Y = 16, 4, 2, 4
PLANE = X * C * Y
NEAR = Z // 4
FAR = Z // 4
SLOT = 3
OWN = 256
D = 1024
SUB = D // 128
STEPS = Z // 2
SPAN = X * C * SLOT
CHUNK = 2 * PLANE * SLOT
ROWS = STEPS * CHUNK
GROUPS = Z * X * C
LINES = Z // Y
DEAD = 2.0
LOW = -8.0


def grp_of(z, x, c):
    return (z * X + x) * C + c


def holder_y(z, c):
    return (z + 2 * c) % Y


def body_kernel(
    emb_ref, dest_ref, out_ref,
    emb_v, dest_v, unit, spread, outgoing, relay, arrived, spread_in, new_v, rows, pen_v, best_v, ra, ba, bs, bb,
    in_sem, near_sem, far_sem, send_sem, recv_sem, relay_send, relay_recv, on_send, a_send, a_recv, b_send, b_recv,
):
    g = lax.axis_index("grp")
    y = lax.axis_index("tile")
    z = g // (X * C)
    x = (g // C) % X
    c = g % C
    me = (x * C + c) * Y + y
    holder = y == holder_y(z, c)

    load = pltpu.make_async_copy(emb_ref, emb_v, in_sem.at[0])
    load.start()
    load_dest = pltpu.make_async_copy(dest_ref, dest_v, in_sem.at[1])
    load_dest.start()

    barrier = pltpu.get_barrier_semaphore()

    def greet_line(sem_of):
        for d in range(1, NEAR + 1):
            for to in ((z + d) % Z, (z + Z - d) % Z):
                pl.semaphore_signal(
                    sem_of(d), inc=1, device_id=(grp_of(to, x, c), y), device_id_type=MESH
                )

    greet_line(lambda d: barrier)

    def mate(i):
        return (x + 2 + i // (C * Y)) % X, (y + 2 + (i // C) % Y) % Y, (c + i) % C

    itself = X // 2 * C * Y + Y // 2 * C

    for i in range(PLANE):
        if i != itself:
            to_x, to_y, to_c = mate(i)
            pl.semaphore_signal(
                barrier, inc=1, device_id=(grp_of(z, to_x, to_c), to_y), device_id_type=MESH
            )

    load_dest.wait()
    dest = dest_v[...].reshape(1, OWN)
    sub = lax.broadcasted_iota(jnp.int32, (OWN, OWN), 0)
    lane = lax.broadcasted_iota(jnp.int32, (OWN, OWN), 1)
    dest_down = jnp.sum(jnp.where(sub == lane, dest, 0), axis=1, keepdims=True)
    rank = jnp.sum(jnp.where((dest_down == dest) & (sub < lane), 1, 0), axis=0, keepdims=True)
    position = dest * SLOT + rank

    load.wait()

    def normalise(i, carry):
        part = pl.ds(pl.multiple_of(i * 32, 32), 32)
        wide = emb_v[part, :].astype(jnp.float32)
        norm = jnp.sqrt(jnp.sum(wide * wide, axis=1, keepdims=True)) + 1e-6
        unit[part, :] = (wide / norm).astype(jnp.bfloat16)
        return carry

    lax.fori_loop(0, OWN // 32, normalise, 0)

    pl.semaphore_wait(barrier, 2 * NEAR + PLANE - 1)
    greet_line(lambda d: near_sem.at[d - 1])

    def up(d):
        return (z + d) % Z

    def down(d):
        return (z + Z - d) % Z

    def pack(e):
        first, second = up(e + 1), jnp.where(e == STEPS - 1, z, down(e + 1))
        r = lax.broadcasted_iota(jnp.int32, (2 * SPAN, 1), 0)
        ids = r + jnp.where(r < SPAN, first * SPAN, second * SPAN - SPAN)
        pick = ids == position
        chosen = jnp.dot(
            jnp.where(pick, 1.0, 0.0).astype(jnp.bfloat16), unit[...],
            preferred_element_type=jnp.float32,
        )
        live = jnp.sum(jnp.where(pick, 1.0, 0.0), axis=1, keepdims=True)
        head = lax.broadcasted_iota(jnp.int32, (2 * SPAN, 128), 1) == 0
        for k in range(SUB):
            part = chosen[:, 128 * k : 128 * (k + 1)]
            if k == 0:
                part = jnp.where(head & (live < 0.5), DEAD, part)
            spread[pl.ds(k, 2 * SPAN, stride=SUB), :] = part
        outgoing[pl.ds(e * 2 * SPAN, 2 * SPAN)] = (
            spread[...].reshape(2 * SPAN, SUB, 128).astype(jnp.bfloat16)
        )

    def post(src, to_z, in_plane, half, e, sem):
        dst = arrived.at[pl.ds((half * PLANE + me) * SLOT, SLOT)]
        to_y = holder_y(to_z, in_plane % C)
        pltpu.make_async_remote_copy(
            src_ref=src, dst_ref=dst, send_sem=sem, recv_sem=recv_sem.at[e],
            device_id=(to_z * (X * C) + in_plane, to_y), device_id_type=MESH,
        ).start()

    def from_outgoing(half, in_plane):
        return outgoing.at[pl.ds(half * SPAN + in_plane * SLOT, SLOT)]

    def send(e):
        for i in range(X * C):
            in_plane = (x * C + c + i) % (X * C)
            for s, to_z in enumerate((up(e + 1), down(e + 1))):
                half = e * 2 + s
                post(from_outgoing(half, in_plane), to_z, in_plane, half, e, send_sem)

    def send_here():
        half, e = 2 * STEPS - 1, STEPS - 1

        def one(i, carry):
            in_plane = (x * C + c + i) % (X * C)
            mine = (in_plane == x * C + c) & holder
            src = from_outgoing(half, in_plane)

            @pl.when(mine)
            def _():
                dst = arrived.at[pl.ds((half * PLANE + me) * SLOT, SLOT)]
                pltpu.make_async_copy(src, dst, recv_sem.at[e]).start()

            @pl.when(jnp.logical_not(mine))
            def _():
                post(src, z, in_plane, half, e, send_sem)

            return carry

        lax.fori_loop(0, X * C, one, 0)

    def send_relay(k):
        e = STEPS - 1 - k

        def hop(to_z, src, dst):
            pltpu.make_async_remote_copy(
                src_ref=src, dst_ref=dst, send_sem=relay_send, recv_sem=relay_recv.at[k],
                device_id=(grp_of(to_z, x, c), y), device_id_type=MESH,
            ).start()

        @pl.when(k == 0)
        def _():
            lower = outgoing.at[pl.ds(2 * e * SPAN, SPAN // 2)]
            upper = outgoing.at[pl.ds(2 * e * SPAN + SPAN // 2, SPAN // 2)]
            hop(up(1), lower, relay.at[0, pl.ds(0, SPAN // 2)])
            hop(down(1), upper, relay.at[1, pl.ds(SPAN // 2, SPAN // 2)])

        @pl.when(k > 0)
        def _():
            hop(up(1), outgoing.at[pl.ds(2 * e * SPAN, SPAN)], relay.at[2 * k])
            hop(down(1), outgoing.at[pl.ds((2 * e + 1) * SPAN, SPAN)], relay.at[2 * k + 1])

    def pass_relay(k, carry):
        e = STEPS - 1 - k

        @pl.when(k == 0)
        def _():
            pltpu.make_async_copy(relay.at[0], relay.at[0], relay_recv.at[0]).wait()

        @pl.when(k > 0)
        def _():
            both = relay.at[pl.ds(2 * k, 2)]
            pltpu.make_async_copy(both, both, relay_recv.at[k]).wait()

        def one(i, carry):
            s = i % 2
            in_plane = (x * C + c + i // 2) % (X * C)
            half = 2 * e + jnp.where(k == 0, 0, s)

            @pl.when((k > 0) | (in_plane // (X * C // 2) == s))
            def _():
                post(
                    relay.at[2 * k + s, pl.ds(in_plane * SLOT, SLOT)],
                    jnp.where(s == 0, up(e), down(e)), in_plane, half, e, on_send,
                )

            return carry

        lax.fori_loop(0, 2 * X * C, one, 0)
        return carry

    def step_out(i, carry):
        e = jnp.where(i < FAR, STEPS - 1 - i, jnp.where(i == STEPS - 1, 0, i - FAR + 1))
        pack(e)

        @pl.when(i < FAR)
        def _():
            send_relay(i)

        @pl.when((i >= FAR) & (i < STEPS - 1))
        def _():
            pl.semaphore_wait(near_sem.at[e], 2)

        @pl.when(i == STEPS - 2)
        def _():
            pl.semaphore_wait(near_sem.at[0], 2)
            for to in (up(NEAR), down(NEAR)):
                pl.semaphore_signal(
                    far_sem, inc=1, device_id=(grp_of(to, x, c), y), device_id_type=MESH
                )

        @pl.when(i == STEPS - 1)
        def _():
            pl.semaphore_wait(far_sem, 2)
            lax.fori_loop(0, FAR, pass_relay, 0)

        @pl.when(i >= FAR)
        def _():
            send(e)

        @pl.when(i == FAR)
        def _():
            send_here()

        return carry

    lax.fori_loop(0, STEPS, step_out, 0)

    def take(e):
        here = pl.ds(pl.multiple_of(e * CHUNK, CHUNK), CHUNK)
        block = arrived.at[here]
        pltpu.make_async_copy(block, block, recv_sem.at[e]).wait()
        spread_in[...] = block[...].astype(jnp.float32).reshape(CHUNK * SUB, 128)
        for k in range(SUB):
            new_v[:, 128 * k : 128 * (k + 1)] = spread_in[
                pl.ds(k, CHUNK, stride=SUB), :
            ].astype(jnp.bfloat16)
        new = new_v[...]
        dead = spread_in[pl.ds(0, CHUNK, stride=SUB), :][:, 0:1] > 1.5
        minus = jnp.where(dead, LOW, 0.0)
        sub = lax.broadcasted_iota(jnp.int32, (CHUNK, CHUNK), 0)
        lane = lax.broadcasted_iota(jnp.int32, (CHUNK, CHUNK), 1)
        same = sub == lane

        def scores(others):
            return lax.dot_general(
                new, others, (((1,), (1,)), ((), ())), preferred_element_type=jnp.float32
            )

        old = scores(rows[...])
        own = jnp.where(same, LOW, scores(new) + minus)
        best = jnp.maximum(best_v[...], jnp.max(old + minus, axis=0, keepdims=True))
        top = jnp.max(old + pen_v[...], axis=1, keepdims=True)
        mine = jnp.maximum(
            jnp.max(own, axis=0, keepdims=True),
            jnp.max(jnp.where(same, top, LOW), axis=0, keepdims=True),
        )
        across = jnp.sum(jnp.where(same, minus, 0.0), axis=0, keepdims=True)
        at = lax.broadcasted_iota(jnp.int32, (1, ROWS), 1)
        inside = (at >= e * CHUNK) & (at < (e + 1) * CHUNK)
        best_v[...] = jnp.where(inside, jnp.concatenate([mine] * STEPS, axis=1), best)
        pen_v[...] = jnp.where(inside, jnp.concatenate([across] * STEPS, axis=1), pen_v[...])
        rows[here, :] = new

    @pl.when(holder)
    def _():
        rows[...] = jnp.zeros((ROWS, D), jnp.bfloat16)
        pen_v[...] = jnp.full((1, ROWS), LOW, jnp.float32)
        best_v[...] = jnp.full((1, ROWS), -1.0, jnp.float32)

        def compare(i, carry):
            take(jnp.where(i < FAR - 1, i + 1, jnp.where(i == STEPS - 1, 0, STEPS + FAR - 2 - i)))
            return carry

        lax.fori_loop(0, STEPS, compare, 0)
        best = jnp.maximum(best_v[...], -1.0)
        width = PLANE * SLOT
        fill = jnp.zeros((1, 128 - width), jnp.float32)
        for e in reversed(range(STEPS)):
            for s in range(2):
                i = e * 2 + s
                ra[i] = jnp.concatenate([best[:, i * width : (i + 1) * width], fill], axis=1)
                src, dst = ra.at[i], ba.at[z // Y]
                if i == Z - 1:
                    pltpu.make_async_copy(src, dst, a_recv).start()
                else:
                    to_z = down(e + 1) if s == 0 else up(e + 1)
                    pltpu.make_async_remote_copy(
                        src_ref=src, dst_ref=dst, send_sem=a_send, recv_sem=a_recv,
                        device_id=(grp_of(to_z, x, c), y), device_id_type=MESH,
                    ).start()

    pltpu.make_async_copy(ba, ba, a_recv).wait()
    sub = lax.broadcasted_iota(jnp.int32, (PLANE, 128), 0)
    lane = lax.broadcasted_iota(jnp.int32, (PLANE, 128), 1)
    turned = jnp.zeros((PLANE, 128), jnp.float32)
    for j in range(SLOT):
        its = lane == sub * SLOT + j
        for h in range(LINES):
            column = jnp.sum(jnp.where(its, ba[h], 0.0), axis=1, keepdims=True)
            turned = jnp.where(lane == h * SLOT + j, column, turned)
    bs[...] = turned.reshape(PLANE, 1, 128)

    for i in range(PLANE):
        to_x, to_y, to_c = mate(i)
        to = (to_x * C + to_c) * Y + to_y
        if i == itself:
            pltpu.make_async_copy(bs.at[me], bb.at[me], b_recv).start()
        else:
            pltpu.make_async_remote_copy(
                src_ref=bs.at[to], dst_ref=bb.at[me], send_sem=b_send, recv_sem=b_recv,
                device_id=(grp_of(z, to_x, to_c), to_y), device_id_type=MESH,
            ).start()

    dz = dest // (X * C)
    dx = (dest // C) % X
    dc = dest % C
    line = (dx * C + dc) * Y + holder_y(dz, dc)
    spot = (dz // Y) * SLOT + rank
    sub = lax.broadcasted_iota(jnp.int32, (PLANE, OWN), 0)
    pltpu.make_async_copy(bb, bb, b_recv).wait()
    table = bb[...].reshape(PLANE, 128)
    value = jnp.zeros((PLANE, OWN), jnp.float32)
    for k in range(LINES * SLOT):
        value = jnp.where(spot == k, table[:, k : k + 1], value)
    answer = jnp.sum(jnp.where(sub == line, value, 0.0), axis=0, keepdims=True)
    out_ref[...] = answer.reshape(OWN)

    others = bs.at[pl.ds(0, PLANE - 1)]
    pltpu.make_async_copy(others, others, b_send).wait()

    straight = 2 * FAR * SPAN + SPAN
    by_relay = 2 * FAR * SPAN - SPAN

    def all_left(count, sem):
        gone = outgoing.at[pl.ds(0, count)]
        pltpu.make_async_copy(gone, gone, sem).wait()

    all_left(by_relay, relay_send)
    all_left(by_relay, on_send)

    @pl.when(holder)
    def _():
        left = ra.at[pl.ds(0, Z - 1)]
        pltpu.make_async_copy(left, left, a_send).wait()
        all_left(straight - SLOT, send_sem)

    @pl.when(jnp.logical_not(holder))
    def _():
        all_left(straight, send_sem)


def shards(emb, dest):
    dma = pltpu.SemaphoreType.DMA
    regular = pltpu.SemaphoreType.REGULAR
    return pl.pallas_call(
        body_kernel,
        out_shape=jax.ShapeDtypeStruct((OWN,), jnp.float32),
        in_specs=[pl.BlockSpec(memory_space=pl.ANY)] * 2,
        out_specs=pl.BlockSpec(memory_space=pltpu.VMEM),
        scratch_shapes=[
            pltpu.VMEM((OWN, D), jnp.bfloat16),
            pltpu.VMEM((OWN,), jnp.int32),
            pltpu.VMEM((OWN, D), jnp.bfloat16),
            pltpu.VMEM((2 * SPAN * SUB, 128), jnp.float32),
            pltpu.VMEM((GROUPS * SLOT, SUB, 128), jnp.bfloat16),
            pltpu.VMEM((2 * FAR, SPAN, SUB, 128), jnp.bfloat16),
            pltpu.VMEM((ROWS, SUB, 128), jnp.bfloat16),
            pltpu.VMEM((CHUNK * SUB, 128), jnp.float32),
            pltpu.VMEM((CHUNK, D), jnp.bfloat16),
            pltpu.VMEM((ROWS, D), jnp.bfloat16),
            pltpu.VMEM((1, ROWS), jnp.float32),
            pltpu.VMEM((1, ROWS), jnp.float32),
            pltpu.VMEM((Z, 1, 128), jnp.float32),
            pltpu.VMEM((LINES, 1, 128), jnp.float32),
            pltpu.VMEM((PLANE, 1, 128), jnp.float32),
            pltpu.VMEM((PLANE, 1, 128), jnp.float32),
            pltpu.SemaphoreType.DMA((2,)),
            pltpu.SemaphoreType.REGULAR((NEAR,)),
            regular,
            dma,
            pltpu.SemaphoreType.DMA((STEPS,)),
            dma,
            pltpu.SemaphoreType.DMA((FAR,)),
            dma,
            dma,
            dma,
            dma,
            dma,
        ],
        compiler_params=pltpu.CompilerParams(
            collective_id=0, has_side_effects=True, vmem_limit_bytes=60 << 20
        ),
        name="dedup",
    )(emb, dest)


def solution(mesh):
    in_specs = (P(("grp", "tile"), None), P(("grp", "tile")))
    out_specs = P(("grp", "tile"))
    return jax.shard_map(shards, mesh=mesh, in_specs=in_specs, out_specs=out_specs, check_vma=False)
```

```python
import jax
import jax.numpy as jnp
from jax import lax
from jax.experimental import pallas as pl
from jax.experimental.pallas import tpu as pltpu
from jax.sharding import PartitionSpec as P

MESH = pl.DeviceIdType.MESH
Z, X, C, Y = 16, 4, 2, 4
PLANE = X * C * Y
NEAR = Z // 4
FAR = Z // 4
SLOT = 3
OWN = 256
D = 1024
SUB = D // 128
STEPS = Z // 2
SPAN = X * C * SLOT
CHUNK = 2 * PLANE * SLOT
ROWS = STEPS * CHUNK
GROUPS = Z * X * C
LINES = Z // Y
DEAD = 2.0
LOW = -8.0


def grp_of(z, x, c):
    return (z * X + x) * C + c


def holder_y(z, c):
    return (z + 2 * c) % Y


def body_kernel(
    emb_ref, dest_ref, out_ref,
    emb_v, dest_v, unit, spread, outgoing, relay, arrived, spread_in, new_v, rows, pen_v, best_v, ra, ba, bs, bb,
    in_sem, near_sem, far_sem, send_sem, recv_sem, relay_send, relay_recv, on_send, a_send, a_recv, b_send, b_recv,
):
    g = lax.axis_index("grp")
    y = lax.axis_index("tile")
    z = g // (X * C)
    x = (g // C) % X
    c = g % C
    me = (x * C + c) * Y + y
    holder = y == holder_y(z, c)

    load = pltpu.make_async_copy(emb_ref, emb_v, in_sem.at[0])
    load.start()
    load_dest = pltpu.make_async_copy(dest_ref, dest_v, in_sem.at[1])
    load_dest.start()

    barrier = pltpu.get_barrier_semaphore()

    def greet_line(sem_of):
        def step(d, carry):
            for to in ((z + d) % Z, (z + Z - d) % Z):
                pl.semaphore_signal(
                    sem_of(d), inc=1, device_id=(grp_of(to, x, c), y), device_id_type=MESH
                )
            return carry

        lax.fori_loop(1, NEAR + 1, step, 0)

    greet_line(lambda d: barrier)

    def mate(i):
        return (x + 2 + i // (C * Y)) % X, (y + 2 + (i // C) % Y) % Y, (c + i) % C

    itself = X // 2 * C * Y + Y // 2 * C

    for i in range(PLANE):
        if i != itself:
            to_x, to_y, to_c = mate(i)
            pl.semaphore_signal(
                barrier, inc=1, device_id=(grp_of(z, to_x, to_c), to_y), device_id_type=MESH
            )

    load_dest.wait()
    dest = dest_v[...].reshape(1, OWN)
    sub = lax.broadcasted_iota(jnp.int32, (OWN, OWN), 0)
    lane = lax.broadcasted_iota(jnp.int32, (OWN, OWN), 1)
    dest_down = jnp.sum(jnp.where(sub == lane, dest, 0), axis=1, keepdims=True)
    rank = jnp.sum(jnp.where((dest_down == dest) & (sub < lane), 1, 0), axis=0, keepdims=True)
    position = dest * SLOT + rank

    load.wait()

    def normalise(i, carry):
        part = pl.ds(pl.multiple_of(i * 32, 32), 32)
        wide = emb_v[part, :].astype(jnp.float32)
        norm = jnp.sqrt(jnp.sum(wide * wide, axis=1, keepdims=True)) + 1e-6
        unit[part, :] = (wide / norm).astype(jnp.bfloat16)
        return carry

    lax.fori_loop(0, OWN // 32, normalise, 0)

    pl.semaphore_wait(barrier, 2 * NEAR + PLANE - 1)
    greet_line(lambda d: near_sem.at[d - 1])

    def up(d):
        return (z + d) % Z

    def down(d):
        return (z + Z - d) % Z

    def pack(e):
        first, second = up(e + 1), jnp.where(e == STEPS - 1, z, down(e + 1))
        r = lax.broadcasted_iota(jnp.int32, (2 * SPAN, 1), 0)
        ids = r + jnp.where(r < SPAN, first * SPAN, second * SPAN - SPAN)
        pick = ids == position
        chosen = jnp.dot(
            jnp.where(pick, 1.0, 0.0).astype(jnp.bfloat16), unit[...],
            preferred_element_type=jnp.float32,
        )
        live = jnp.sum(jnp.where(pick, 1.0, 0.0), axis=1, keepdims=True)
        head = lax.broadcasted_iota(jnp.int32, (2 * SPAN, 128), 1) == 0
        for k in range(SUB):
            part = chosen[:, 128 * k : 128 * (k + 1)]
            if k == 0:
                part = jnp.where(head & (live < 0.5), DEAD, part)
            spread[pl.ds(k, 2 * SPAN, stride=SUB), :] = part
        outgoing[pl.ds(e * 2 * SPAN, 2 * SPAN)] = (
            spread[...].reshape(2 * SPAN, SUB, 128).astype(jnp.bfloat16)
        )

    def post(src, to_z, in_plane, half, e, sem):
        dst = arrived.at[pl.ds((half * PLANE + me) * SLOT, SLOT)]
        to_y = holder_y(to_z, in_plane % C)
        pltpu.make_async_remote_copy(
            src_ref=src, dst_ref=dst, send_sem=sem, recv_sem=recv_sem.at[e],
            device_id=(to_z * (X * C) + in_plane, to_y), device_id_type=MESH,
        ).start()

    def from_outgoing(half, in_plane):
        return outgoing.at[pl.ds(half * SPAN + in_plane * SLOT, SLOT)]

    def send(e):
        def one(i, carry):
            s = i % 2
            in_plane = (x * C + c + i // 2) % (X * C)
            half = e * 2 + s
            post(
                from_outgoing(half, in_plane), jnp.where(s == 0, up(e + 1), down(e + 1)),
                in_plane, half, e, send_sem,
            )
            return carry

        lax.fori_loop(0, 2 * X * C, one, 0)

    def send_here():
        half, e = 2 * STEPS - 1, STEPS - 1

        def one(i, carry):
            in_plane = (x * C + c + i) % (X * C)
            mine = (in_plane == x * C + c) & holder
            src = from_outgoing(half, in_plane)

            @pl.when(mine)
            def _():
                dst = arrived.at[pl.ds((half * PLANE + me) * SLOT, SLOT)]
                pltpu.make_async_copy(src, dst, recv_sem.at[e]).start()

            @pl.when(jnp.logical_not(mine))
            def _():
                post(src, z, in_plane, half, e, send_sem)

            return carry

        lax.fori_loop(0, X * C, one, 0)

    def send_relay(k):
        e = STEPS - 1 - k

        def hop(to_z, src, dst):
            pltpu.make_async_remote_copy(
                src_ref=src, dst_ref=dst, send_sem=relay_send, recv_sem=relay_recv.at[k],
                device_id=(grp_of(to_z, x, c), y), device_id_type=MESH,
            ).start()

        @pl.when(k == 0)
        def _():
            lower = outgoing.at[pl.ds(2 * e * SPAN, SPAN // 2)]
            upper = outgoing.at[pl.ds(2 * e * SPAN + SPAN // 2, SPAN // 2)]
            hop(up(1), lower, relay.at[0, pl.ds(0, SPAN // 2)])
            hop(down(1), upper, relay.at[1, pl.ds(SPAN // 2, SPAN // 2)])

        @pl.when(k > 0)
        def _():
            hop(up(1), outgoing.at[pl.ds(2 * e * SPAN, SPAN)], relay.at[2 * k])
            hop(down(1), outgoing.at[pl.ds((2 * e + 1) * SPAN, SPAN)], relay.at[2 * k + 1])

    def pass_relay(k, carry):
        e = STEPS - 1 - k

        @pl.when(k == 0)
        def _():
            pltpu.make_async_copy(relay.at[0], relay.at[0], relay_recv.at[0]).wait()

        @pl.when(k > 0)
        def _():
            both = relay.at[pl.ds(2 * k, 2)]
            pltpu.make_async_copy(both, both, relay_recv.at[k]).wait()

        def one(i, carry):
            s = i % 2
            in_plane = (x * C + c + i // 2) % (X * C)
            half = 2 * e + jnp.where(k == 0, 0, s)

            @pl.when((k > 0) | (in_plane // (X * C // 2) == s))
            def _():
                post(
                    relay.at[2 * k + s, pl.ds(in_plane * SLOT, SLOT)],
                    jnp.where(s == 0, up(e), down(e)), in_plane, half, e, on_send,
                )

            return carry

        lax.fori_loop(0, 2 * X * C, one, 0)
        return carry

    def step_out(i, carry):
        e = jnp.where(i < FAR, STEPS - 1 - i, jnp.where(i == STEPS - 1, 0, i - FAR + 1))
        pack(e)

        @pl.when(i < FAR)
        def _():
            send_relay(i)

        @pl.when((i >= FAR) & (i < STEPS - 1))
        def _():
            pl.semaphore_wait(near_sem.at[e], 2)

        @pl.when(i == STEPS - 2)
        def _():
            pl.semaphore_wait(near_sem.at[0], 2)
            for to in (up(NEAR), down(NEAR)):
                pl.semaphore_signal(
                    far_sem, inc=1, device_id=(grp_of(to, x, c), y), device_id_type=MESH
                )

        @pl.when(i == STEPS - 1)
        def _():
            pl.semaphore_wait(far_sem, 2)
            lax.fori_loop(0, FAR, pass_relay, 0)

        @pl.when(i >= FAR)
        def _():
            send(e)

        @pl.when(i == FAR)
        def _():
            send_here()

        return carry

    lax.fori_loop(0, STEPS, step_out, 0)

    def take(e):
        here = pl.ds(pl.multiple_of(e * CHUNK, CHUNK), CHUNK)
        block = arrived.at[here]
        pltpu.make_async_copy(block, block, recv_sem.at[e]).wait()
        spread_in[...] = block[...].astype(jnp.float32).reshape(CHUNK * SUB, 128)
        for k in range(SUB):
            new_v[:, 128 * k : 128 * (k + 1)] = spread_in[
                pl.ds(k, CHUNK, stride=SUB), :
            ].astype(jnp.bfloat16)
        new = new_v[...]
        dead = spread_in[pl.ds(0, CHUNK, stride=SUB), :][:, 0:1] > 1.5
        minus = jnp.where(dead, LOW, 0.0)
        sub = lax.broadcasted_iota(jnp.int32, (CHUNK, CHUNK), 0)
        lane = lax.broadcasted_iota(jnp.int32, (CHUNK, CHUNK), 1)
        same = sub == lane

        def scores(others):
            return lax.dot_general(
                new, others, (((1,), (1,)), ((), ())), preferred_element_type=jnp.float32
            )

        old = scores(rows[...])
        own = jnp.where(same, LOW, scores(new) + minus)
        best = jnp.maximum(best_v[...], jnp.max(old + minus, axis=0, keepdims=True))
        top = jnp.max(old + pen_v[...], axis=1, keepdims=True)
        mine = jnp.maximum(
            jnp.max(own, axis=0, keepdims=True),
            jnp.max(jnp.where(same, top, LOW), axis=0, keepdims=True),
        )
        across = jnp.sum(jnp.where(same, minus, 0.0), axis=0, keepdims=True)
        at = lax.broadcasted_iota(jnp.int32, (1, ROWS), 1)
        inside = (at >= e * CHUNK) & (at < (e + 1) * CHUNK)
        best_v[...] = jnp.where(inside, jnp.concatenate([mine] * STEPS, axis=1), best)
        pen_v[...] = jnp.where(inside, jnp.concatenate([across] * STEPS, axis=1), pen_v[...])
        rows[here, :] = new

    @pl.when(holder)
    def _():
        rows[...] = jnp.zeros((ROWS, D), jnp.bfloat16)
        pen_v[...] = jnp.full((1, ROWS), LOW, jnp.float32)
        best_v[...] = jnp.full((1, ROWS), -1.0, jnp.float32)

        def compare(i, carry):
            take(jnp.where(i < FAR - 1, i + 1, jnp.where(i == STEPS - 1, 0, STEPS + FAR - 2 - i)))
            return carry

        lax.fori_loop(0, STEPS, compare, 0)
        best = jnp.maximum(best_v[...], -1.0)
        width = PLANE * SLOT
        fill = jnp.zeros((1, 128 - width), jnp.float32)
        for e in reversed(range(STEPS)):
            for s in range(2):
                i = e * 2 + s
                ra[i] = jnp.concatenate([best[:, i * width : (i + 1) * width], fill], axis=1)
                src, dst = ra.at[i], ba.at[z // Y]
                if i == Z - 1:
                    pltpu.make_async_copy(src, dst, a_recv.at[z // Y]).start()
                else:
                    to_z = down(e + 1) if s == 0 else up(e + 1)
                    pltpu.make_async_remote_copy(
                        src_ref=src, dst_ref=dst, send_sem=a_send, recv_sem=a_recv.at[z // Y],
                        device_id=(grp_of(to_z, x, c), y), device_id_type=MESH,
                    ).start()

    sub = lax.broadcasted_iota(jnp.int32, (PLANE, 128), 0)
    lane = lax.broadcasted_iota(jnp.int32, (PLANE, 128), 1)
    turned = jnp.zeros((PLANE, 128), jnp.float32)
    nearest = (z + Z - (y + 2 * c) % Y + Y // 2) // Y
    for k in (0, 1, 3, 2):
        h = (nearest + k) % LINES
        pltpu.make_async_copy(ba.at[h], ba.at[h], a_recv.at[h]).wait()
        for j in range(SLOT):
            its = lane == sub * SLOT + j
            column = jnp.sum(jnp.where(its, ba[h], 0.0), axis=1, keepdims=True)
            turned = jnp.where(lane == h * SLOT + j, column, turned)
    bs[...] = turned.reshape(PLANE, 1, 128)

    for i in range(PLANE):
        to_x, to_y, to_c = mate(i)
        to = (to_x * C + to_c) * Y + to_y
        if i == itself:
            pltpu.make_async_copy(bs.at[me], bb.at[me], b_recv).start()
        else:
            pltpu.make_async_remote_copy(
                src_ref=bs.at[to], dst_ref=bb.at[me], send_sem=b_send, recv_sem=b_recv,
                device_id=(grp_of(z, to_x, to_c), to_y), device_id_type=MESH,
            ).start()

    dz = dest // (X * C)
    dx = (dest // C) % X
    dc = dest % C
    line = (dx * C + dc) * Y + holder_y(dz, dc)
    spot = (dz // Y) * SLOT + rank
    sub = lax.broadcasted_iota(jnp.int32, (PLANE, OWN), 0)
    pltpu.make_async_copy(bb, bb, b_recv).wait()
    table = bb[...].reshape(PLANE, 128)
    value = jnp.zeros((PLANE, OWN), jnp.float32)
    for k in range(LINES * SLOT):
        value = jnp.where(spot == k, table[:, k : k + 1], value)
    answer = jnp.sum(jnp.where(sub == line, value, 0.0), axis=0, keepdims=True)
    out_ref[...] = answer.reshape(OWN)

    others = bs.at[pl.ds(0, PLANE - 1)]
    pltpu.make_async_copy(others, others, b_send).wait()

    straight = 2 * FAR * SPAN + SPAN
    by_relay = 2 * FAR * SPAN - SPAN

    def all_left(count, sem):
        gone = outgoing.at[pl.ds(0, count)]
        pltpu.make_async_copy(gone, gone, sem).wait()

    all_left(by_relay, relay_send)
    all_left(by_relay, on_send)

    @pl.when(holder)
    def _():
        left = ra.at[pl.ds(0, Z - 1)]
        pltpu.make_async_copy(left, left, a_send).wait()
        all_left(straight - SLOT, send_sem)

    @pl.when(jnp.logical_not(holder))
    def _():
        all_left(straight, send_sem)


def shards(emb, dest):
    dma = pltpu.SemaphoreType.DMA
    regular = pltpu.SemaphoreType.REGULAR
    return pl.pallas_call(
        body_kernel,
        out_shape=jax.ShapeDtypeStruct((OWN,), jnp.float32),
        in_specs=[pl.BlockSpec(memory_space=pl.ANY)] * 2,
        out_specs=pl.BlockSpec(memory_space=pltpu.VMEM),
        scratch_shapes=[
            pltpu.VMEM((OWN, D), jnp.bfloat16),
            pltpu.VMEM((OWN,), jnp.int32),
            pltpu.VMEM((OWN, D), jnp.bfloat16),
            pltpu.VMEM((2 * SPAN * SUB, 128), jnp.float32),
            pltpu.VMEM((GROUPS * SLOT, SUB, 128), jnp.bfloat16),
            pltpu.VMEM((2 * FAR, SPAN, SUB, 128), jnp.bfloat16),
            pltpu.VMEM((ROWS, SUB, 128), jnp.bfloat16),
            pltpu.VMEM((CHUNK * SUB, 128), jnp.float32),
            pltpu.VMEM((CHUNK, D), jnp.bfloat16),
            pltpu.VMEM((ROWS, D), jnp.bfloat16),
            pltpu.VMEM((1, ROWS), jnp.float32),
            pltpu.VMEM((1, ROWS), jnp.float32),
            pltpu.VMEM((Z, 1, 128), jnp.float32),
            pltpu.VMEM((LINES, 1, 128), jnp.float32),
            pltpu.VMEM((PLANE, 1, 128), jnp.float32),
            pltpu.VMEM((PLANE, 1, 128), jnp.float32),
            pltpu.SemaphoreType.DMA((2,)),
            pltpu.SemaphoreType.REGULAR((NEAR,)),
            regular,
            dma,
            pltpu.SemaphoreType.DMA((STEPS,)),
            dma,
            pltpu.SemaphoreType.DMA((FAR,)),
            dma,
            dma,
            pltpu.SemaphoreType.DMA((LINES,)),
            dma,
            dma,
        ],
        compiler_params=pltpu.CompilerParams(
            collective_id=0, has_side_effects=True, vmem_limit_bytes=60 << 20
        ),
        name="dedup",
    )(emb, dest)


def solution(mesh):
    in_specs = (P(("grp", "tile"), None), P(("grp", "tile")))
    out_specs = P(("grp", "tile"))
    return jax.shard_map(shards, mesh=mesh, in_specs=in_specs, out_specs=out_specs, check_vma=False)
```
